32 devices in a mesh: batch: 8 (over y, x, core), tok: 4 (over z).
Axes of the slice: x: 2, y: 2, z: 4, core: 2. Of those that a mesh axis runs over, the one named last changes fastest.
Arguments:
- block_input: bfloat16 [16, 1280, 1024], P('batch', 'tok'), may hold values from -6 to 6
- crop_ids: int32 [16, 1280], P('batch'), may hold values from 0 to 63, as said below
- ln1_gain: float32 [1024], replicated, may hold values from 0.1 to 1.9
- ln1_bias: float32 [1024], replicated, may hold values from -3 to 3
- w_qkv: bfloat16 [1024, 3072], replicated, may hold values from -0.1875 to 0.1875
- q_bias: float32 [1024], replicated, may hold values from -3 to 3
- v_bias: float32 [1024], replicated, may hold values from -3 to 3
- w_out: bfloat16 [1024, 1024], replicated, may hold values from -0.75 to 0.75
- out_bias: float32 [1024], replicated, may hold values from -3 to 3
- ln2_gain: float32 [1024], replicated, may hold values from 0.1 to 1.9
- ln2_bias: float32 [1024], replicated, may hold values from -3 to 3
- w_fc1: bfloat16 [1024, 4096], replicated, may hold values from -0.1875 to 0.1875
- fc1_bias: float32 [4096], replicated, may hold values from -3 to 3
- w_fc2: bfloat16 [4096, 1024], replicated, may hold values from -0.09375 to 0.09375
- fc2_bias: float32 [1024], replicated, may hold values from -3 to 3
- out_grad: bfloat16 [16, 1280, 1024], P('batch', 'tok'), may hold values from -6 to 6
Outputs:
- block_output: bfloat16 [16, 1280, 1024], P('batch', 'tok')
- input_grad: bfloat16 [16, 1280, 1024], P('batch', 'tok')
- grad_ln1_gain: float32 [1024], P('batch')
- grad_ln1_bias: float32 [1024], P('batch')
- grad_qkv: float32 [1024, 3072], P(None, 'batch')
- grad_q_bias: float32 [1024], P('batch')
- grad_v_bias: float32 [1024], P('batch')
- grad_out: float32 [1024, 1024], P(None, 'batch')
- grad_out_bias: float32 [1024], P('batch')
- grad_ln2_gain: float32 [1024], P('batch')
- grad_ln2_bias: float32 [1024], P('batch')
- grad_fc1: float32 [1024, 4096], P(None, 'batch')
- grad_fc1_bias: float32 [4096], P('batch')
- grad_fc2: float32 [4096, 1024], P(None, 'batch')
- grad_fc2_bias: float32 [1024], P('batch')
The draws below stay inside these ranges and needn't reach their ends.
Inputs may be any that keep to these rules, and one draw needn't show every extreme that they name: `crop_ids`: A pack holds 8 images; image j has crops j * 8 + c, where crops c = 0 to 1 hold 50 tokens each and crops c = 2 to 7 hold 10 tokens each; the tokens of all crops stand in an order drawn at random within the pack.
All inputs are finite; a program needn't handle non-finite values.
Results may differ from the reference program's by a relative error of at most 0.014.
Values may be sent and summed in bfloat16 or wider, within the bound.
No kernel may reach another device: no remote copies, remote signals or barrier semaphores. Data moves between devices by JAX's collectives and lax.ppermute only.
A program may use at most 320 MiB of HBM per device.

```python
import jax
import jax.numpy as jnp
from jax import lax

D = 1024
H = 16
HD = 64
FF = 4096
GLOBAL_N = 2
GLOBAL_LEN = 50
LOCAL_N = 6
LOCAL_LEN = 10
IMG_LEN = 160
SEQ_LEN = 1280
PACKS = 16


def draw_crop_ids(key, part):
    key = jax.random.fold_in(key, 11)
    positions = jnp.arange(SEQ_LEN, dtype=jnp.int32)
    image_number = positions // IMG_LEN
    within = positions % IMG_LEN
    global_span = GLOBAL_N * GLOBAL_LEN
    crop_local = jnp.where(within < global_span, within // GLOBAL_LEN, GLOBAL_N + (within - global_span) // LOCAL_LEN)
    labels = (image_number * (GLOBAL_N + LOCAL_N) + crop_local).astype(jnp.int32)
    pack_keys = jax.random.split(key, PACKS)

    def shuffle(pack_key):
        return jax.random.permutation(pack_key, SEQ_LEN)
    orders = jax.vmap(shuffle)(pack_keys)
    return labels[orders].astype(jnp.int32)


def with_spikes(result, own_key, source, target, shards_of, factor):
    def block_of(axis_at):
        return (jnp.arange(result.shape[axis_at]) // (result.shape[axis_at] // shards_of)).reshape((-1,) + (1,) * (result.ndim - 1 - axis_at))

    first = jax.random.permutation(own_key, shards_of)[block_of(target)]
    other_side = (block_of(target) + shards_of // 2) % shards_of
    return jnp.where((block_of(source) == first) | (block_of(source) == other_side), factor * result, result)


def block_levels(rng, shape, cuts, low, top_value):
    level, own = 1.0, jax.random.fold_in(rng, 6)
    for position, blocks in cuts:
        draws = jnp.exp(jax.random.uniform(jax.random.fold_in(own, position), (blocks,), jnp.float32, low / len(cuts), top_value / len(cuts)))
        level = level * jnp.repeat(draws, shape[position] // blocks).reshape([-1 if axis == position else 1 for axis in range(len(shape))])
    return level


def normal_values(key, extent, spread, reach, cuts=(), kind=jnp.bfloat16):
    level = block_levels(key, extent, cuts, -0.22, 0.18) if cuts else 1.0
    drawn = jax.random.normal(key, extent, jnp.float32) * spread * level
    return jnp.minimum(jnp.maximum(drawn, -reach), reach).astype(kind)


def bell_draw_with(stream_key, dims, scale, bound, shards, heavy, held_as=jnp.bfloat16):
    result = scale * jax.random.normal(stream_key, dims, jnp.float32)
    if shards:
        result = result * block_levels(stream_key, dims, shards, -0.22, 0.18)
    return jnp.clip(with_spikes(result, jax.random.fold_in(stream_key, 3), *heavy), -bound, bound).astype(held_as)


def setup_inputs(seed: int = 0) -> dict:
    arg_keys = jax.random.split(jax.random.key(seed), 17)
    return {
        "block_input": normal_values(arg_keys[0], (PACKS, SEQ_LEN, D), 1.0, 6.0, ((0, 8), (1, 4))),
        "crop_ids": draw_crop_ids(jax.random.fold_in(arg_keys[16], 71), 0),
        "ln1_gain": jnp.clip(1.0 + 0.18 * jax.random.normal(arg_keys[2], (D,), jnp.float32), 0.1, 1.9),
        "ln1_bias": normal_values(arg_keys[3], (D,), 0.5, 3.0, (), jnp.float32),
        "w_qkv": normal_values(arg_keys[4], (D, 3 * D), D ** -0.5, 0.1875),
        "q_bias": normal_values(arg_keys[5], (D,), 0.5, 3.0, (), jnp.float32),
        "v_bias": normal_values(arg_keys[6], (D,), 0.5, 3.0, (), jnp.float32),
        "w_out": normal_values(arg_keys[7], (D, D), (D // 16) ** -0.5, 0.75),
        "out_bias": normal_values(arg_keys[8], (D,), 0.5, 3.0, (), jnp.float32),
        "ln2_gain": jnp.clip(1.0 + 0.18 * jax.random.normal(arg_keys[9], (D,), jnp.float32), 0.1, 1.9),
        "ln2_bias": normal_values(arg_keys[10], (D,), 0.5, 3.0, (), jnp.float32),
        "w_fc1": normal_values(arg_keys[11], (D, FF), D ** -0.5, 0.1875),
        "fc1_bias": normal_values(arg_keys[12], (FF,), 0.5, 3.0, (), jnp.float32),
        "w_fc2": normal_values(arg_keys[13], (FF, D), FF ** -0.5, 0.09375),
        "fc2_bias": normal_values(arg_keys[14], (D,), 0.5, 3.0, (), jnp.float32),
        "out_grad": bell_draw_with(arg_keys[15], (PACKS, SEQ_LEN, D), 1.0, 6.0, ((0, 8), (1, 4)), (0, 2, 8, 2.0)),
    }


epsilon = 1e-06
masked_score = -1000000000.0
highest = lax.Precision.HIGHEST

@jax.custom_vjp
def low(v):
    return lax.optimization_barrier(v.astype(jnp.bfloat16)).astype(jnp.float32)

@jax.custom_vjp
def low_back(v):
    return v

def low_keep(v):
    return (low(v), None)

def low_pass(kept, grad):
    return (grad,)

def back_keep(v):
    return (v, None)

def back_low(kept, grad):
    return (low(grad),)
low.defvjp(low_keep, low_pass)
low_back.defvjp(back_keep, back_low)

def layer_norm(values, gain, shift):
    center = values - lax.optimization_barrier(jnp.mean(values, axis=-1, keepdims=True))
    variance = lax.optimization_barrier(jnp.mean(center * center, axis=-1, keepdims=True))
    return center * lax.rsqrt(variance + epsilon) * gain + shift

def attend_pieces(pieces):
    query, key_part, value, crops = pieces
    group, length, features = query.shape
    queries = query.reshape(group, length, H, HD)
    keys = key_part.reshape(group, length, H, HD)
    values = value.reshape(group, length, H, HD)
    raw = jnp.einsum('bshd,blhd->bhsl', queries, keys, precision=highest)
    scores = low_back(raw * HD ** (-0.5))
    same_crop = crops[:, :, None] == crops[:, None, :]
    scores = jnp.where(same_crop[:, None], scores, masked_score)
    row_max = lax.optimization_barrier(jnp.max(scores, axis=-1, keepdims=True))
    expo = jnp.exp(scores - row_max)
    prob = low(expo / lax.optimization_barrier(jnp.sum(expo, axis=-1, keepdims=True)))
    mixed = jnp.einsum('bhsl,blhd->bshd', prob, values, precision=highest)
    return mixed.reshape(group, length, features)

def reference(block_input, crop_ids, ln1_gain, ln1_bias, w_qkv, q_bias, v_bias, w_out, out_bias, ln2_gain, ln2_bias, w_fc1, fc1_bias, w_fc2, fc2_bias, out_grad):
    attend_block = jax.checkpoint(attend_pieces)

    def forward(inputs, gain_one, shift_one, weight_qkv, bias_query, bias_value, weight_out, bias_out, gain_two, shift_two, weight_one, bias_one, weight_two, bias_two):
        packs, length, features = inputs.shape
        normed = low(layer_norm(inputs, gain_one, shift_one))
        joined = jnp.einsum('ild,de->ile', normed, weight_qkv, precision=highest)
        query = low_back(low(joined[..., :features] + bias_query))
        key_part = low_back(low(joined[..., features:2 * features]))
        value = low_back(low(joined[..., 2 * features:] + bias_value))
        shape_group = (packs, 1, length, features)
        grouped = lax.map(attend_block, (query.reshape(shape_group), key_part.reshape(shape_group), value.reshape(shape_group), crop_ids.reshape(packs, 1, length)))
        attended = low_back(low(grouped.reshape(packs, length, features)))
        branch = low_back(jnp.einsum('ild,de->ile', attended, weight_out, precision=highest) + bias_out)
        resid = inputs + branch
        normed_two = low(layer_norm(resid, gain_two, shift_two))
        pre_act = low_back(jnp.einsum('ild,df->ilf', normed_two, weight_one, precision=highest) + bias_one)
        hidden = low(jax.nn.gelu(pre_act, approximate=False))
        return resid + low_back(jnp.einsum('ilf,fd->ild', hidden, weight_two, precision=highest) + bias_two)
    params = (block_input.astype(jnp.float32), ln1_gain.astype(jnp.float32), ln1_bias.astype(jnp.float32), w_qkv.astype(jnp.float32), q_bias.astype(jnp.float32), v_bias.astype(jnp.float32), w_out.astype(jnp.float32), out_bias.astype(jnp.float32), ln2_gain.astype(jnp.float32), ln2_bias.astype(jnp.float32), w_fc1.astype(jnp.float32), fc1_bias.astype(jnp.float32), w_fc2.astype(jnp.float32), fc2_bias.astype(jnp.float32))
    output, backward = jax.vjp(forward, *params)
    grads = backward(out_grad.astype(jnp.float32))
    return (output.astype(jnp.bfloat16), grads[0].astype(jnp.bfloat16), grads[1], grads[2], grads[3], grads[4], grads[5], grads[6], grads[7], grads[8], grads[9], grads[10], grads[11], grads[12], grads[13])
```

```python
import jax
import jax.numpy as jnp
from jax import lax
from jax.experimental import pallas as pl
from jax.experimental.pallas import tpu as pltpu
from jax.sharding import PartitionSpec as P

H = 16
HD = 64
IMAGE = 160


epsilon = 1e-06
masked_score = -1000000000.0


def layer_norm(values, gain, shift):
    center = values - jnp.mean(values, axis=-1, keepdims=True)
    variance = jnp.mean(center * center, axis=-1, keepdims=True)
    return center * lax.rsqrt(variance + epsilon) * gain + shift


def split_heads(values):
    return values.reshape(values.shape[0], H, HD)


def join_heads(values):
    return values.reshape(values.shape[0], H * HD)


def column_sum(values):
    return jnp.sum(values.astype(jnp.float32), axis=(0, 1))


def project_qkv(inputs, ln1_gain, ln1_bias, w_qkv, q_bias, v_bias):
    normed, norm_back = jax.vjp(layer_norm, inputs, ln1_gain, ln1_bias)
    normed_low = normed.astype(jnp.bfloat16)
    joined = jnp.dot(normed_low, w_qkv, preferred_element_type=jnp.float32)
    features = inputs.shape[-1]
    query_low = (joined[..., :features] + q_bias).astype(jnp.bfloat16)
    key_low = joined[..., features : 2 * features].astype(jnp.bfloat16)
    value_low = (joined[..., 2 * features :] + v_bias).astype(jnp.bfloat16)
    return (normed_low, norm_back, query_low, key_low, value_low)


def pack_scores(query_pack, key_pack, same_pack):
    raw = jnp.einsum(
        "shd,lhd->hsl",
        split_heads(query_pack),
        split_heads(key_pack),
        preferred_element_type=jnp.float32,
    )
    return jnp.where(same_pack[None], raw * HD ** (-0.5), masked_score)


def attend_forward(pieces):
    query_pack, key_pack, value_pack, same_pack = pieces
    scores = pack_scores(query_pack, key_pack, same_pack)
    row_max = jnp.max(scores, axis=-1, keepdims=True)
    expo = jnp.exp(scores - row_max)
    totals = jnp.sum(expo, axis=-1, keepdims=True)
    log_total = row_max + jnp.log(totals)
    prob_low = (expo / totals).astype(jnp.bfloat16)
    mixed = jnp.einsum(
        "hsl,lhd->shd", prob_low, split_heads(value_pack), preferred_element_type=jnp.float32
    )
    return (join_heads(mixed).astype(jnp.bfloat16), log_total)


def attend_backward(pieces):
    query_pack, key_pack, value_pack, same_pack, log_total, grad_pack = pieces
    score_scale = HD ** (-0.5)
    scores_again = pack_scores(query_pack, key_pack, same_pack)
    prob_full = jnp.exp(scores_again - log_total)
    prob_back = prob_full.astype(jnp.bfloat16)
    grad_heads = split_heads(grad_pack)
    grad_prob = jnp.einsum(
        "shd,lhd->hsl", grad_heads, split_heads(value_pack), preferred_element_type=jnp.float32
    )
    spread = jnp.sum(prob_full * grad_prob, axis=-1, keepdims=True)
    grad_scores = (prob_full * (grad_prob - spread)).astype(jnp.bfloat16)
    grad_query = join_heads(
        jnp.einsum(
            "hsl,lhd->shd", grad_scores, split_heads(key_pack), preferred_element_type=jnp.float32
        )
        * score_scale
    ).astype(jnp.bfloat16)
    key_terms = join_heads(
        jnp.einsum(
            "hsl,shd->lhd", grad_scores, split_heads(query_pack), preferred_element_type=jnp.float32
        )
        * score_scale
    )
    value_terms = join_heads(
        jnp.einsum("hsl,shd->lhd", prob_back, grad_heads, preferred_element_type=jnp.float32)
    )
    return (grad_query, key_terms, value_terms)


def in_place(
    block_input,
    crop_ids,
    ln1_gain,
    ln1_bias,
    w_qkv,
    q_bias,
    v_bias,
    w_out,
    out_bias,
    ln2_gain,
    ln2_bias,
    w_fc1,
    fc1_bias,
    w_fc2,
    fc2_bias,
    out_grad,
):
    packs, local_rows, features = block_input.shape
    offset = lax.axis_index("tok") * local_rows
    own_crop = lax.dynamic_slice_in_dim(crop_ids, offset, local_rows, 1)
    same_crop = own_crop[:, :, None] == crop_ids[:, None, :]
    inputs = block_input.astype(jnp.float32)
    normed_one, norm_one_back, query_low, key_low, value_low = project_qkv(
        inputs, ln1_gain, ln1_bias, w_qkv, q_bias, v_bias
    )
    key_all, value_all = (
        lax.all_gather(key_low, "tok", axis=1, tiled=True),
        lax.all_gather(value_low, "tok", axis=1, tiled=True),
    )
    attended, log_total = lax.map(attend_forward, (query_low, key_all, value_all, same_crop))
    resid = inputs + jnp.dot(attended, w_out, preferred_element_type=jnp.float32) + out_bias
    normed_two, norm_two_back = jax.vjp(layer_norm, resid, ln2_gain, ln2_bias)
    normed_two_low = normed_two.astype(jnp.bfloat16)
    pre_act = jnp.dot(normed_two_low, w_fc1, preferred_element_type=jnp.float32) + fc1_bias

    def gelu_exact(values):
        return jax.nn.gelu(values, approximate=False)

    activated, gelu_back = jax.vjp(gelu_exact, pre_act)
    hidden = activated.astype(jnp.bfloat16)
    output = resid + jnp.dot(hidden, w_fc2, preferred_element_type=jnp.float32) + fc2_bias
    out_grad_full = out_grad.astype(jnp.float32)
    grad_fc2 = jnp.einsum("bsf,bsd->fd", hidden, out_grad, preferred_element_type=jnp.float32)
    grad_fc2_bias = column_sum(out_grad)
    grad_hidden = jnp.einsum("bsd,fd->bsf", out_grad, w_fc2, preferred_element_type=jnp.float32)
    grad_pre = gelu_back(grad_hidden)[0].astype(jnp.bfloat16)
    grad_fc1 = jnp.einsum(
        "bsd,bsf->df", normed_two_low, grad_pre, preferred_element_type=jnp.float32
    )
    grad_fc1_bias = column_sum(grad_pre)
    grad_normed_two = jnp.einsum("bsf,df->bsd", grad_pre, w_fc1, preferred_element_type=jnp.float32)
    resid_term, grad_ln2_gain, grad_ln2_bias = norm_two_back(grad_normed_two)
    grad_resid = out_grad_full + resid_term
    grad_branch = grad_resid.astype(jnp.bfloat16)
    grad_out = jnp.einsum("bsd,bse->de", attended, grad_branch, preferred_element_type=jnp.float32)
    grad_out_bias = column_sum(grad_branch)
    grad_attended = jnp.einsum(
        "bse,de->bsd", grad_branch, w_out, preferred_element_type=jnp.float32
    ).astype(jnp.bfloat16)
    normed_one, norm_one_back, query_low, key_low, value_low = project_qkv(
        inputs, ln1_gain, ln1_bias, w_qkv, q_bias, v_bias
    )
    key_all, value_all = (
        lax.all_gather(key_low, "tok", axis=1, tiled=True),
        lax.all_gather(value_low, "tok", axis=1, tiled=True),
    )
    grad_query, key_terms, value_terms = lax.map(
        attend_backward, (query_low, key_all, value_all, same_crop, log_total, grad_attended)
    )
    grad_key_sum, grad_value_sum = (
        lax.psum_scatter(key_terms, "tok", scatter_dimension=1, tiled=True),
        lax.psum_scatter(value_terms, "tok", scatter_dimension=1, tiled=True),
    )
    grad_key = grad_key_sum.astype(jnp.bfloat16)
    grad_value = grad_value_sum.astype(jnp.bfloat16)
    grad_joined = jnp.concatenate([grad_query, grad_key, grad_value], axis=-1)
    grad_qkv = jnp.einsum(
        "bsd,bse->de", normed_one, grad_joined, preferred_element_type=jnp.float32
    )
    grad_q_bias = column_sum(grad_query)
    grad_v_bias = column_sum(grad_value)
    grad_normed_one = jnp.einsum(
        "bse,de->bsd", grad_joined, w_qkv, preferred_element_type=jnp.float32
    )
    input_term, grad_ln1_gain, grad_ln1_bias = norm_one_back(grad_normed_one)
    input_grad = (grad_resid + input_term).astype(jnp.bfloat16)
    shares = (
        lax.psum_scatter(grad_ln1_gain, "batch", scatter_dimension=0, tiled=True),
        lax.psum_scatter(grad_ln1_bias, "batch", scatter_dimension=0, tiled=True),
        lax.psum_scatter(grad_qkv, "batch", scatter_dimension=1, tiled=True),
        lax.psum_scatter(grad_q_bias, "batch", scatter_dimension=0, tiled=True),
        lax.psum_scatter(grad_v_bias, "batch", scatter_dimension=0, tiled=True),
        lax.psum_scatter(grad_out, "batch", scatter_dimension=1, tiled=True),
        lax.psum_scatter(grad_out_bias, "batch", scatter_dimension=0, tiled=True),
        lax.psum_scatter(grad_ln2_gain, "batch", scatter_dimension=0, tiled=True),
        lax.psum_scatter(grad_ln2_bias, "batch", scatter_dimension=0, tiled=True),
        lax.psum_scatter(grad_fc1, "batch", scatter_dimension=1, tiled=True),
        lax.psum_scatter(grad_fc1_bias, "batch", scatter_dimension=0, tiled=True),
        lax.psum_scatter(grad_fc2, "batch", scatter_dimension=1, tiled=True),
        lax.psum_scatter(grad_fc2_bias, "batch", scatter_dimension=0, tiled=True),
    )
    summed = (
        lax.psum(shares[0].astype(jnp.bfloat16), "tok").astype(jnp.float32),
        lax.psum(shares[1].astype(jnp.bfloat16), "tok").astype(jnp.float32),
        lax.psum(shares[2].astype(jnp.bfloat16), "tok").astype(jnp.float32),
        lax.psum(shares[3].astype(jnp.bfloat16), "tok").astype(jnp.float32),
        lax.psum(shares[4].astype(jnp.bfloat16), "tok").astype(jnp.float32),
        lax.psum(shares[5].astype(jnp.bfloat16), "tok").astype(jnp.float32),
        lax.psum(shares[6].astype(jnp.bfloat16), "tok").astype(jnp.float32),
        lax.psum(shares[7].astype(jnp.bfloat16), "tok").astype(jnp.float32),
        lax.psum(shares[8].astype(jnp.bfloat16), "tok").astype(jnp.float32),
        lax.psum(shares[9].astype(jnp.bfloat16), "tok").astype(jnp.float32),
        lax.psum(shares[10].astype(jnp.bfloat16), "tok").astype(jnp.float32),
        lax.psum(shares[11].astype(jnp.bfloat16), "tok").astype(jnp.float32),
        lax.psum(shares[12].astype(jnp.bfloat16), "tok").astype(jnp.float32),
    )
    return (
        output.astype(jnp.bfloat16),
        input_grad,
        summed[0],
        summed[1],
        summed[2],
        summed[3],
        summed[4],
        summed[5],
        summed[6],
        summed[7],
        summed[8],
        summed[9],
        summed[10],
        summed[11],
        summed[12],
    )


def crop_of_row(axis):
    row = lax.broadcasted_iota(jnp.int32, (IMAGE, IMAGE), axis)
    return jnp.where(row < 50, 0, jnp.where(row < 100, 1, 2 + (row - 100) // 10))


def head_halves(dtype):
    lane = lax.broadcasted_iota(jnp.int32, (1, 2 * HD), 1)
    first = (lane < HD).astype(jnp.float32)
    return first, (first.astype(dtype), (1.0 - first).astype(dtype))


def head_prob(query_half, keys, same_crop):
    raw = lax.dot_general(
        query_half, keys, (((1,), (1,)), ((), ())), preferred_element_type=jnp.float32
    )
    scores = jnp.where(same_crop, raw * HD ** (-0.5), masked_score)
    expo = jnp.exp(scores - jnp.max(scores, axis=-1, keepdims=True))
    return expo / jnp.sum(expo, axis=-1, keepdims=True)


def attend_image(joined_ref, out_ref):
    features = out_ref.shape[1]
    same_crop = crop_of_row(0) == crop_of_row(1)
    first, halves = head_halves(joined_ref.dtype)
    for at in range(0, features, 2 * HD):
        query = joined_ref[:, at : at + 2 * HD]
        keys = joined_ref[:, features + at : features + at + 2 * HD]
        values = joined_ref[:, 2 * features + at : 2 * features + at + 2 * HD]
        mixed = []
        for half in halves:
            prob = head_prob(query * half, keys, same_crop).astype(jnp.bfloat16)
            mixed.append(jnp.dot(prob, values, preferred_element_type=jnp.float32))
        both = mixed[0] * first + mixed[1] * (1.0 - first)
        out_ref[:, at : at + 2 * HD] = both.astype(out_ref.dtype)


def attend_image_back(joined_ref, grad_ref, out_ref):
    features = grad_ref.shape[1]
    same_crop = crop_of_row(0) == crop_of_row(1)
    first, halves = head_halves(joined_ref.dtype)
    scale = HD ** (-0.5)
    for at in range(0, features, 2 * HD):
        query = joined_ref[:, at : at + 2 * HD]
        keys = joined_ref[:, features + at : features + at + 2 * HD]
        values = joined_ref[:, 2 * features + at : 2 * features + at + 2 * HD]
        grad = grad_ref[:, at : at + 2 * HD]
        terms = []
        for half in halves:
            prob = head_prob(query * half, keys, same_crop)
            grad_prob = lax.dot_general(
                grad * half, values, (((1,), (1,)), ((), ())), preferred_element_type=jnp.float32
            )
            spread = jnp.sum(prob * grad_prob, axis=-1, keepdims=True)
            grad_scores = (prob * (grad_prob - spread)).astype(jnp.bfloat16)
            over_rows = (((0,), (0,)), ((), ()))
            terms.append(
                (
                    jnp.dot(grad_scores, keys, preferred_element_type=jnp.float32) * scale,
                    lax.dot_general(
                        grad_scores, query, over_rows, preferred_element_type=jnp.float32
                    )
                    * scale,
                    lax.dot_general(
                        prob.astype(jnp.bfloat16),
                        grad,
                        over_rows,
                        preferred_element_type=jnp.float32,
                    ),
                )
            )
        for part in range(3):
            both = terms[0][part] * first + terms[1][part] * (1.0 - first)
            place = part * features + at
            out_ref[:, place : place + 2 * HD] = both.astype(out_ref.dtype)


def image_attention(joined):
    rows, width = joined.shape
    return pl.pallas_call(
        attend_image,
        grid=(rows // IMAGE,),
        in_specs=[pl.BlockSpec((IMAGE, width), lambda i: (i, 0))],
        out_specs=pl.BlockSpec((IMAGE, width // 3), lambda i: (i, 0)),
        out_shape=jax.ShapeDtypeStruct((rows, width // 3), jnp.bfloat16),
        compiler_params=pltpu.CompilerParams(vmem_limit_bytes=32 * 1024 * 1024),
    )(joined)


def image_attention_back(joined, grad):
    rows, width = joined.shape
    return pl.pallas_call(
        attend_image_back,
        grid=(rows // IMAGE,),
        in_specs=[
            pl.BlockSpec((IMAGE, width), lambda i: (i, 0)),
            pl.BlockSpec((IMAGE, width // 3), lambda i: (i, 0)),
        ],
        out_specs=pl.BlockSpec((IMAGE, width), lambda i: (i, 0)),
        out_shape=jax.ShapeDtypeStruct((rows, width), jnp.bfloat16),
        compiler_params=pltpu.CompilerParams(vmem_limit_bytes=32 * 1024 * 1024),
    )(joined, grad)


def exchange_plan(crop_ids):
    packs, length = crop_ids.shape
    groups, me = lax.axis_size("tok"), lax.axis_index("tok")
    local = length // groups
    rows = packs * local
    capacity = -(-rows * 13 // (groups * 10) // 16) * 16
    order = crop_ids * length + jnp.arange(length, dtype=jnp.int32)
    rank = jnp.sum((order[:, None, :] < order[:, :, None]).astype(jnp.int32), axis=-1)
    target = rank // local

    def by_source(values):
        return values.reshape(packs, groups, local).transpose(1, 0, 2).reshape(groups, rows)

    target = by_source(target)
    place = by_source(rank % local + local * jnp.arange(packs, dtype=jnp.int32)[:, None])
    number = jnp.arange(rows, dtype=jnp.int32)
    earlier = number[None, :] < number[:, None]
    slot = jnp.sum(
        ((target[:, :, None] == target[:, None, :]) & earlier).astype(jnp.int32), axis=-1
    )
    overflow = jnp.max(slot) >= capacity
    fits = slot < capacity
    own = lax.dynamic_index_in_dim
    send_at = jnp.where(
        own(fits, me, 0, False), (own(target, me, 0, False) ^ me) * capacity + own(slot, me, 0, False), -1
    )
    source = jnp.arange(groups, dtype=jnp.int32)[:, None]
    arrive_at = jnp.where((target == me) & fits, (source ^ me) * capacity + slot + 1, 0)
    hits = (place[None] == number[:, None, None]) & (target == me)[None]
    receive_at = jnp.sum(jnp.where(hits, arrive_at[None], 0), axis=(1, 2)) - 1
    lanes = jnp.arange(groups * capacity, dtype=jnp.int32)
    send = (send_at[:, None] == lanes).astype(jnp.bfloat16)
    receive = (receive_at[:, None] == lanes).astype(jnp.bfloat16)
    return send, receive, overflow


def swap_groups(parcels):
    groups = lax.axis_size("tok")
    parts = jnp.split(parcels, groups, axis=0)
    moved = [parts[0]]
    for step in range(1, groups):
        pairs = [(i, i ^ step) for i in range(groups)]
        moved.append(lax.ppermute(parts[step], "tok", pairs))
    return jnp.concatenate(moved, axis=0)


def spread_rows(choice, values):
    return lax.dot_general(
        choice, values, (((0,), (0,)), ((), ())), preferred_element_type=jnp.float32
    ).astype(jnp.bfloat16)


def gather_rows(choice, values):
    return jnp.dot(choice, values, preferred_element_type=jnp.float32).astype(jnp.bfloat16)


def move_rows(outgoing, incoming, values):
    return gather_rows(incoming, swap_groups(spread_rows(outgoing, values)))


def dot_rows(left, right):
    return lax.dot_general(
        left, right, (((0,), (0,)), ((), ())), preferred_element_type=jnp.float32
    )


def dot_back(left, weight):
    return lax.dot_general(
        left, weight, (((1,), (1,)), ((), ())), preferred_element_type=jnp.float32
    )


def row_sum(values):
    return jnp.sum(values.astype(jnp.float32), axis=0)


def share_columns(grad):
    part = lax.psum_scatter(
        grad.astype(jnp.bfloat16), "batch", scatter_dimension=grad.ndim - 1, tiled=True
    )
    return lax.psum(part, "tok").astype(jnp.float32)


def on_device(
    block_input,
    crop_ids,
    ln1_gain,
    ln1_bias,
    w_qkv,
    q_bias,
    v_bias,
    w_out,
    out_bias,
    ln2_gain,
    ln2_bias,
    w_fc1,
    fc1_bias,
    w_fc2,
    fc2_bias,
    out_grad,
):
    packs, local_rows, features = block_input.shape
    rows = packs * local_rows
    send, receive, overflow = exchange_plan(crop_ids)
    low_input = move_rows(send, receive, block_input.reshape(rows, features))
    low_grad = move_rows(send, receive, out_grad.reshape(rows, features))
    inputs = low_input.astype(jnp.float32)
    normed_one, norm_one_back, query, key, value = project_qkv(
        inputs, ln1_gain, ln1_bias, w_qkv, q_bias, v_bias
    )
    joined = jnp.concatenate([query, key, value], axis=-1)
    attended = image_attention(joined)
    resid = inputs + jnp.dot(attended, w_out, preferred_element_type=jnp.float32) + out_bias
    normed_two, norm_two_back = jax.vjp(layer_norm, resid, ln2_gain, ln2_bias)
    normed_two_low = normed_two.astype(jnp.bfloat16)
    pre_act = jnp.dot(normed_two_low, w_fc1, preferred_element_type=jnp.float32) + fc1_bias

    def gelu_exact(values):
        return jax.nn.gelu(values, approximate=False)

    activated, gelu_back = jax.vjp(gelu_exact, pre_act)
    hidden = activated.astype(jnp.bfloat16)
    output = resid + jnp.dot(hidden, w_fc2, preferred_element_type=jnp.float32) + fc2_bias
    output = move_rows(receive, send, output.astype(jnp.bfloat16))
    grad_fc2 = dot_rows(hidden, low_grad)
    grad_fc2_bias = row_sum(low_grad)
    grad_pre = gelu_back(dot_back(low_grad, w_fc2))[0].astype(jnp.bfloat16)
    grad_fc1 = dot_rows(normed_two_low, grad_pre)
    grad_fc1_bias = row_sum(grad_pre)
    resid_term, grad_ln2_gain, grad_ln2_bias = norm_two_back(dot_back(grad_pre, w_fc1))
    grad_resid = low_grad.astype(jnp.float32) + resid_term
    grad_branch = grad_resid.astype(jnp.bfloat16)
    grad_out = dot_rows(attended, grad_branch)
    grad_out_bias = row_sum(grad_branch)
    grad_attended = dot_back(grad_branch, w_out).astype(jnp.bfloat16)
    grad_joined = image_attention_back(joined, grad_attended)
    grad_qkv = dot_rows(normed_one, grad_joined)
    grad_joined_bias = row_sum(grad_joined)
    input_term, grad_ln1_gain, grad_ln1_bias = norm_one_back(dot_back(grad_joined, w_qkv))
    input_grad = (grad_resid + input_term).astype(jnp.bfloat16)
    input_grad = move_rows(receive, send, input_grad)

    shards = lax.axis_size("batch")
    short = [
        grad_ln1_gain,
        grad_ln1_bias,
        grad_joined_bias[:features],
        grad_joined_bias[2 * features :],
        grad_out_bias,
        grad_ln2_gain,
        grad_ln2_bias,
        grad_fc1_bias,
        grad_fc2_bias,
        jnp.broadcast_to(overflow.astype(jnp.float32), (shards,)),
    ]
    widths = [one.shape[0] // shards for one in short]
    packed = jnp.concatenate([one.reshape(shards, -1) for one in short], axis=1)
    packed = lax.psum(lax.psum_scatter(packed, "batch", scatter_dimension=0, tiled=True), "tok")
    pieces, at = [], 0
    for width in widths:
        pieces.append(packed[0, at : at + width])
        at += width
    fast = (
        output.reshape(block_input.shape),
        input_grad.reshape(block_input.shape),
        pieces[0],
        pieces[1],
        share_columns(grad_qkv),
        pieces[2],
        pieces[3],
        share_columns(grad_out),
        pieces[4],
        pieces[5],
        pieces[6],
        share_columns(grad_fc1),
        pieces[7],
        share_columns(grad_fc2),
        pieces[8],
    )
    def unfinished(state):
        return state[0] > 0.5

    def redo(state):
        return (
            jnp.float32(0.0),
            in_place(
                block_input,
                crop_ids,
                ln1_gain,
                ln1_bias,
                w_qkv,
                q_bias,
                v_bias,
                w_out,
                out_bias,
                ln2_gain,
                ln2_bias,
                w_fc1,
                fc1_bias,
                w_fc2,
                fc2_bias,
                out_grad,
            ),
        )

    return lax.while_loop(unfinished, redo, (pieces[9][0], fast))[1]


def solution(mesh):
    in_specs = (
        P("batch", "tok", None),
        P("batch", None),
        P(),
        P(),
        P(),
        P(),
        P(),
        P(),
        P(),
        P(),
        P(),
        P(),
        P(),
        P(),
        P(),
        P("batch", "tok", None),
    )
    out_specs = (
        P("batch", "tok", None),
        P("batch", "tok", None),
        P("batch"),
        P("batch"),
        P(None, "batch"),
        P("batch"),
        P("batch"),
        P(None, "batch"),
        P("batch"),
        P("batch"),
        P("batch"),
        P(None, "batch"),
        P("batch"),
        P(None, "batch"),
        P("batch"),
    )
    return jax.shard_map(
        on_device, mesh=mesh, in_specs=in_specs, out_specs=out_specs, check_vma=False
    )
```

```python
import functools

import jax
import jax.numpy as jnp
from jax import lax
from jax.experimental import pallas as pl
from jax.experimental.pallas import tpu as pltpu
from jax.sharding import PartitionSpec as P

H = 16
HD = 64
IMAGE = 160


epsilon = 1e-06
masked_score = -1000000000.0


def layer_norm(values, gain, shift):
    center = values - jnp.mean(values, axis=-1, keepdims=True)
    variance = jnp.mean(center * center, axis=-1, keepdims=True)
    return center * lax.rsqrt(variance + epsilon) * gain + shift


def split_heads(values):
    return values.reshape(values.shape[0], H, HD)


def join_heads(values):
    return values.reshape(values.shape[0], H * HD)


def column_sum(values):
    return jnp.sum(values.astype(jnp.float32), axis=(0, 1))


def project_qkv(inputs, ln1_gain, ln1_bias, w_qkv, q_bias, v_bias):
    normed, norm_back = jax.vjp(layer_norm, inputs, ln1_gain, ln1_bias)
    normed_low = normed.astype(jnp.bfloat16)
    joined = jnp.dot(normed_low, w_qkv, preferred_element_type=jnp.float32)
    features = inputs.shape[-1]
    query_low = (joined[..., :features] + q_bias).astype(jnp.bfloat16)
    key_low = joined[..., features : 2 * features].astype(jnp.bfloat16)
    value_low = (joined[..., 2 * features :] + v_bias).astype(jnp.bfloat16)
    return (normed_low, norm_back, query_low, key_low, value_low)


def pack_scores(query_pack, key_pack, same_pack):
    raw = jnp.einsum(
        "shd,lhd->hsl",
        split_heads(query_pack),
        split_heads(key_pack),
        preferred_element_type=jnp.float32,
    )
    return jnp.where(same_pack[None], raw * HD ** (-0.5), masked_score)


def attend_forward(pieces):
    query_pack, key_pack, value_pack, same_pack = pieces
    scores = pack_scores(query_pack, key_pack, same_pack)
    row_max = jnp.max(scores, axis=-1, keepdims=True)
    expo = jnp.exp(scores - row_max)
    totals = jnp.sum(expo, axis=-1, keepdims=True)
    log_total = row_max + jnp.log(totals)
    prob_low = (expo / totals).astype(jnp.bfloat16)
    mixed = jnp.einsum(
        "hsl,lhd->shd", prob_low, split_heads(value_pack), preferred_element_type=jnp.float32
    )
    return (join_heads(mixed).astype(jnp.bfloat16), log_total)


def attend_backward(pieces):
    query_pack, key_pack, value_pack, same_pack, log_total, grad_pack = pieces
    score_scale = HD ** (-0.5)
    scores_again = pack_scores(query_pack, key_pack, same_pack)
    prob_full = jnp.exp(scores_again - log_total)
    prob_back = prob_full.astype(jnp.bfloat16)
    grad_heads = split_heads(grad_pack)
    grad_prob = jnp.einsum(
        "shd,lhd->hsl", grad_heads, split_heads(value_pack), preferred_element_type=jnp.float32
    )
    spread = jnp.sum(prob_full * grad_prob, axis=-1, keepdims=True)
    grad_scores = (prob_full * (grad_prob - spread)).astype(jnp.bfloat16)
    grad_query = join_heads(
        jnp.einsum(
            "hsl,lhd->shd", grad_scores, split_heads(key_pack), preferred_element_type=jnp.float32
        )
        * score_scale
    ).astype(jnp.bfloat16)
    key_terms = join_heads(
        jnp.einsum(
            "hsl,shd->lhd", grad_scores, split_heads(query_pack), preferred_element_type=jnp.float32
        )
        * score_scale
    )
    value_terms = join_heads(
        jnp.einsum("hsl,shd->lhd", prob_back, grad_heads, preferred_element_type=jnp.float32)
    )
    return (grad_query, key_terms, value_terms)


def in_place(
    block_input,
    crop_ids,
    ln1_gain,
    ln1_bias,
    w_qkv,
    q_bias,
    v_bias,
    w_out,
    out_bias,
    ln2_gain,
    ln2_bias,
    w_fc1,
    fc1_bias,
    w_fc2,
    fc2_bias,
    out_grad,
):
    packs, local_rows, features = block_input.shape
    offset = lax.axis_index("tok") * local_rows
    own_crop = lax.dynamic_slice_in_dim(crop_ids, offset, local_rows, 1)
    same_crop = own_crop[:, :, None] == crop_ids[:, None, :]
    inputs = block_input.astype(jnp.float32)
    normed_one, norm_one_back, query_low, key_low, value_low = project_qkv(
        inputs, ln1_gain, ln1_bias, w_qkv, q_bias, v_bias
    )
    key_all, value_all = (
        lax.all_gather(key_low, "tok", axis=1, tiled=True),
        lax.all_gather(value_low, "tok", axis=1, tiled=True),
    )
    attended, log_total = lax.map(attend_forward, (query_low, key_all, value_all, same_crop))
    resid = inputs + jnp.dot(attended, w_out, preferred_element_type=jnp.float32) + out_bias
    normed_two, norm_two_back = jax.vjp(layer_norm, resid, ln2_gain, ln2_bias)
    normed_two_low = normed_two.astype(jnp.bfloat16)
    pre_act = jnp.dot(normed_two_low, w_fc1, preferred_element_type=jnp.float32) + fc1_bias

    def gelu_exact(values):
        return jax.nn.gelu(values, approximate=False)

    activated, gelu_back = jax.vjp(gelu_exact, pre_act)
    hidden = activated.astype(jnp.bfloat16)
    output = resid + jnp.dot(hidden, w_fc2, preferred_element_type=jnp.float32) + fc2_bias
    out_grad_full = out_grad.astype(jnp.float32)
    grad_fc2 = jnp.einsum("bsf,bsd->fd", hidden, out_grad, preferred_element_type=jnp.float32)
    grad_fc2_bias = column_sum(out_grad)
    grad_hidden = jnp.einsum("bsd,fd->bsf", out_grad, w_fc2, preferred_element_type=jnp.float32)
    grad_pre = gelu_back(grad_hidden)[0].astype(jnp.bfloat16)
    grad_fc1 = jnp.einsum(
        "bsd,bsf->df", normed_two_low, grad_pre, preferred_element_type=jnp.float32
    )
    grad_fc1_bias = column_sum(grad_pre)
    grad_normed_two = jnp.einsum("bsf,df->bsd", grad_pre, w_fc1, preferred_element_type=jnp.float32)
    resid_term, grad_ln2_gain, grad_ln2_bias = norm_two_back(grad_normed_two)
    grad_resid = out_grad_full + resid_term
    grad_branch = grad_resid.astype(jnp.bfloat16)
    grad_out = jnp.einsum("bsd,bse->de", attended, grad_branch, preferred_element_type=jnp.float32)
    grad_out_bias = column_sum(grad_branch)
    grad_attended = jnp.einsum(
        "bse,de->bsd", grad_branch, w_out, preferred_element_type=jnp.float32
    ).astype(jnp.bfloat16)
    normed_one, norm_one_back, query_low, key_low, value_low = project_qkv(
        inputs, ln1_gain, ln1_bias, w_qkv, q_bias, v_bias
    )
    key_all, value_all = (
        lax.all_gather(key_low, "tok", axis=1, tiled=True),
        lax.all_gather(value_low, "tok", axis=1, tiled=True),
    )
    grad_query, key_terms, value_terms = lax.map(
        attend_backward, (query_low, key_all, value_all, same_crop, log_total, grad_attended)
    )
    grad_key_sum, grad_value_sum = (
        lax.psum_scatter(key_terms, "tok", scatter_dimension=1, tiled=True),
        lax.psum_scatter(value_terms, "tok", scatter_dimension=1, tiled=True),
    )
    grad_key = grad_key_sum.astype(jnp.bfloat16)
    grad_value = grad_value_sum.astype(jnp.bfloat16)
    grad_joined = jnp.concatenate([grad_query, grad_key, grad_value], axis=-1)
    grad_qkv = jnp.einsum(
        "bsd,bse->de", normed_one, grad_joined, preferred_element_type=jnp.float32
    )
    grad_q_bias = column_sum(grad_query)
    grad_v_bias = column_sum(grad_value)
    grad_normed_one = jnp.einsum(
        "bse,de->bsd", grad_joined, w_qkv, preferred_element_type=jnp.float32
    )
    input_term, grad_ln1_gain, grad_ln1_bias = norm_one_back(grad_normed_one)
    input_grad = (grad_resid + input_term).astype(jnp.bfloat16)
    shares = (
        lax.psum_scatter(grad_ln1_gain, "batch", scatter_dimension=0, tiled=True),
        lax.psum_scatter(grad_ln1_bias, "batch", scatter_dimension=0, tiled=True),
        lax.psum_scatter(grad_qkv, "batch", scatter_dimension=1, tiled=True),
        lax.psum_scatter(grad_q_bias, "batch", scatter_dimension=0, tiled=True),
        lax.psum_scatter(grad_v_bias, "batch", scatter_dimension=0, tiled=True),
        lax.psum_scatter(grad_out, "batch", scatter_dimension=1, tiled=True),
        lax.psum_scatter(grad_out_bias, "batch", scatter_dimension=0, tiled=True),
        lax.psum_scatter(grad_ln2_gain, "batch", scatter_dimension=0, tiled=True),
        lax.psum_scatter(grad_ln2_bias, "batch", scatter_dimension=0, tiled=True),
        lax.psum_scatter(grad_fc1, "batch", scatter_dimension=1, tiled=True),
        lax.psum_scatter(grad_fc1_bias, "batch", scatter_dimension=0, tiled=True),
        lax.psum_scatter(grad_fc2, "batch", scatter_dimension=1, tiled=True),
        lax.psum_scatter(grad_fc2_bias, "batch", scatter_dimension=0, tiled=True),
    )
    summed = (
        lax.psum(shares[0].astype(jnp.bfloat16), "tok").astype(jnp.float32),
        lax.psum(shares[1].astype(jnp.bfloat16), "tok").astype(jnp.float32),
        lax.psum(shares[2].astype(jnp.bfloat16), "tok").astype(jnp.float32),
        lax.psum(shares[3].astype(jnp.bfloat16), "tok").astype(jnp.float32),
        lax.psum(shares[4].astype(jnp.bfloat16), "tok").astype(jnp.float32),
        lax.psum(shares[5].astype(jnp.bfloat16), "tok").astype(jnp.float32),
        lax.psum(shares[6].astype(jnp.bfloat16), "tok").astype(jnp.float32),
        lax.psum(shares[7].astype(jnp.bfloat16), "tok").astype(jnp.float32),
        lax.psum(shares[8].astype(jnp.bfloat16), "tok").astype(jnp.float32),
        lax.psum(shares[9].astype(jnp.bfloat16), "tok").astype(jnp.float32),
        lax.psum(shares[10].astype(jnp.bfloat16), "tok").astype(jnp.float32),
        lax.psum(shares[11].astype(jnp.bfloat16), "tok").astype(jnp.float32),
        lax.psum(shares[12].astype(jnp.bfloat16), "tok").astype(jnp.float32),
    )
    return (
        output.astype(jnp.bfloat16),
        input_grad,
        summed[0],
        summed[1],
        summed[2],
        summed[3],
        summed[4],
        summed[5],
        summed[6],
        summed[7],
        summed[8],
        summed[9],
        summed[10],
        summed[11],
        summed[12],
    )


def crop_of_row(axis):
    row = lax.broadcasted_iota(jnp.int32, (IMAGE, IMAGE), axis)
    return jnp.where(row < 50, 0, jnp.where(row < 100, 1, 2 + (row - 100) // 10))


def head_halves(dtype):
    lane = lax.broadcasted_iota(jnp.int32, (1, 2 * HD), 1)
    first = (lane < HD).astype(jnp.float32)
    return first, (first.astype(dtype), (1.0 - first).astype(dtype))


def head_prob(query_half, keys, same_crop):
    raw = lax.dot_general(
        query_half, keys, (((1,), (1,)), ((), ())), preferred_element_type=jnp.float32
    )
    scores = jnp.where(same_crop, raw * HD ** (-0.5), masked_score)
    expo = jnp.exp(scores - jnp.max(scores, axis=-1, keepdims=True))
    return expo / jnp.sum(expo, axis=-1, keepdims=True)


def attend_image(joined_ref, out_ref):
    features = out_ref.shape[1]
    same_crop = crop_of_row(0) == crop_of_row(1)
    first, halves = head_halves(joined_ref.dtype)
    for at in range(0, features, 2 * HD):
        query = joined_ref[:, at : at + 2 * HD]
        keys = joined_ref[:, features + at : features + at + 2 * HD]
        values = joined_ref[:, 2 * features + at : 2 * features + at + 2 * HD]
        mixed = []
        for half in halves:
            prob = head_prob(query * half, keys, same_crop).astype(jnp.bfloat16)
            mixed.append(jnp.dot(prob, values, preferred_element_type=jnp.float32))
        both = mixed[0] * first + mixed[1] * (1.0 - first)
        out_ref[:, at : at + 2 * HD] = both.astype(out_ref.dtype)


def attend_image_back(joined_ref, grad_ref, out_ref):
    features = grad_ref.shape[1]
    same_crop = crop_of_row(0) == crop_of_row(1)
    first, halves = head_halves(joined_ref.dtype)
    scale = HD ** (-0.5)
    for at in range(0, features, 2 * HD):
        query = joined_ref[:, at : at + 2 * HD]
        keys = joined_ref[:, features + at : features + at + 2 * HD]
        values = joined_ref[:, 2 * features + at : 2 * features + at + 2 * HD]
        grad = grad_ref[:, at : at + 2 * HD]
        terms = []
        for half in halves:
            prob = head_prob(query * half, keys, same_crop)
            grad_prob = lax.dot_general(
                grad * half, values, (((1,), (1,)), ((), ())), preferred_element_type=jnp.float32
            )
            spread = jnp.sum(prob * grad_prob, axis=-1, keepdims=True)
            grad_scores = (prob * (grad_prob - spread)).astype(jnp.bfloat16)
            over_rows = (((0,), (0,)), ((), ()))
            terms.append(
                (
                    jnp.dot(grad_scores, keys, preferred_element_type=jnp.float32) * scale,
                    lax.dot_general(
                        grad_scores, query, over_rows, preferred_element_type=jnp.float32
                    )
                    * scale,
                    lax.dot_general(
                        prob.astype(jnp.bfloat16),
                        grad,
                        over_rows,
                        preferred_element_type=jnp.float32,
                    ),
                )
            )
        for part in range(3):
            both = terms[0][part] * first + terms[1][part] * (1.0 - first)
            place = part * features + at
            out_ref[:, place : place + 2 * HD] = both.astype(out_ref.dtype)


def image_attention(joined):
    rows, width = joined.shape
    return pl.pallas_call(
        attend_image,
        grid=(rows // IMAGE,),
        in_specs=[pl.BlockSpec((IMAGE, width), lambda i: (i, 0))],
        out_specs=pl.BlockSpec((IMAGE, width // 3), lambda i: (i, 0)),
        out_shape=jax.ShapeDtypeStruct((rows, width // 3), jnp.bfloat16),
        compiler_params=pltpu.CompilerParams(vmem_limit_bytes=32 * 1024 * 1024),
    )(joined)


def image_attention_back(joined, grad):
    rows, width = joined.shape
    return pl.pallas_call(
        attend_image_back,
        grid=(rows // IMAGE,),
        in_specs=[
            pl.BlockSpec((IMAGE, width), lambda i: (i, 0)),
            pl.BlockSpec((IMAGE, width // 3), lambda i: (i, 0)),
        ],
        out_specs=pl.BlockSpec((IMAGE, width), lambda i: (i, 0)),
        out_shape=jax.ShapeDtypeStruct((rows, width), jnp.bfloat16),
        compiler_params=pltpu.CompilerParams(vmem_limit_bytes=32 * 1024 * 1024),
    )(joined, grad)


def exchange_plan(crop_ids):
    packs, length = crop_ids.shape
    groups, me = lax.axis_size("tok"), lax.axis_index("tok")
    local = length // groups
    rows = packs * local
    capacity = -(-rows * 13 // (groups * 10) // 16) * 16
    order = crop_ids * length + jnp.arange(length, dtype=jnp.int32)
    rank = jnp.sum((order[:, None, :] < order[:, :, None]).astype(jnp.int32), axis=-1)
    target = rank // local

    def by_source(values):
        return values.reshape(packs, groups, local).transpose(1, 0, 2).reshape(groups, rows)

    target = by_source(target)
    place = by_source(rank % local + local * jnp.arange(packs, dtype=jnp.int32)[:, None])
    number = jnp.arange(rows, dtype=jnp.int32)
    earlier = number[None, :] < number[:, None]
    slot = jnp.sum(
        ((target[:, :, None] == target[:, None, :]) & earlier).astype(jnp.int32), axis=-1
    )
    overflow = jnp.max(slot) >= capacity
    fits = slot < capacity
    own = lax.dynamic_index_in_dim
    send_at = jnp.where(
        own(fits, me, 0, False), (own(target, me, 0, False) ^ me) * capacity + own(slot, me, 0, False), -1
    )
    source = jnp.arange(groups, dtype=jnp.int32)[:, None]
    arrive_at = jnp.where((target == me) & fits, (source ^ me) * capacity + slot + 1, 0)
    hits = (place[None] == number[:, None, None]) & (target == me)[None]
    receive_at = jnp.sum(jnp.where(hits, arrive_at[None], 0), axis=(1, 2)) - 1
    lanes = jnp.arange(groups * capacity, dtype=jnp.int32)
    send = (send_at[:, None] == lanes).astype(jnp.bfloat16)
    receive = (receive_at[:, None] == lanes).astype(jnp.bfloat16)
    return send, receive, overflow


def swap_groups(parcels):
    groups = lax.axis_size("tok")
    parts = jnp.split(parcels, groups, axis=0)
    moved = [parts[0]]
    for step in range(1, groups):
        pairs = [(i, i ^ step) for i in range(groups)]
        moved.append(lax.ppermute(parts[step], "tok", pairs))
    return jnp.concatenate(moved, axis=0)


def spread_rows(choice, values):
    return lax.dot_general(
        choice, values, (((0,), (0,)), ((), ())), preferred_element_type=jnp.float32
    ).astype(jnp.bfloat16)


def gather_rows(choice, values):
    return jnp.dot(choice, values, preferred_element_type=jnp.float32).astype(jnp.bfloat16)


def move_rows(outgoing, incoming, values):
    return gather_rows(incoming, swap_groups(spread_rows(outgoing, values)))


def row_sum(values):
    return jnp.sum(values.astype(jnp.float32), axis=0)


SLABS = 8
MIB = 1024 * 1024
LOW = jnp.bfloat16


def dot(left, right):
    return jnp.dot(left, right, preferred_element_type=jnp.float32)


def dot_back(left, weight):
    return lax.dot_general(
        left, weight, (((1,), (1,)), ((), ())), preferred_element_type=jnp.float32
    )


def dot_rows(left, right):
    return lax.dot_general(
        left, right, (((0,), (0,)), ((), ())), preferred_element_type=jnp.float32
    )


def gelu_and_slope(z):
    tail = jnp.exp(z * z * -0.5)
    t = 1.0 / (1.0 + (0.3275911 * 0.5**0.5) * jnp.abs(z))
    series = 0.7107068705 + t * (-0.7265760135 + t * 0.5307027145)
    beyond = tail * (t * (0.127414796 + t * (-0.142248368 + t * series)))
    below = jnp.where(z >= 0.0, 1.0 - beyond, beyond)
    return z * below, below + z * tail * 0.3989422804014327


def whole_block(shape):
    return pl.BlockSpec(shape, lambda step, *_: (0,) * len(shape))


def feed_forward_kernel(
    x_ref, att_ref, w_out_ref, vec_ref, w1_ref, b1_ref, w2_ref,
    out_ref, n2t_ref, hat_ref, rstd_ref, hidden_ref, slope_ref,
    n2_s, acc_s, *, chunk,
):
    step, steps = pl.program_id(0), pl.num_programs(0)
    rows = x_ref.shape[0]

    @pl.when(step == 0)
    def _():
        def part(i, carry):
            at = pl.ds(pl.multiple_of(i * chunk, chunk), chunk)
            resid = x_ref[at, :].astype(jnp.float32) + dot(att_ref[at, :], w_out_ref[...])
            resid = resid + vec_ref[0:1, :]
            center = resid - jnp.mean(resid, axis=-1, keepdims=True)
            rstd = lax.rsqrt(jnp.mean(center * center, axis=-1, keepdims=True) + epsilon)
            hat = center * rstd
            hat_ref[at, :] = hat.astype(LOW)
            rstd_ref[at, :] = jnp.broadcast_to(rstd, (chunk, rstd_ref.shape[1]))
            acc_s[at, :] = resid + vec_ref[3:4, :]
            n2_s[at, :] = (hat * vec_ref[1:2, :] + vec_ref[2:3, :]).astype(LOW)
            return carry

        lax.fori_loop(0, rows // chunk, part, 0)
        n2t_ref[...] = n2_s[...].T

    act, slope = gelu_and_slope(dot(n2_s[...], w1_ref[...]) + b1_ref[...])
    hidden_ref[...] = act.astype(LOW)
    slope_ref[...] = slope.astype(LOW)
    acc_s[...] += dot(hidden_ref[...], w2_ref[...])

    @pl.when(step == steps - 1)
    def _():
        out_ref[...] = acc_s[...].astype(LOW)


def feed_forward(x, attended, w_out, vectors, w1, b1, w2):
    rows, features = x.shape
    width = w1.shape[1]
    block = width // SLABS
    grown = pl.BlockSpec((rows, block), lambda step: (0, step))
    return pl.pallas_call(
        functools.partial(feed_forward_kernel, chunk=rows // 4),
        grid=(SLABS,),
        in_specs=[
            whole_block(x.shape),
            whole_block(x.shape),
            whole_block(w_out.shape),
            whole_block(vectors.shape),
            pl.BlockSpec((features, block), lambda step: (0, step)),
            pl.BlockSpec((1, block), lambda step: (0, step)),
            pl.BlockSpec((block, features), lambda step: (step, 0)),
        ],
        out_specs=[
            whole_block(x.shape),
            whole_block((features, rows)),
            whole_block(x.shape),
            whole_block((rows, 128)),
            grown,
            grown,
        ],
        out_shape=[
            jax.ShapeDtypeStruct(x.shape, LOW),
            jax.ShapeDtypeStruct((features, rows), LOW),
            jax.ShapeDtypeStruct(x.shape, LOW),
            jax.ShapeDtypeStruct((rows, 128), jnp.float32),
            jax.ShapeDtypeStruct((rows, width), LOW),
            jax.ShapeDtypeStruct((rows, width), LOW),
        ],
        scratch_shapes=[pltpu.VMEM(x.shape, LOW), pltpu.VMEM(x.shape, jnp.float32)],
        compiler_params=pltpu.CompilerParams(vmem_limit_bytes=40 * MIB),
        name="feed_forward",
    )(x, attended, w_out, vectors, w1, b1, w2)


def feed_back_kernel(
    order_ref, og_ref, n2t_ref, w1_ref, w2_ref, hidden_ref, slope_ref,
    dn2_ref, keep1_ref, send1_ref, keep2_ref, send2_ref, db1_ref, ogt_s,
):
    step, steps = pl.program_id(0), pl.num_programs(0)
    features = og_ref.shape[1]
    slab, half = features // SLABS, features // 2

    @pl.when(step == 0)
    def _():
        for p in range(SLABS):
            at = pl.multiple_of(order_ref[1, p] * slab, slab)
            ogt_s[p * slab : (p + 1) * slab, :] = og_ref[:, pl.ds(at, slab)].T
        dn2_ref[...] = jnp.zeros_like(dn2_ref)

    hidden = hidden_ref[...]
    grad = dot_back(og_ref[...], w2_ref[...]) * slope_ref[...].astype(jnp.float32)
    grad = grad.astype(LOW)
    keep2_ref[...] = dot(ogt_s[:half, :], hidden).astype(LOW)
    send2_ref[...] = dot(ogt_s[half:, :], hidden).astype(LOW)
    db1_ref[...] = jnp.sum(grad.astype(jnp.float32), axis=0, keepdims=True)
    dn2_ref[...] += dot_back(grad, w1_ref[...])
    dw1 = dot(n2t_ref[...], grad).astype(LOW)

    @pl.when(step < steps // 2)
    def _():
        keep1_ref[0] = dw1

    @pl.when(step >= steps // 2)
    def _():
        send1_ref[0] = dw1


def feed_back(order, part, parts, og, n2t, w1, w2, hidden, slope):
    rows, features = og.shape
    width = w1.shape[1]
    block = width // (SLABS * parts)
    half = SLABS // 2

    def at(step, order):
        return order[0, step] * parts + part

    return pl.pallas_call(
        feed_back_kernel,
        grid_spec=pltpu.PrefetchScalarGridSpec(
            num_scalar_prefetch=1,
            grid=(SLABS,),
            in_specs=[
                whole_block(og.shape),
                whole_block(n2t.shape),
                pl.BlockSpec((features, block), lambda step, order: (0, at(step, order))),
                pl.BlockSpec((block, features), lambda step, order: (at(step, order), 0)),
                pl.BlockSpec((rows, block), lambda step, order: (0, at(step, order))),
                pl.BlockSpec((rows, block), lambda step, order: (0, at(step, order))),
            ],
            out_specs=[
                whole_block(og.shape),
                pl.BlockSpec(
                    (1, features, block), lambda step, order: (jnp.minimum(step, half - 1), 0, 0)
                ),
                pl.BlockSpec(
                    (1, features, block), lambda step, order: (jnp.maximum(step - half, 0), 0, 0)
                ),
                pl.BlockSpec((features // 2, block), lambda step, order: (0, order[0, step])),
                pl.BlockSpec((features // 2, block), lambda step, order: (0, order[0, step])),
                pl.BlockSpec((1, block), lambda step, order: (0, order[0, step])),
            ],
            scratch_shapes=[pltpu.VMEM((features, rows), LOW)],
        ),
        out_shape=[
            jax.ShapeDtypeStruct(og.shape, jnp.float32),
            jax.ShapeDtypeStruct((half, features, block), LOW),
            jax.ShapeDtypeStruct((half, features, block), LOW),
            jax.ShapeDtypeStruct((features // 2, SLABS * block), LOW),
            jax.ShapeDtypeStruct((features // 2, SLABS * block), LOW),
            jax.ShapeDtypeStruct((1, SLABS * block), jnp.float32),
        ],
        compiler_params=pltpu.CompilerParams(vmem_limit_bytes=40 * MIB),
        name="feed_back",
    )(order, og, n2t, w1, w2, hidden, slope)


def products_kernel(
    order_ref, n1_ref, att_ref, gj_a, gj_b, gb_a, gb_b, short_ref,
    keep_a, send_a, keep_b, send_b, n1t_s, attt_s,
):
    step, steps = pl.program_id(0), pl.num_programs(0)
    half, wide = n1_ref.shape[1] // 2, gj_a.shape[1]

    @pl.when(step == 0)
    def _():
        n1t_s[...] = n1_ref[...].T
        attt_s[...] = att_ref[...].T

    def fill(out_a, out_b):
        out_a[0, :half, :wide] = dot(n1t_s[:half, :], gj_a[...]).astype(LOW)
        out_a[0, :half, wide:] = dot(attt_s[:half, :], gb_a[...]).astype(LOW)
        out_a[0, half:, :] = short_ref[0].astype(LOW)
        out_b[0, :, :wide] = dot(n1t_s[half:, :], gj_b[...]).astype(LOW)
        out_b[0, :, wide:] = dot(attt_s[half:, :], gb_b[...]).astype(LOW)

    @pl.when(step < steps // 2)
    def _():
        fill(keep_a, keep_b)

    @pl.when(step >= steps // 2)
    def _():
        fill(send_a, send_b)


def slab_products(order, normed, attended, joined, branch, short):
    rows, features = normed.shape
    wide, narrow = joined.shape[1] // SLABS, branch.shape[1] // SLABS
    extra = short.shape[1]
    half = SLABS // 2

    def kept(step, order):
        return (jnp.minimum(step, half - 1), 0, 0)

    def sent(step, order):
        return (jnp.maximum(step - half, 0), 0, 0)

    shape_a = (1, features // 2 + extra, wide + narrow)
    shape_b = (1, features // 2, wide + narrow)
    return pl.pallas_call(
        products_kernel,
        grid_spec=pltpu.PrefetchScalarGridSpec(
            num_scalar_prefetch=1,
            grid=(SLABS,),
            in_specs=[
                whole_block(normed.shape),
                whole_block(attended.shape),
                pl.BlockSpec((rows, wide), lambda step, order: (0, order[0, step])),
                pl.BlockSpec((rows, wide), lambda step, order: (0, order[1, step])),
                pl.BlockSpec((rows, narrow), lambda step, order: (0, order[0, step])),
                pl.BlockSpec((rows, narrow), lambda step, order: (0, order[1, step])),
                pl.BlockSpec((1,) + short.shape[1:], lambda step, order: (order[0, step], 0, 0)),
            ],
            out_specs=[
                pl.BlockSpec(shape_a, kept),
                pl.BlockSpec(shape_a, sent),
                pl.BlockSpec(shape_b, kept),
                pl.BlockSpec(shape_b, sent),
            ],
            scratch_shapes=[pltpu.VMEM((features, rows), LOW), pltpu.VMEM((features, rows), LOW)],
        ),
        out_shape=[
            jax.ShapeDtypeStruct((half,) + shape_a[1:], LOW),
            jax.ShapeDtypeStruct((half,) + shape_a[1:], LOW),
            jax.ShapeDtypeStruct((half,) + shape_b[1:], LOW),
            jax.ShapeDtypeStruct((half,) + shape_b[1:], LOW),
        ],
        compiler_params=pltpu.CompilerParams(vmem_limit_bytes=40 * MIB),
        name="slab_products",
    )(order, normed, attended, joined, joined, branch, branch, short)


BITS = ((0, 1, 2), (0, 2, 1))


def slab_order():
    place = jnp.arange(SLABS, dtype=jnp.int32)
    if lax.axis_size("batch") != SLABS:
        return jnp.stack([place, place])
    orders = []
    for bits in BITS:
        apart = sum(((place >> (2 - j)) & 1) << bit for j, bit in enumerate(bits))
        orders.append(apart ^ lax.axis_index("batch"))
    return jnp.stack(orders)


def sum_over_batch(keep, send, bits):
    total = None
    for bit in bits:
        if total is not None:
            half = total.shape[0] // 2
            keep, send = total[:half], total[half:].astype(LOW)
        pairs = [(i, i ^ (1 << bit)) for i in range(SLABS)]
        arrived = lax.ppermute(send, "batch", pairs)
        total = keep.astype(jnp.float32) + arrived.astype(jnp.float32)
    return total[0].astype(LOW)


def share_rows(grad):
    part = lax.psum_scatter(grad, "batch", scatter_dimension=0, tiled=True)
    return lax.psum(part, "tok")


def on_device(
    block_input,
    crop_ids,
    ln1_gain,
    ln1_bias,
    w_qkv,
    q_bias,
    v_bias,
    w_out,
    out_bias,
    ln2_gain,
    ln2_bias,
    w_fc1,
    fc1_bias,
    w_fc2,
    fc2_bias,
    out_grad,
):
    packs, local_rows, features = block_input.shape
    rows = packs * local_rows
    send, receive, overflow = exchange_plan(crop_ids)
    low_input = move_rows(send, receive, block_input.reshape(rows, features))
    held_back, low_input = lax.optimization_barrier((out_grad.reshape(rows, features), low_input))
    low_grad = move_rows(send, receive, held_back)
    inputs = low_input.astype(jnp.float32)
    normed_one, norm_one_back, query, key, value = project_qkv(
        inputs, ln1_gain, ln1_bias, w_qkv, q_bias, v_bias
    )
    joined = jnp.concatenate([query, key, value], axis=-1)
    attended = image_attention(joined)
    vectors = jnp.stack([out_bias, ln2_gain, ln2_bias, fc2_bias] + [jnp.zeros_like(out_bias)] * 4)
    output, normed_two_turned, hat, rstd, hidden, slope = feed_forward(
        low_input, attended, w_out, vectors, w_fc1, fc1_bias[None], w_fc2
    )
    output = move_rows(receive, send, output)

    order = slab_order()
    parts = 2
    backs = [
        feed_back(order, part, parts, low_grad, normed_two_turned, w_fc1, w_fc2, hidden, slope)
        for part in range(parts)
    ]
    grad_fc1_bias = jnp.stack([back[5].reshape(SLABS, -1) for back in backs], axis=1).reshape(-1)

    hat = hat.astype(jnp.float32)
    grad_normed = sum(back[0] for back in backs)
    grad_ln2_gain = jnp.sum(grad_normed * hat, axis=0)
    grad_ln2_bias = jnp.sum(grad_normed, axis=0)
    scaled = grad_normed * ln2_gain
    inner = scaled - jnp.mean(scaled, axis=-1, keepdims=True)
    inner = inner - hat * jnp.mean(scaled * hat, axis=-1, keepdims=True)
    grad_resid = low_grad.astype(jnp.float32) + inner * rstd[:, :1]
    grad_branch = grad_resid.astype(LOW)
    grad_attended = dot_back(grad_branch, w_out).astype(LOW)
    grad_joined = image_attention_back(joined, grad_attended)
    grad_joined_bias = row_sum(grad_joined)
    input_term, grad_ln1_gain, grad_ln1_bias = norm_one_back(dot_back(grad_joined, w_qkv))
    input_grad = (grad_resid + input_term).astype(LOW)
    input_grad = move_rows(receive, send, input_grad)

    short = [
        grad_ln1_gain,
        grad_ln1_bias,
        grad_joined_bias[:features],
        grad_joined_bias[2 * features :],
        row_sum(grad_branch),
        grad_ln2_gain,
        grad_ln2_bias,
        row_sum(low_grad),
        grad_fc1_bias,
        jnp.broadcast_to(overflow.astype(jnp.float32), (SLABS * features // 2,)),
    ]
    short_slabs = jnp.concatenate([one.reshape(SLABS, -1) for one in short], axis=1)
    slab_width = 4 * features // SLABS
    short_slabs = jnp.pad(short_slabs.reshape(SLABS, -1, slab_width), ((0, 0), (0, 12), (0, 0)))
    products = slab_products(order, normed_one, attended, grad_joined, grad_branch, short_slabs)

    shards = lax.axis_size("batch")
    if shards == SLABS:
        first, second = [], []
        for back in backs:
            one = sum_over_batch(back[1], back[2], BITS[0])
            two = sum_over_batch(
                back[3].reshape(SLABS // 2, features // SLABS, -1),
                back[4].reshape(SLABS // 2, features // SLABS, -1),
                BITS[1],
            )
            one, two = lax.psum((one, two), "tok")
            first.append(one)
            second.append(two.reshape(features // SLABS, SLABS, -1))
        top, bottom = lax.psum(
            (
                sum_over_batch(products[0], products[1], BITS[0]),
                sum_over_batch(products[2], products[3], BITS[1]),
            ),
            "tok",
        )
        grad_fc1 = jnp.concatenate(first, axis=1)
        grad_fc2 = jnp.stack(second, axis=2).reshape(features // SLABS, -1).T
        grad_attention = jnp.concatenate([top[: features // 2], bottom], axis=0)
        tail = top[features // 2 :].reshape(-1).astype(jnp.float32)
        size = features // SLABS
        pieces = [tail[i * size : (i + 1) * size] for i in range(8)]
        pieces += [tail[8 * size : 12 * size], tail[12 * size :][:1]]
        grad_qkv, grad_out = grad_attention[:, : 3 * size], grad_attention[:, 3 * size :]
    else:
        fc1 = [jnp.concatenate([back[1], back[2]]) for back in backs]
        grad_fc1 = jnp.stack(fc1, axis=2).transpose(1, 0, 2, 3).reshape(features, -1)
        fc2 = [jnp.concatenate([back[3], back[4]]).reshape(features, SLABS, -1) for back in backs]
        grad_fc2 = share_rows(jnp.stack(fc2, axis=2).reshape(features, -1)).T
        top = jnp.concatenate([products[0], products[1]])[:, : features // 2]
        both = jnp.concatenate([top, jnp.concatenate([products[2], products[3]])], axis=1)
        size = features // SLABS
        grad_qkv = both[:, :, : 3 * size].transpose(1, 0, 2).reshape(features, -1)
        grad_out = both[:, :, 3 * size :].transpose(1, 0, 2).reshape(features, -1)
        grad_fc1, grad_qkv, grad_out = (
            share_rows(one.T).T for one in (grad_fc1, grad_qkv, grad_out)
        )
        widths = [one.shape[0] // shards for one in short]
        packed = jnp.concatenate([one.reshape(shards, -1) for one in short], axis=1)
        packed = share_rows(packed)[0]
        pieces, at = [], 0
        for width in widths:
            pieces.append(packed[at : at + width])
            at += width
    fast = (
        output.reshape(block_input.shape),
        input_grad.reshape(block_input.shape),
        pieces[0],
        pieces[1],
        grad_qkv.astype(jnp.float32),
        pieces[2],
        pieces[3],
        grad_out.astype(jnp.float32),
        pieces[4],
        pieces[5],
        pieces[6],
        grad_fc1.astype(jnp.float32),
        pieces[8],
        grad_fc2.astype(jnp.float32),
        pieces[7],
    )

    def unfinished(state):
        return state[0] > 0.5

    def redo(state):
        return (
            jnp.float32(0.0),
            in_place(
                block_input,
                crop_ids,
                ln1_gain,
                ln1_bias,
                w_qkv,
                q_bias,
                v_bias,
                w_out,
                out_bias,
                ln2_gain,
                ln2_bias,
                w_fc1,
                fc1_bias,
                w_fc2,
                fc2_bias,
                out_grad,
            ),
        )

    return lax.while_loop(unfinished, redo, (pieces[9][0], fast))[1]


def solution(mesh):
    in_specs = (
        P("batch", "tok", None),
        P("batch", None),
        P(),
        P(),
        P(),
        P(),
        P(),
        P(),
        P(),
        P(),
        P(),
        P(),
        P(),
        P(),
        P(),
        P("batch", "tok", None),
    )
    out_specs = (
        P("batch", "tok", None),
        P("batch", "tok", None),
        P("batch"),
        P("batch"),
        P(None, "batch"),
        P("batch"),
        P("batch"),
        P(None, "batch"),
        P("batch"),
        P("batch"),
        P("batch"),
        P(None, "batch"),
        P("batch"),
        P(None, "batch"),
        P("batch"),
    )
    return jax.shard_map(
        on_device, mesh=mesh, in_specs=in_specs, out_specs=out_specs, check_vma=False
    )
```

```python
import jax
import jax.numpy as jnp
from jax import lax
from jax.experimental import pallas as pl
from jax.experimental.pallas import tpu as pltpu
from jax.sharding import PartitionSpec as P

H = 16
HD = 64
IMAGE = 160
LOW = jnp.bfloat16


epsilon = 1e-06
masked_score = -1000000000.0


def layer_norm(values, gain, shift):
    center = values - jnp.mean(values, axis=-1, keepdims=True)
    variance = jnp.mean(center * center, axis=-1, keepdims=True)
    return center * lax.rsqrt(variance + epsilon) * gain + shift


def split_heads(values):
    return values.reshape(values.shape[0], H, HD)


def join_heads(values):
    return values.reshape(values.shape[0], H * HD)


def column_sum(values):
    return jnp.sum(values.astype(jnp.float32), axis=(0, 1))


def project_qkv(inputs, ln1_gain, ln1_bias, w_qkv, q_bias, v_bias):
    normed, norm_back = jax.vjp(layer_norm, inputs, ln1_gain, ln1_bias)
    normed_low = normed.astype(jnp.bfloat16)
    joined = jnp.dot(normed_low, w_qkv, preferred_element_type=jnp.float32)
    features = inputs.shape[-1]
    query_low = (joined[..., :features] + q_bias).astype(jnp.bfloat16)
    key_low = joined[..., features : 2 * features].astype(jnp.bfloat16)
    value_low = (joined[..., 2 * features :] + v_bias).astype(jnp.bfloat16)
    return (normed_low, norm_back, query_low, key_low, value_low)


def pack_scores(query_pack, key_pack, same_pack):
    raw = jnp.einsum(
        "shd,lhd->hsl",
        split_heads(query_pack),
        split_heads(key_pack),
        preferred_element_type=jnp.float32,
    )
    return jnp.where(same_pack[None], raw * HD ** (-0.5), masked_score)


def attend_forward(pieces):
    query_pack, key_pack, value_pack, same_pack = pieces
    scores = pack_scores(query_pack, key_pack, same_pack)
    row_max = jnp.max(scores, axis=-1, keepdims=True)
    expo = jnp.exp(scores - row_max)
    totals = jnp.sum(expo, axis=-1, keepdims=True)
    log_total = row_max + jnp.log(totals)
    prob_low = (expo / totals).astype(jnp.bfloat16)
    mixed = jnp.einsum(
        "hsl,lhd->shd", prob_low, split_heads(value_pack), preferred_element_type=jnp.float32
    )
    return (join_heads(mixed).astype(jnp.bfloat16), log_total)


def attend_backward(pieces):
    query_pack, key_pack, value_pack, same_pack, log_total, grad_pack = pieces
    score_scale = HD ** (-0.5)
    scores_again = pack_scores(query_pack, key_pack, same_pack)
    prob_full = jnp.exp(scores_again - log_total)
    prob_back = prob_full.astype(jnp.bfloat16)
    grad_heads = split_heads(grad_pack)
    grad_prob = jnp.einsum(
        "shd,lhd->hsl", grad_heads, split_heads(value_pack), preferred_element_type=jnp.float32
    )
    spread = jnp.sum(prob_full * grad_prob, axis=-1, keepdims=True)
    grad_scores = (prob_full * (grad_prob - spread)).astype(jnp.bfloat16)
    grad_query = join_heads(
        jnp.einsum(
            "hsl,lhd->shd", grad_scores, split_heads(key_pack), preferred_element_type=jnp.float32
        )
        * score_scale
    ).astype(jnp.bfloat16)
    key_terms = join_heads(
        jnp.einsum(
            "hsl,shd->lhd", grad_scores, split_heads(query_pack), preferred_element_type=jnp.float32
        )
        * score_scale
    )
    value_terms = join_heads(
        jnp.einsum("hsl,shd->lhd", prob_back, grad_heads, preferred_element_type=jnp.float32)
    )
    return (grad_query, key_terms, value_terms)


def swap(values, axis, apart):
    return lax.ppermute(values, axis, [(i, i ^ apart) for i in range(lax.axis_size(axis))])


def gather_tokens(values):
    groups, me = lax.axis_size("tok"), lax.axis_index("tok")
    held = jnp.stack([values] + [swap(values, "tok", step) for step in range(1, groups)])
    return jnp.concatenate(
        [lax.dynamic_index_in_dim(held, me ^ at, 0, False) for at in range(groups)], axis=1
    )


def scatter_tokens(values):
    groups, me = lax.axis_size("tok"), lax.axis_index("tok")
    length = values.shape[1] // groups

    def part(at):
        return lax.dynamic_slice_in_dim(values, at * length, length, 1)

    return part(me) + sum(swap(part(me ^ step), "tok", step) for step in range(1, groups))


def sum_tokens(values):
    groups, me = lax.axis_size("tok"), lax.axis_index("tok")
    held, bits = values, []
    bit = 1
    while bit < groups:
        bits.append(bit)
        pairs = held.reshape((held.shape[0] // 2, 2) + held.shape[1:])
        own = jnp.where(me & bit, 1, 0)
        other = lax.dynamic_index_in_dim(pairs, 1 - own, 1, False).astype(LOW)
        held = lax.dynamic_index_in_dim(pairs, own, 1, False).astype(jnp.float32)
        held = held + swap(other, "tok", bit).astype(jnp.float32)
        bit *= 2
    held = held.astype(LOW)
    for bit in reversed(bits):
        arrived = swap(held, "tok", bit)
        own = (me & bit) > 0
        held = jnp.where(own, jnp.stack([arrived, held], 1), jnp.stack([held, arrived], 1))
        held = held.reshape((-1,) + held.shape[2:])
    return held


def share_slabs(slabs):
    me, held = lax.axis_index("batch"), slabs
    bit = 1
    while bit < lax.axis_size("batch"):
        pairs = held.reshape((held.shape[0] // 2, 2) + held.shape[1:])
        own = jnp.where(me & bit, 1, 0)
        other = lax.dynamic_index_in_dim(pairs, 1 - own, 1, False).astype(LOW)
        held = lax.dynamic_index_in_dim(pairs, own, 1, False).astype(jnp.float32)
        held = held + swap(other, "batch", bit).astype(jnp.float32)
        bit *= 2
    flat = held[0].reshape(-1)
    groups = lax.axis_size("tok")
    padded = jnp.pad(flat, (0, -flat.size % groups)).astype(LOW).reshape(groups, -1)
    return sum_tokens(padded).reshape(-1)[: flat.size].reshape(slabs.shape[1:])


def share_columns(grad):
    shards = lax.axis_size("batch")
    if grad.ndim == 1:
        return share_slabs(grad.astype(LOW).reshape(shards, -1)).astype(jnp.float32)
    slabs = grad.astype(LOW).reshape(grad.shape[0], shards, -1).transpose(1, 0, 2)
    return share_slabs(slabs).astype(jnp.float32)


def in_place(
    block_input,
    crop_ids,
    ln1_gain,
    ln1_bias,
    w_qkv,
    q_bias,
    v_bias,
    w_out,
    out_bias,
    ln2_gain,
    ln2_bias,
    w_fc1,
    fc1_bias,
    w_fc2,
    fc2_bias,
    out_grad,
):
    packs, local_rows, features = block_input.shape
    offset = lax.axis_index("tok") * local_rows
    own_crop = lax.dynamic_slice_in_dim(crop_ids, offset, local_rows, 1)
    same_crop = own_crop[:, :, None] == crop_ids[:, None, :]
    inputs = block_input.astype(jnp.float32)
    normed_one, norm_one_back, query_low, key_low, value_low = project_qkv(
        inputs, ln1_gain, ln1_bias, w_qkv, q_bias, v_bias
    )
    key_all, value_all = (
        gather_tokens(key_low),
        gather_tokens(value_low),
    )
    attended, log_total = lax.map(attend_forward, (query_low, key_all, value_all, same_crop))
    resid = inputs + jnp.dot(attended, w_out, preferred_element_type=jnp.float32) + out_bias
    normed_two, norm_two_back = jax.vjp(layer_norm, resid, ln2_gain, ln2_bias)
    normed_two_low = normed_two.astype(jnp.bfloat16)
    pre_act = jnp.dot(normed_two_low, w_fc1, preferred_element_type=jnp.float32) + fc1_bias

    def gelu_exact(values):
        return jax.nn.gelu(values, approximate=False)

    activated, gelu_back = jax.vjp(gelu_exact, pre_act)
    hidden = activated.astype(jnp.bfloat16)
    output = resid + jnp.dot(hidden, w_fc2, preferred_element_type=jnp.float32) + fc2_bias
    out_grad_full = out_grad.astype(jnp.float32)
    grad_fc2 = jnp.einsum("bsf,bsd->fd", hidden, out_grad, preferred_element_type=jnp.float32)
    grad_fc2_bias = column_sum(out_grad)
    grad_hidden = jnp.einsum("bsd,fd->bsf", out_grad, w_fc2, preferred_element_type=jnp.float32)
    grad_pre = gelu_back(grad_hidden)[0].astype(jnp.bfloat16)
    grad_fc1 = jnp.einsum(
        "bsd,bsf->df", normed_two_low, grad_pre, preferred_element_type=jnp.float32
    )
    grad_fc1_bias = column_sum(grad_pre)
    grad_normed_two = jnp.einsum("bsf,df->bsd", grad_pre, w_fc1, preferred_element_type=jnp.float32)
    resid_term, grad_ln2_gain, grad_ln2_bias = norm_two_back(grad_normed_two)
    grad_resid = out_grad_full + resid_term
    grad_branch = grad_resid.astype(jnp.bfloat16)
    grad_out = jnp.einsum("bsd,bse->de", attended, grad_branch, preferred_element_type=jnp.float32)
    grad_out_bias = column_sum(grad_branch)
    grad_attended = jnp.einsum(
        "bse,de->bsd", grad_branch, w_out, preferred_element_type=jnp.float32
    ).astype(jnp.bfloat16)
    normed_one, norm_one_back, query_low, key_low, value_low = project_qkv(
        inputs, ln1_gain, ln1_bias, w_qkv, q_bias, v_bias
    )
    key_all, value_all = (
        gather_tokens(key_low),
        gather_tokens(value_low),
    )
    grad_query, key_terms, value_terms = lax.map(
        attend_backward, (query_low, key_all, value_all, same_crop, log_total, grad_attended)
    )
    grad_key_sum, grad_value_sum = (
        scatter_tokens(key_terms),
        scatter_tokens(value_terms),
    )
    grad_key = grad_key_sum.astype(jnp.bfloat16)
    grad_value = grad_value_sum.astype(jnp.bfloat16)
    grad_joined = jnp.concatenate([grad_query, grad_key, grad_value], axis=-1)
    grad_qkv = jnp.einsum(
        "bsd,bse->de", normed_one, grad_joined, preferred_element_type=jnp.float32
    )
    grad_q_bias = column_sum(grad_query)
    grad_v_bias = column_sum(grad_value)
    grad_normed_one = jnp.einsum(
        "bse,de->bsd", grad_joined, w_qkv, preferred_element_type=jnp.float32
    )
    input_term, grad_ln1_gain, grad_ln1_bias = norm_one_back(grad_normed_one)
    input_grad = (grad_resid + input_term).astype(jnp.bfloat16)
    summed = [
        share_columns(grad)
        for grad in (
            grad_ln1_gain,
            grad_ln1_bias,
            grad_qkv,
            grad_q_bias,
            grad_v_bias,
            grad_out,
            grad_out_bias,
            grad_ln2_gain,
            grad_ln2_bias,
            grad_fc1,
            grad_fc1_bias,
            grad_fc2,
            grad_fc2_bias,
        )
    ]
    return (
        output.astype(jnp.bfloat16),
        input_grad,
        summed[0],
        summed[1],
        summed[2],
        summed[3],
        summed[4],
        summed[5],
        summed[6],
        summed[7],
        summed[8],
        summed[9],
        summed[10],
        summed[11],
        summed[12],
    )


def crop_of_row(axis):
    row = lax.broadcasted_iota(jnp.int32, (IMAGE, IMAGE), axis)
    return jnp.where(row < 50, 0, jnp.where(row < 100, 1, 2 + (row - 100) // 10))


def head_halves(dtype):
    lane = lax.broadcasted_iota(jnp.int32, (1, 2 * HD), 1)
    first = (lane < HD).astype(jnp.float32)
    return first, (first.astype(dtype), (1.0 - first).astype(dtype))


def head_prob(query_half, keys, same_crop):
    raw = lax.dot_general(
        query_half, keys, (((1,), (1,)), ((), ())), preferred_element_type=jnp.float32
    )
    scores = jnp.where(same_crop, raw * HD ** (-0.5), masked_score)
    expo = jnp.exp(scores - jnp.max(scores, axis=-1, keepdims=True))
    return expo / jnp.sum(expo, axis=-1, keepdims=True)


def attend_image(joined_ref, out_ref):
    features = out_ref.shape[1]
    same_crop = crop_of_row(0) == crop_of_row(1)
    first, halves = head_halves(joined_ref.dtype)
    for at in range(0, features, 2 * HD):
        query = joined_ref[:, at : at + 2 * HD]
        keys = joined_ref[:, features + at : features + at + 2 * HD]
        values = joined_ref[:, 2 * features + at : 2 * features + at + 2 * HD]
        mixed = []
        for half in halves:
            prob = head_prob(query * half, keys, same_crop).astype(jnp.bfloat16)
            mixed.append(jnp.dot(prob, values, preferred_element_type=jnp.float32))
        both = mixed[0] * first + mixed[1] * (1.0 - first)
        out_ref[:, at : at + 2 * HD] = both.astype(out_ref.dtype)


def image_attention(joined, after):
    rows, width = joined.shape
    return call(
        attend_image,
        "attention",
        (rows // IMAGE,),
        [(joined, pl.BlockSpec((IMAGE, width), lambda step: (step, 0)))],
        [((rows, width // 3), LOW, pl.BlockSpec((IMAGE, width // 3), lambda step: (step, 0)))],
        flops=8 * MICROSECOND,
        after=after,
    )[0]


def exchange_plan(crop_ids):
    packs, length = crop_ids.shape
    groups, me = lax.axis_size("tok"), lax.axis_index("tok")
    local = length // groups
    rows = packs * local
    capacity = -(-rows * 13 // (groups * 10) // 16) * 16
    order = crop_ids * length + jnp.arange(length, dtype=jnp.int32)
    rank = jnp.sum((order[:, None, :] < order[:, :, None]).astype(jnp.int32), axis=-1)
    target = rank // local

    def by_source(values):
        return values.reshape(packs, groups, local).transpose(1, 0, 2).reshape(groups, rows)

    target = by_source(target)
    place = by_source(rank % local + local * jnp.arange(packs, dtype=jnp.int32)[:, None])
    number = jnp.arange(rows, dtype=jnp.int32)
    earlier = number[None, :] < number[:, None]
    slot = jnp.sum(
        ((target[:, :, None] == target[:, None, :]) & earlier).astype(jnp.int32), axis=-1
    )
    overflow = jnp.max(slot) >= capacity
    fits = slot < capacity
    own = lax.dynamic_index_in_dim
    send_at = jnp.where(
        own(fits, me, 0, False), (own(target, me, 0, False) ^ me) * capacity + own(slot, me, 0, False), -1
    )
    source = jnp.arange(groups, dtype=jnp.int32)[:, None]
    arrive_at = jnp.where((target == me) & fits, (source ^ me) * capacity + slot + 1, 0)
    hits = (place[None] == number[:, None, None]) & (target == me)[None]
    receive_at = jnp.sum(jnp.where(hits, arrive_at[None], 0), axis=(1, 2)) - 1
    lanes = jnp.arange(groups * capacity, dtype=jnp.int32)
    send, receive = ((at[:, None] == lanes).astype(LOW) for at in (send_at, receive_at))
    send_turned, receive_turned = (
        (lanes[:, None] == at).astype(LOW) for at in (send_at, receive_at)
    )
    return send, receive, send_turned, receive_turned, overflow


def gather_rows(choice, values):
    return jnp.dot(choice, values, preferred_element_type=jnp.float32).astype(jnp.bfloat16)


SLABS = 8
MIB = 1024 * 1024
MICROSECOND = 1000 * 1000 * 1000


def dot(left, right):
    return jnp.dot(left, right, preferred_element_type=jnp.float32)


def dot_back(left, weight):
    return lax.dot_general(
        left, weight, (((1,), (1,)), ((), ())), preferred_element_type=jnp.float32
    )


def gelu_and_slope(z):
    tail = jnp.exp(z * z * -0.5)
    t = 1.0 / (1.0 + (0.3275911 * 0.5**0.5) * jnp.abs(z))
    series = 0.7107068705 + t * (-0.7265760135 + t * 0.5307027145)
    beyond = tail * (t * (0.127414796 + t * (-0.142248368 + t * series)))
    below = jnp.where(z >= 0.0, 1.0 - beyond, beyond)
    return z * below, below + z * tail * 0.3989422804014327


def whole_block(shape):
    return pl.BlockSpec(shape, lambda step, *_: (0,) * len(shape))


UNREAD = pl.BlockSpec(memory_space=pl.ANY)


BIG = 2 * MIB


def place_of(shape, dtype):
    size = dtype.dtype.itemsize
    for extent in shape:
        size *= extent
    return pltpu.HBM(shape, dtype) if size >= BIG else jax.ShapeDtypeStruct(shape, dtype)


def stay(array):
    if array.size * array.dtype.itemsize > BIG:
        return pltpu.with_memory_space_constraint(array, pltpu.HBM)
    return array


def call(kernel, name, grid, ins, outs, flops, scratch=(), order=None, after=(), aliases=None):
    first = 0 if order is None else 1
    given = first + len(ins)

    def body(*refs):
        kernel(*refs[:given], *refs[given + len(after) :])

    return pl.pallas_call(
        body,
        grid_spec=pltpu.PrefetchScalarGridSpec(
            num_scalar_prefetch=first,
            grid=grid,
            in_specs=[spec for _, spec in ins] + [UNREAD] * len(after),
            out_specs=[spec for _, _, spec in outs],
            scratch_shapes=list(scratch),
        ),
        out_shape=[place_of(shape, dtype) for shape, dtype, _ in outs],
        input_output_aliases=aliases or {},
        compiler_params=pltpu.CompilerParams(vmem_limit_bytes=40 * MIB),
        cost_estimate=pl.CostEstimate(flops=flops, bytes_accessed=0, transcendentals=0),
        name=name,
    )(*([] if order is None else [order]), *[stay(array) for array, _ in ins], *after)


def hold_until(values, after):
    count = len(values)
    return pl.pallas_call(
        lambda *refs: None,
        in_specs=[UNREAD] * (count + len(after)),
        out_specs=[UNREAD] * count,
        out_shape=[jax.ShapeDtypeStruct(one.shape, one.dtype) for one in values],
        input_output_aliases={i: i for i in range(count)},
        name="hold_until",
    )(*values, *after)


def project_kernel(
    part0, part1, part2, part3, receive_ref, vec_ref, w_ref, bias_ref,
    x_ref, normed_ref, joined_ref, parcels,
):
    rows = x_ref.shape[0]
    chunk = rows // 4
    size = part0.shape[0]

    @pl.when(pl.program_id(0) == 0)
    def _():
        for i, ref in enumerate((part0, part1, part2, part3)):
            parcels[i * size : (i + 1) * size, :] = ref[...]

        def part(i, carry):
            at = pl.ds(pl.multiple_of(i * chunk, chunk), chunk)
            x = dot(receive_ref[at, :], parcels[...])
            x_ref[at, :] = x.astype(LOW)
            center = x - jnp.mean(x, axis=-1, keepdims=True)
            rstd = lax.rsqrt(jnp.mean(center * center, axis=-1, keepdims=True) + epsilon)
            normed = center * rstd * vec_ref[4:5, :] + vec_ref[5:6, :]
            normed_ref[at, :] = normed.astype(LOW)
            return carry

        lax.fori_loop(0, rows // chunk, part, 0)

    joined_ref[...] = (dot(normed_ref[...], w_ref[...]) + bias_ref[...]).astype(LOW)


def project(parts, receive, vectors, w_qkv, bias):
    rows, features = receive.shape[0], w_qkv.shape[0]
    block = features // 2
    return call(
        project_kernel,
        "project",
        (w_qkv.shape[1] // block,),
        [(part, whole_block(part.shape)) for part in parts]
        + [
            (receive, whole_block(receive.shape)),
            (vectors, whole_block(vectors.shape)),
            (w_qkv, pl.BlockSpec((features, block), lambda step: (0, step))),
            (bias, pl.BlockSpec((1, block), lambda step: (0, step))),
        ],
        [
            ((rows, features), LOW, whole_block((rows, features))),
            ((rows, features), LOW, whole_block((rows, features))),
            ((rows, w_qkv.shape[1]), LOW, pl.BlockSpec((rows, block), lambda step: (0, step))),
        ],
        flops=10 * MICROSECOND,
        scratch=[pltpu.VMEM((4 * parts[0].shape[0], features), LOW)],
    )


def feed_forward_kernel(
    x_ref, att_ref, w_out_ref, vec_ref, w1_ref, b1_ref, w2_ref, turn_ref,
    part0, part1, part2, part3, n2t_ref, hat_ref, rstd_ref, hidden_ref, slope_ref,
    n2_s, acc_s,
):
    step, steps = pl.program_id(0), pl.num_programs(0)
    rows = x_ref.shape[0]
    chunk = rows // 4

    @pl.when(step == 0)
    def _():
        def part(i, carry):
            at = pl.ds(pl.multiple_of(i * chunk, chunk), chunk)
            resid = x_ref[at, :].astype(jnp.float32) + dot(att_ref[at, :], w_out_ref[...])
            resid = resid + vec_ref[0:1, :]
            center = resid - jnp.mean(resid, axis=-1, keepdims=True)
            rstd = lax.rsqrt(jnp.mean(center * center, axis=-1, keepdims=True) + epsilon)
            hat = center * rstd
            hat_ref[at, :] = hat.astype(LOW)
            rstd_ref[at, :] = jnp.broadcast_to(rstd, (chunk, rstd_ref.shape[1]))
            acc_s[at, :] = resid + vec_ref[3:4, :]
            n2_s[at, :] = (hat * vec_ref[1:2, :] + vec_ref[2:3, :]).astype(LOW)
            return carry

        lax.fori_loop(0, rows // chunk, part, 0)
        n2t_ref[...] = n2_s[...].T

    act, slope = gelu_and_slope(dot(n2_s[...], w1_ref[...]) + b1_ref[...])
    hidden_ref[...] = act.astype(LOW)
    slope_ref[...] = slope.astype(LOW)
    acc_s[...] += dot(hidden_ref[...], w2_ref[...])

    @pl.when(step == steps - 1)
    def _():
        size = part0.shape[0]
        for i, ref in enumerate((part0, part1, part2, part3)):
            ref[...] = dot(turn_ref[i * size : (i + 1) * size, :], acc_s[...].astype(LOW)).astype(LOW)


def parcels_out(turned, features):
    shape = (turned.shape[0] // 4, features)
    return [(shape, LOW, whole_block(shape))] * 4


def feed_forward(x, attended, w_out, vectors, w1, b1, w2, turned):
    rows, features = x.shape
    width = w1.shape[1]
    block = width // SLABS
    grown = pl.BlockSpec((rows, block), lambda step: (0, step))
    return call(
        feed_forward_kernel,
        "feed_forward",
        (SLABS,),
        [
            (x, whole_block(x.shape)),
            (attended, whole_block(x.shape)),
            (w_out, whole_block(w_out.shape)),
            (vectors, whole_block(vectors.shape)),
            (w1, pl.BlockSpec((features, block), lambda step: (0, step))),
            (b1, pl.BlockSpec((1, block), lambda step: (0, step))),
            (w2, pl.BlockSpec((block, features), lambda step: (step, 0))),
            (turned, whole_block(turned.shape)),
        ],
        parcels_out(turned, features)
        + [
            ((features, rows), LOW, whole_block((features, rows))),
            (x.shape, LOW, whole_block(x.shape)),
            ((rows, 128), jnp.float32, whole_block((rows, 128))),
            ((rows, width), LOW, grown),
            ((rows, width), LOW, grown),
        ],
        flops=27 * MICROSECOND,
        scratch=[pltpu.VMEM(x.shape, LOW), pltpu.VMEM(x.shape, jnp.float32)],
    )


def kept(step, order):
    return (jnp.minimum(step, SLABS // 2 - 1), 0, 0)


def sent(step, order):
    return (jnp.maximum(step - SLABS // 2, 0), 0, 0)


def halves_out(extra, rows, width):
    outs = []
    for more in (extra, 0):
        shape = (rows + more, width)
        for place in (kept, sent):
            outs.append(((SLABS // 2,) + shape, LOW, pl.BlockSpec((1,) + shape, place)))
    return outs


def feed_back_kernel(
    order_ref, og_ref, n2t_ref, w1_ref, w2_ref, hidden_ref, slope_ref,
    dn2_ref, keep1_ref, send1_ref, keep2_ref, send2_ref, db1_ref, ogt_s,
):
    step, steps = pl.program_id(0), pl.num_programs(0)
    features = og_ref.shape[1]
    slab, half = features // SLABS, features // 2

    @pl.when(step == 0)
    def _():
        for p in range(SLABS):
            at = pl.multiple_of(order_ref[1, p] * slab, slab)
            ogt_s[p * slab : (p + 1) * slab, :] = og_ref[:, pl.ds(at, slab)].T
        dn2_ref[...] = jnp.zeros_like(dn2_ref)

    hidden = hidden_ref[...]
    grad = dot_back(og_ref[...], w2_ref[...]) * slope_ref[...].astype(jnp.float32)
    grad = grad.astype(LOW)
    keep2_ref[0] = dot(ogt_s[:half, :], hidden).astype(LOW)
    send2_ref[0] = dot(ogt_s[half:, :], hidden).astype(LOW)
    db1_ref[...] = column_total(grad.astype(jnp.float32))
    dn2_ref[...] += dot_back(grad, w1_ref[...])
    dw1 = dot(n2t_ref[...], grad).astype(LOW)

    @pl.when(step < steps // 2)
    def _():
        keep1_ref[0] = dw1

    @pl.when(step >= steps // 2)
    def _():
        send1_ref[0] = dw1


def feed_back(order, part, parts, og, n2t, w1, w2, hidden, slope, after):
    rows, features = og.shape
    width = w1.shape[1]
    block = width // (SLABS * parts)
    half = SLABS // 2

    def at(step, order):
        return order[0, step] * parts + part

    columns = pl.BlockSpec((rows, block), lambda step, order: (0, at(step, order)))
    turned = pl.BlockSpec(
        (1, features // 2, block), lambda step, order: (order[0, step], 0, 0)
    )
    return call(
        feed_back_kernel,
        "feed_back",
        (SLABS,),
        [
            (og, whole_block(og.shape)),
            (n2t, whole_block(n2t.shape)),
            (w1, pl.BlockSpec((features, block), lambda step, order: (0, at(step, order)))),
            (w2, pl.BlockSpec((block, features), lambda step, order: (at(step, order), 0))),
            (hidden, columns),
            (slope, columns),
        ],
        [
            (og.shape, jnp.float32, whole_block(og.shape)),
            ((half, features, block), LOW, pl.BlockSpec((1, features, block), kept)),
            ((half, features, block), LOW, pl.BlockSpec((1, features, block), sent)),
            ((SLABS, features // 2, block), LOW, turned),
            ((SLABS, features // 2, block), LOW, turned),
            (
                (1, SLABS * block),
                jnp.float32,
                pl.BlockSpec((1, block), lambda step, order: (0, order[0, step])),
            ),
        ],
        flops=18 * MICROSECOND,
        scratch=[pltpu.VMEM((features, rows), LOW)],
        order=order,
        after=after,
    )


def norm_back(grad, gain, hat, rstd):
    scaled = grad * gain
    inner = scaled - jnp.mean(scaled, axis=-1, keepdims=True)
    return (inner - hat * jnp.mean(scaled * hat, axis=-1, keepdims=True)) * rstd


def column_total(values):
    return jnp.sum(values, axis=0, keepdims=True)


def second_norm_kernel(
    first_ref, second_ref, og_ref, hat_ref, rstd_ref, vec_ref, w_out_ref,
    branch_ref, att_ref, sums_ref,
):
    @pl.when(pl.program_id(0) == 0)
    def _():
        sums_ref[...] = jnp.zeros_like(sums_ref)

    grad, hat = first_ref[...] + second_ref[...], hat_ref[...].astype(jnp.float32)
    og = og_ref[...].astype(jnp.float32)
    resid = og + norm_back(grad, vec_ref[1:2, :], hat, rstd_ref[:, 0:1])
    branch = resid.astype(LOW)
    branch_ref[...] = branch
    att_ref[...] = dot_back(branch, w_out_ref[...]).astype(LOW)
    sums_ref[0:1, :] += column_total(branch.astype(jnp.float32))
    sums_ref[1:2, :] += column_total(grad * hat)
    sums_ref[2:3, :] += column_total(grad)
    sums_ref[3:4, :] += column_total(og)


def second_norm_back(first, second, og, hat, rstd, vectors, w_out, after):
    rows, features = og.shape
    chunk = pl.BlockSpec((rows // 4, features), lambda step: (step, 0))
    return call(
        second_norm_kernel,
        "second_norm_back",
        (4,),
        [
            (first, chunk),
            (second, chunk),
            (og, chunk),
            (hat, chunk),
            (rstd, pl.BlockSpec((rows // 4, rstd.shape[1]), lambda step: (step, 0))),
            (vectors, whole_block(vectors.shape)),
            (w_out, whole_block(w_out.shape)),
        ],
        [
            (og.shape, LOW, chunk),
            (og.shape, LOW, chunk),
            ((8, features), jnp.float32, whole_block((8, features))),
        ],
        flops=6 * MICROSECOND,
        after=after,
    )


def attend_image_back(joined_ref, grad_ref, out_ref):
    features = grad_ref.shape[1]
    same_crop = crop_of_row(0) == crop_of_row(1)
    first, halves = head_halves(joined_ref.dtype)
    scale = HD ** (-0.5)
    for at in range(0, features, 2 * HD):
        query = joined_ref[:, at : at + 2 * HD]
        keys = joined_ref[:, features + at : features + at + 2 * HD]
        values = joined_ref[:, 2 * features + at : 2 * features + at + 2 * HD]
        grad = grad_ref[:, at : at + 2 * HD]
        terms = []
        for half in halves:
            scores = jnp.where(same_crop, dot_back(keys * half, query) * scale, masked_score)
            expo = jnp.exp(scores - jnp.max(scores, axis=0, keepdims=True))
            prob = expo * (1.0 / jnp.sum(expo, axis=0, keepdims=True))
            grad_prob = dot_back(values * half, grad)
            spread = jnp.sum(prob * grad_prob, axis=0, keepdims=True)
            grad_scores = (prob * (grad_prob - spread)).astype(LOW)
            terms.append(
                (
                    dot(grad_scores.T, keys) * scale,
                    dot(grad_scores, query) * scale,
                    dot(prob.astype(LOW), grad),
                )
            )
        for part in range(3):
            both = terms[0][part] * first + terms[1][part] * (1.0 - first)
            place = part * features + at
            out_ref[:, place : place + 2 * HD] = both.astype(out_ref.dtype)


def image_attention_back(joined, grad, part, parts, earlier, after):
    rows, width = joined.shape
    steps = rows // IMAGE // parts

    def kernel(joined_ref, grad_ref, *rest):
        attend_image_back(joined_ref, grad_ref, rest[-1])

    image = pl.BlockSpec((IMAGE, width), lambda step: (step + part * steps, 0))
    ins = [
        (joined, image),
        (grad, pl.BlockSpec((IMAGE, width // 3), lambda step: (step + part * steps, 0))),
    ]
    if earlier is not None:
        ins.append((earlier, UNREAD))
    return call(
        kernel,
        "attention_back",
        (steps,),
        ins,
        [((rows, width), LOW, image)],
        flops=17 * MICROSECOND,
        after=after,
        aliases=None if earlier is None else {2: 0},
    )[0]


def first_norm_kernel(
    joined_ref, w_ref, x_ref, branch_ref, vec_ref, turn_ref,
    part0, part1, part2, part3, sums_ref, joined_sums_ref, acc_s, out_s,
):
    step, steps = pl.program_id(0), pl.num_programs(0)
    rows = x_ref.shape[0]
    chunk = rows // 4

    @pl.when(step == 0)
    def _():
        acc_s[...] = jnp.zeros_like(acc_s)

    acc_s[...] += dot_back(joined_ref[...], w_ref[...])
    joined_sums_ref[...] = column_total(joined_ref[...].astype(jnp.float32))

    @pl.when(step == steps - 1)
    def _():
        sums_ref[...] = jnp.zeros_like(sums_ref)

        def part(i, carry):
            at = pl.ds(pl.multiple_of(i * chunk, chunk), chunk)
            x = x_ref[at, :].astype(jnp.float32)
            center = x - jnp.mean(x, axis=-1, keepdims=True)
            rstd = lax.rsqrt(jnp.mean(center * center, axis=-1, keepdims=True) + epsilon)
            grad, hat = acc_s[at, :], center * rstd
            term = norm_back(grad, vec_ref[4:5, :], hat, rstd)
            out_s[at, :] = (branch_ref[at, :].astype(jnp.float32) + term).astype(LOW)
            sums_ref[0:1, :] += column_total(grad * hat)
            sums_ref[1:2, :] += column_total(grad)
            return carry

        lax.fori_loop(0, rows // chunk, part, 0)
        size = part0.shape[0]
        for i, ref in enumerate((part0, part1, part2, part3)):
            ref[...] = dot(turn_ref[i * size : (i + 1) * size, :], out_s[...]).astype(LOW)


def first_norm_back(grad_joined, w_qkv, x, branch, vectors, turned, after):
    rows, features = x.shape
    block = features // 2
    return call(
        first_norm_kernel,
        "first_norm_back",
        (w_qkv.shape[1] // block,),
        [
            (grad_joined, pl.BlockSpec((rows, block), lambda step: (0, step))),
            (w_qkv, pl.BlockSpec((features, block), lambda step: (0, step))),
            (x, whole_block(x.shape)),
            (branch, whole_block(x.shape)),
            (vectors, whole_block(vectors.shape)),
            (turned, whole_block(turned.shape)),
        ],
        parcels_out(turned, features)
        + [
            ((8, features), jnp.float32, whole_block((8, features))),
            ((1, w_qkv.shape[1]), jnp.float32, pl.BlockSpec((1, block), lambda step: (0, step))),
        ],
        flops=10 * MICROSECOND,
        scratch=[pltpu.VMEM(x.shape, jnp.float32), pltpu.VMEM(x.shape, LOW)],
        after=after,
    )


def products_kernel(
    order_ref, n1_ref, att_ref, gj_a, gj_b, gb_a, gb_b, short_ref,
    keep_a, send_a, keep_b, send_b, n1t_s, attt_s,
):
    step, steps = pl.program_id(0), pl.num_programs(0)
    half, wide = n1_ref.shape[1] // 2, gj_a.shape[1]

    @pl.when(step == 0)
    def _():
        n1t_s[...] = n1_ref[...].T
        attt_s[...] = att_ref[...].T

    def fill(out_a, out_b):
        out_a[0, :half, :wide] = dot(n1t_s[:half, :], gj_a[...]).astype(LOW)
        out_a[0, :half, wide:] = dot(attt_s[:half, :], gb_a[...]).astype(LOW)
        out_a[0, half:, :] = short_ref[0].astype(LOW)
        out_b[0, :, :wide] = dot(n1t_s[half:, :], gj_b[...]).astype(LOW)
        out_b[0, :, wide:] = dot(attt_s[half:, :], gb_b[...]).astype(LOW)

    @pl.when(step < steps // 2)
    def _():
        fill(keep_a, keep_b)

    @pl.when(step >= steps // 2)
    def _():
        fill(send_a, send_b)


def attention_products(order, normed, attended, joined, branch, short, after):
    rows, features = normed.shape
    wide, narrow = joined.shape[1] // SLABS, branch.shape[1] // SLABS
    return call(
        products_kernel,
        "attention_products",
        (SLABS,),
        [
            (normed, whole_block(normed.shape)),
            (attended, whole_block(attended.shape)),
            (joined, pl.BlockSpec((rows, wide), lambda step, order: (0, order[0, step]))),
            (joined, pl.BlockSpec((rows, wide), lambda step, order: (0, order[1, step]))),
            (branch, pl.BlockSpec((rows, narrow), lambda step, order: (0, order[0, step]))),
            (branch, pl.BlockSpec((rows, narrow), lambda step, order: (0, order[1, step]))),
            (short, pl.BlockSpec((1,) + short.shape[1:], lambda step, order: (order[0, step], 0, 0))),
        ],
        halves_out(short.shape[1], features // 2, wide + narrow),
        flops=15 * MICROSECOND,
        scratch=[pltpu.VMEM((features, rows), LOW), pltpu.VMEM((features, rows), LOW)],
        order=order,
        after=after,
    )


BITS = ((1, 2, 4), (1, 4, 2))


def slab_order():
    place = jnp.arange(SLABS, dtype=jnp.int32)
    if lax.axis_size("batch") != SLABS:
        return jnp.stack([place, place])
    orders = []
    for bits in BITS:
        apart = sum(((place >> (2 - j)) & 1) * bit for j, bit in enumerate(bits))
        orders.append(apart ^ lax.axis_index("batch"))
    return jnp.stack(orders)


class Sums:
    def __init__(self, axes, keep_a, send_a, keep_b, send_b):
        self.axes, self.stage = axes, 0
        self.terms, self.send = ([keep_a], [keep_b]), [send_a, send_b]

    def move(self):
        arrived = [swap(send, "batch", bits[self.stage]) for send, bits in zip(self.send, BITS)]
        terms = [own + [other] for own, other in zip(self.terms, arrived)]
        self.stage += 1
        if self.stage == 3:
            return [total(each).reshape(-1, each[0].shape[-1]) for each in terms]
        halves = [
            [jnp.split(one, 2, axis) for one in each] for each, axis in zip(terms, self.axes)
        ]
        self.terms = [[one[0] for one in each] for each in halves]
        self.send = [total([one[1] for one in each]).astype(LOW) for each in halves]
        return list(self.send)

    def hold(self, after):
        self.send = hold_until(list(self.send), after)


def total(terms):
    return sum(one.astype(jnp.float32) for one in terms)


class TokenSum:
    def __init__(self, values):
        self.low = jnp.where(lax.axis_index("tok") & 1, 1, 0)
        self.high = lax.axis_index("tok") >> 1
        pairs = values.reshape((2, 2) + values.shape[1:])
        self.keep = lax.dynamic_index_in_dim(pairs, self.low, 1, False)
        self.send = lax.dynamic_index_in_dim(pairs, 1 - self.low, 1, False).astype(LOW)

    def hold(self, after):
        self.send = hold_until([self.send], after)[0]

    def one(self, beside=()):
        keep = hold_until([self.keep], beside)[0] if beside else self.keep
        whole = keep + swap(self.send, "tok", 1).astype(jnp.float32)
        self.keep = lax.dynamic_index_in_dim(whole, self.high, 0, False)
        self.send = lax.dynamic_index_in_dim(whole, 1 - self.high, 0, False).astype(LOW)
        return self.send

    def two(self, beside=()):
        keep = hold_until([self.keep], beside)[0] if beside else self.keep
        self.send = (keep + swap(self.send, "tok", 2).astype(jnp.float32)).astype(LOW)
        return self.send

    def back(self, apart, own, axis, beside):
        other = swap(self.send, "tok", apart)
        kept = hold_until([self.send], beside)[0] if beside else self.send
        pair = jnp.stack([kept, other], axis), jnp.stack([other, kept], axis)
        return jnp.where(own == 0, pair[0], pair[1])

    def three(self, beside=()):
        self.send = self.back(2, self.high, 0, beside)
        return self.send

    def four(self, beside=()):
        whole = self.back(1, self.low, 1, beside)
        whole = whole.reshape((4,) + whole.shape[2:])
        return [one.reshape(-1, one.shape[-1]) for one in jnp.split(whole, 2, axis=1)]


def token_sum(top, bottom):
    parts = [one.reshape(4, -1, one.shape[1]) for one in (top, bottom)]
    return TokenSum(jnp.concatenate(parts, axis=1))


def spread_parts(turned, values):
    parts = [gather_rows(choice, values) for choice in jnp.split(turned, lax.axis_size("tok"))]
    parts[1] = hold_until(parts[1:2], parts[2:])[0]
    return parts


def swap_groups(parts):
    return [parts[0]] + [swap(parts[step], "tok", step) for step in range(1, len(parts))]


def place_rows(choice, parts):
    return gather_rows(choice, jnp.concatenate(parts, axis=0))


def on_device(
    block_input,
    crop_ids,
    ln1_gain,
    ln1_bias,
    w_qkv,
    q_bias,
    v_bias,
    w_out,
    out_bias,
    ln2_gain,
    ln2_bias,
    w_fc1,
    fc1_bias,
    w_fc2,
    fc2_bias,
    out_grad,
):
    packs, local_rows, features = block_input.shape
    rows = packs * local_rows
    shards = lax.axis_size("batch")
    paired = shards == SLABS
    send, receive, send_turned, receive_turned, overflow = exchange_plan(crop_ids)
    arrived = swap_groups(spread_parts(send_turned, block_input.reshape(rows, features)))
    held_back = spread_parts(send_turned, out_grad.reshape(rows, features))
    held_back = hold_until(held_back, arrived[1:])
    vectors = [out_bias, ln2_gain, ln2_bias, fc2_bias, ln1_gain, ln1_bias]
    vectors = jnp.stack(vectors + [jnp.zeros_like(out_bias)] * 2)
    bias = jnp.concatenate([q_bias, jnp.zeros_like(q_bias), v_bias])[None]
    low_input, normed_one, joined = project(arrived, receive, vectors, w_qkv, bias)
    grad_parts = swap_groups(held_back)
    attended = image_attention(joined, [])
    *parts, n2t, hat, rstd, hidden, slope = feed_forward(
        low_input, attended, w_out, vectors, w_fc1, fc1_bias[None], w_fc2, receive_turned
    )
    low_grad = place_rows(receive, grad_parts)
    order = slab_order()

    def back(part, after):
        return list(
            feed_back(order, part, 2, low_grad, n2t, w_fc1, w_fc2, hidden, slope, after)
        )

    backs = [back(0, parts[1:])]
    parts = swap_groups(parts)
    backs.append(back(1, [backs[0][1], backs[0][3], parts[2]]))
    size = features // SLABS
    sums = []
    far = hold_until([backs[1][2], backs[1][4]], parts[1:])
    backs[1][2], backs[1][4] = far
    if paired:
        for dn2, keep1, send1, keep2, send2, _ in backs:
            turned = [one.reshape(SLABS, SLABS // 2, size, -1) for one in (keep2, send2)]
            sums.append(Sums((0, 1), keep1, send1, *turned))
    wait = sums[0].move() if paired else []
    grad_branch, grad_attended, sums_two = second_norm_back(
        backs[0][0], backs[1][0], low_grad, hat, rstd, vectors, w_out, wait
    )
    wait = sums[1].move() if paired else []
    grad_joined = image_attention_back(joined, grad_attended, 0, 2, None, wait)
    if paired:
        sums[1].hold([grad_joined])
        wait = sums[0].move()
    grad_joined = image_attention_back(joined, grad_attended, 1, 2, grad_joined, wait)
    if paired:
        left = token_sum(*sums[0].move())
        wait = [left.send]
    *input_parts, sums_one, joined_sums = first_norm_back(
        grad_joined, w_qkv, low_input, grad_branch, vectors, receive_turned, wait
    )
    if paired:
        wait = [left.one()] + sums[1].move() + input_parts[1:]

    short = [
        sums_one[0],
        sums_one[1],
        joined_sums[0, :features],
        joined_sums[0, 2 * features :],
        sums_two[0],
        sums_two[1],
        sums_two[2],
        sums_two[3],
        jnp.stack([each[5].reshape(SLABS, -1) for each in backs], axis=1).reshape(-1),
        jnp.broadcast_to(overflow.astype(jnp.float32), (SLABS * features // 2,)),
    ]
    short_slabs = jnp.concatenate([each.reshape(SLABS, -1) for each in short], axis=1)
    short_slabs = short_slabs.reshape(SLABS, -1, 4 * size)
    short_slabs = jnp.pad(short_slabs, ((0, 0), (0, 64 - short_slabs.shape[1]), (0, 0)))
    products = attention_products(
        order, normed_one, attended, grad_joined, grad_branch, short_slabs, wait
    )
    input_parts = swap_groups(input_parts)
    output = place_rows(send, parts)
    input_grad = place_rows(send, input_parts)

    if paired:
        right = token_sum(*sums[1].move())
        three = Sums((0, 0), *products)
        three.hold([left.two(), right.send])
        three.move()
        left.three(three.send)
        right.one(three.send)
        first = left.four()
        three.move()
        three.hold([first[0], right.two(), *input_parts[1:]])
        right.three(three.send)
        top, bottom = three.move()
        last = token_sum(top, jnp.pad(bottom, ((0, top.shape[0] - bottom.shape[0]), (0, 0))))
        last.hold([right.send])
        second = right.four([last.send])
        last.one()
        last.two()
        last.three()
        third = last.four()
        fc1 = jnp.concatenate([first[0], second[0]], axis=1)
        fc2 = [one[1].reshape(SLABS, size, -1) for one in (first, second)]
        grad_fc1 = fc1
        grad_fc2 = jnp.stack(fc2, axis=1).transpose(0, 1, 3, 2).reshape(-1, size)
        halves = [one[: features // 2] for one in third]
        grad_attention = jnp.concatenate(halves, axis=0)
        grad_qkv, grad_out = grad_attention[:, : 3 * size], grad_attention[:, 3 * size :]
        tail = third[0][features // 2 :].reshape(-1).astype(jnp.float32)
        pieces = [tail[i * size : (i + 1) * size] for i in range(8)]
        pieces += [tail[8 * size : 12 * size], tail[12 * size :][:1]]
    else:
        fc1 = jnp.stack([jnp.concatenate(each[1:3]) for each in backs], axis=2)
        grad_fc1 = share_columns(fc1.transpose(1, 0, 2, 3).reshape(features, -1))
        fc2 = jnp.stack([jnp.concatenate(each[3:5], axis=1) for each in backs], axis=2)
        fc2 = fc2.transpose(1, 0, 2, 3).reshape(shards, features // shards, -1)
        grad_fc2 = share_slabs(fc2).T
        both = [jnp.concatenate(products[:2])[:, : features // 2], jnp.concatenate(products[2:])]
        both = jnp.concatenate(both, axis=1)
        grad_qkv = share_columns(both[:, :, : 3 * size].transpose(1, 0, 2).reshape(features, -1))
        grad_out = share_columns(both[:, :, 3 * size :].transpose(1, 0, 2).reshape(features, -1))
        widths = [each.shape[0] // shards for each in short]
        packed = jnp.concatenate([each.reshape(shards, -1) for each in short], axis=1)
        packed = share_slabs(packed.astype(LOW)).astype(jnp.float32)
        pieces, at = [], 0
        for width in widths:
            pieces.append(packed[at : at + width])
            at += width
    fast = (
        output.reshape(block_input.shape),
        input_grad.reshape(block_input.shape),
        pieces[0],
        pieces[1],
        grad_qkv.astype(jnp.float32),
        pieces[2],
        pieces[3],
        grad_out.astype(jnp.float32),
        pieces[4],
        pieces[5],
        pieces[6],
        grad_fc1.astype(jnp.float32),
        pieces[8],
        grad_fc2.astype(jnp.float32),
        pieces[7],
    )

    def unfinished(state):
        return state[0] > 0.5

    def redo(state):
        return (
            jnp.float32(0.0),
            in_place(
                block_input,
                crop_ids,
                ln1_gain,
                ln1_bias,
                w_qkv,
                q_bias,
                v_bias,
                w_out,
                out_bias,
                ln2_gain,
                ln2_bias,
                w_fc1,
                fc1_bias,
                w_fc2,
                fc2_bias,
                out_grad,
            ),
        )

    return lax.while_loop(unfinished, redo, (pieces[9][0], fast))[1]


def solution(mesh):
    in_specs = (
        P("batch", "tok", None),
        P("batch", None),
        P(),
        P(),
        P(),
        P(),
        P(),
        P(),
        P(),
        P(),
        P(),
        P(),
        P(),
        P(),
        P(),
        P("batch", "tok", None),
    )
    out_specs = (
        P("batch", "tok", None),
        P("batch", "tok", None),
        P("batch"),
        P("batch"),
        P(None, "batch"),
        P("batch"),
        P("batch"),
        P(None, "batch"),
        P("batch"),
        P("batch"),
        P("batch"),
        P(None, "batch"),
        P("batch"),
        P(None, "batch"),
        P("batch"),
    )
    return jax.shard_map(
        on_device, mesh=mesh, in_specs=in_specs, out_specs=out_specs, check_vma=False
    )
```

```python
import functools

import jax
import jax.numpy as jnp
from jax import lax
from jax.experimental import pallas as pl
from jax.experimental.pallas import tpu as pltpu
from jax.sharding import PartitionSpec as P

H = 16
HD = 64
IMAGE = 160
LOW = jnp.bfloat16


epsilon = 1e-06
masked_score = -1000000000.0


def layer_norm(values, gain, shift):
    center = values - jnp.mean(values, axis=-1, keepdims=True)
    variance = jnp.mean(center * center, axis=-1, keepdims=True)
    return center * lax.rsqrt(variance + epsilon) * gain + shift


def split_heads(values):
    return values.reshape(values.shape[0], H, HD)


def join_heads(values):
    return values.reshape(values.shape[0], H * HD)


def column_sum(values):
    return jnp.sum(values.astype(jnp.float32), axis=(0, 1))


def project_qkv(inputs, ln1_gain, ln1_bias, w_qkv, q_bias, v_bias):
    normed, norm_back = jax.vjp(layer_norm, inputs, ln1_gain, ln1_bias)
    normed_low = normed.astype(jnp.bfloat16)
    joined = jnp.dot(normed_low, w_qkv, preferred_element_type=jnp.float32)
    features = inputs.shape[-1]
    query_low = (joined[..., :features] + q_bias).astype(jnp.bfloat16)
    key_low = joined[..., features : 2 * features].astype(jnp.bfloat16)
    value_low = (joined[..., 2 * features :] + v_bias).astype(jnp.bfloat16)
    return (normed_low, norm_back, query_low, key_low, value_low)


def pack_scores(query_pack, key_pack, same_pack):
    raw = jnp.einsum(
        "shd,lhd->hsl",
        split_heads(query_pack),
        split_heads(key_pack),
        preferred_element_type=jnp.float32,
    )
    return jnp.where(same_pack[None], raw * HD ** (-0.5), masked_score)


def attend_forward(pieces):
    query_pack, key_pack, value_pack, same_pack = pieces
    scores = pack_scores(query_pack, key_pack, same_pack)
    row_max = jnp.max(scores, axis=-1, keepdims=True)
    expo = jnp.exp(scores - row_max)
    totals = jnp.sum(expo, axis=-1, keepdims=True)
    log_total = row_max + jnp.log(totals)
    prob_low = (expo / totals).astype(jnp.bfloat16)
    mixed = jnp.einsum(
        "hsl,lhd->shd", prob_low, split_heads(value_pack), preferred_element_type=jnp.float32
    )
    return (join_heads(mixed).astype(jnp.bfloat16), log_total)


def attend_backward(pieces):
    query_pack, key_pack, value_pack, same_pack, log_total, grad_pack = pieces
    score_scale = HD ** (-0.5)
    scores_again = pack_scores(query_pack, key_pack, same_pack)
    prob_full = jnp.exp(scores_again - log_total)
    prob_back = prob_full.astype(jnp.bfloat16)
    grad_heads = split_heads(grad_pack)
    grad_prob = jnp.einsum(
        "shd,lhd->hsl", grad_heads, split_heads(value_pack), preferred_element_type=jnp.float32
    )
    spread = jnp.sum(prob_full * grad_prob, axis=-1, keepdims=True)
    grad_scores = (prob_full * (grad_prob - spread)).astype(jnp.bfloat16)
    grad_query = join_heads(
        jnp.einsum(
            "hsl,lhd->shd", grad_scores, split_heads(key_pack), preferred_element_type=jnp.float32
        )
        * score_scale
    ).astype(jnp.bfloat16)
    key_terms = join_heads(
        jnp.einsum(
            "hsl,shd->lhd", grad_scores, split_heads(query_pack), preferred_element_type=jnp.float32
        )
        * score_scale
    )
    value_terms = join_heads(
        jnp.einsum("hsl,shd->lhd", prob_back, grad_heads, preferred_element_type=jnp.float32)
    )
    return (grad_query, key_terms, value_terms)


def swap(values, axis, apart):
    return lax.ppermute(values, axis, [(i, i ^ apart) for i in range(lax.axis_size(axis))])


def gather_tokens(values):
    groups, me = lax.axis_size("tok"), lax.axis_index("tok")
    held = jnp.stack([values] + [swap(values, "tok", step) for step in range(1, groups)])
    return jnp.concatenate(
        [lax.dynamic_index_in_dim(held, me ^ at, 0, False) for at in range(groups)], axis=1
    )


def scatter_tokens(values):
    groups, me = lax.axis_size("tok"), lax.axis_index("tok")
    length = values.shape[1] // groups

    def part(at):
        return lax.dynamic_slice_in_dim(values, at * length, length, 1)

    return part(me) + sum(swap(part(me ^ step), "tok", step) for step in range(1, groups))


def sum_tokens(values):
    groups, me = lax.axis_size("tok"), lax.axis_index("tok")
    held, bits = values, []
    bit = 1
    while bit < groups:
        bits.append(bit)
        pairs = held.reshape((held.shape[0] // 2, 2) + held.shape[1:])
        own = jnp.where(me & bit, 1, 0)
        other = lax.dynamic_index_in_dim(pairs, 1 - own, 1, False).astype(LOW)
        held = lax.dynamic_index_in_dim(pairs, own, 1, False).astype(jnp.float32)
        held = held + swap(other, "tok", bit).astype(jnp.float32)
        bit *= 2
    held = held.astype(LOW)
    for bit in reversed(bits):
        arrived = swap(held, "tok", bit)
        own = (me & bit) > 0
        held = jnp.where(own, jnp.stack([arrived, held], 1), jnp.stack([held, arrived], 1))
        held = held.reshape((-1,) + held.shape[2:])
    return held


def share_slabs(slabs):
    me, held = lax.axis_index("batch"), slabs
    bit = 1
    while bit < lax.axis_size("batch"):
        pairs = held.reshape((held.shape[0] // 2, 2) + held.shape[1:])
        own = jnp.where(me & bit, 1, 0)
        other = lax.dynamic_index_in_dim(pairs, 1 - own, 1, False).astype(LOW)
        held = lax.dynamic_index_in_dim(pairs, own, 1, False).astype(jnp.float32)
        held = held + swap(other, "batch", bit).astype(jnp.float32)
        bit *= 2
    flat = held[0].reshape(-1)
    groups = lax.axis_size("tok")
    padded = jnp.pad(flat, (0, -flat.size % groups)).astype(LOW).reshape(groups, -1)
    return sum_tokens(padded).reshape(-1)[: flat.size].reshape(slabs.shape[1:])


def share_columns(grad):
    shards = lax.axis_size("batch")
    if grad.ndim == 1:
        return share_slabs(grad.astype(LOW).reshape(shards, -1)).astype(jnp.float32)
    slabs = grad.astype(LOW).reshape(grad.shape[0], shards, -1).transpose(1, 0, 2)
    return share_slabs(slabs).astype(jnp.float32)


def in_place(
    block_input,
    crop_ids,
    ln1_gain,
    ln1_bias,
    w_qkv,
    q_bias,
    v_bias,
    w_out,
    out_bias,
    ln2_gain,
    ln2_bias,
    w_fc1,
    fc1_bias,
    w_fc2,
    fc2_bias,
    out_grad,
):
    packs, local_rows, features = block_input.shape
    offset = lax.axis_index("tok") * local_rows
    own_crop = lax.dynamic_slice_in_dim(crop_ids, offset, local_rows, 1)
    same_crop = own_crop[:, :, None] == crop_ids[:, None, :]
    inputs = block_input.astype(jnp.float32)
    normed_one, norm_one_back, query_low, key_low, value_low = project_qkv(
        inputs, ln1_gain, ln1_bias, w_qkv, q_bias, v_bias
    )
    key_all, value_all = (
        gather_tokens(key_low),
        gather_tokens(value_low),
    )
    attended, log_total = lax.map(attend_forward, (query_low, key_all, value_all, same_crop))
    resid = inputs + jnp.dot(attended, w_out, preferred_element_type=jnp.float32) + out_bias
    normed_two, norm_two_back = jax.vjp(layer_norm, resid, ln2_gain, ln2_bias)
    normed_two_low = normed_two.astype(jnp.bfloat16)
    pre_act = jnp.dot(normed_two_low, w_fc1, preferred_element_type=jnp.float32) + fc1_bias

    def gelu_exact(values):
        return jax.nn.gelu(values, approximate=False)

    activated, gelu_back = jax.vjp(gelu_exact, pre_act)
    hidden = activated.astype(jnp.bfloat16)
    output = resid + jnp.dot(hidden, w_fc2, preferred_element_type=jnp.float32) + fc2_bias
    out_grad_full = out_grad.astype(jnp.float32)
    grad_fc2 = jnp.einsum("bsf,bsd->fd", hidden, out_grad, preferred_element_type=jnp.float32)
    grad_fc2_bias = column_sum(out_grad)
    grad_hidden = jnp.einsum("bsd,fd->bsf", out_grad, w_fc2, preferred_element_type=jnp.float32)
    grad_pre = gelu_back(grad_hidden)[0].astype(jnp.bfloat16)
    grad_fc1 = jnp.einsum(
        "bsd,bsf->df", normed_two_low, grad_pre, preferred_element_type=jnp.float32
    )
    grad_fc1_bias = column_sum(grad_pre)
    grad_normed_two = jnp.einsum("bsf,df->bsd", grad_pre, w_fc1, preferred_element_type=jnp.float32)
    resid_term, grad_ln2_gain, grad_ln2_bias = norm_two_back(grad_normed_two)
    grad_resid = out_grad_full + resid_term
    grad_branch = grad_resid.astype(jnp.bfloat16)
    grad_out = jnp.einsum("bsd,bse->de", attended, grad_branch, preferred_element_type=jnp.float32)
    grad_out_bias = column_sum(grad_branch)
    grad_attended = jnp.einsum(
        "bse,de->bsd", grad_branch, w_out, preferred_element_type=jnp.float32
    ).astype(jnp.bfloat16)
    normed_one, norm_one_back, query_low, key_low, value_low = project_qkv(
        inputs, ln1_gain, ln1_bias, w_qkv, q_bias, v_bias
    )
    key_all, value_all = (
        gather_tokens(key_low),
        gather_tokens(value_low),
    )
    grad_query, key_terms, value_terms = lax.map(
        attend_backward, (query_low, key_all, value_all, same_crop, log_total, grad_attended)
    )
    grad_key_sum, grad_value_sum = (
        scatter_tokens(key_terms),
        scatter_tokens(value_terms),
    )
    grad_key = grad_key_sum.astype(jnp.bfloat16)
    grad_value = grad_value_sum.astype(jnp.bfloat16)
    grad_joined = jnp.concatenate([grad_query, grad_key, grad_value], axis=-1)
    grad_qkv = jnp.einsum(
        "bsd,bse->de", normed_one, grad_joined, preferred_element_type=jnp.float32
    )
    grad_q_bias = column_sum(grad_query)
    grad_v_bias = column_sum(grad_value)
    grad_normed_one = jnp.einsum(
        "bse,de->bsd", grad_joined, w_qkv, preferred_element_type=jnp.float32
    )
    input_term, grad_ln1_gain, grad_ln1_bias = norm_one_back(grad_normed_one)
    input_grad = (grad_resid + input_term).astype(jnp.bfloat16)
    summed = [
        share_columns(grad)
        for grad in (
            grad_ln1_gain,
            grad_ln1_bias,
            grad_qkv,
            grad_q_bias,
            grad_v_bias,
            grad_out,
            grad_out_bias,
            grad_ln2_gain,
            grad_ln2_bias,
            grad_fc1,
            grad_fc1_bias,
            grad_fc2,
            grad_fc2_bias,
        )
    ]
    return (
        output.astype(jnp.bfloat16),
        input_grad,
        summed[0],
        summed[1],
        summed[2],
        summed[3],
        summed[4],
        summed[5],
        summed[6],
        summed[7],
        summed[8],
        summed[9],
        summed[10],
        summed[11],
        summed[12],
    )


def crop_of_row(axis):
    row = lax.broadcasted_iota(jnp.int32, (IMAGE, IMAGE), axis)
    return jnp.where(row < 50, 0, jnp.where(row < 100, 1, 2 + (row - 100) // 10))


def head_halves(dtype):
    lane = lax.broadcasted_iota(jnp.int32, (1, 2 * HD), 1)
    first = (lane < HD).astype(jnp.float32)
    return first, (first.astype(dtype), (1.0 - first).astype(dtype))


def head_prob(query_half, keys, same_crop):
    raw = lax.dot_general(
        query_half, keys, (((1,), (1,)), ((), ())), preferred_element_type=jnp.float32
    )
    scores = jnp.where(same_crop, raw * HD ** (-0.5), masked_score)
    expo = jnp.exp(scores - jnp.max(scores, axis=-1, keepdims=True))
    return expo / jnp.sum(expo, axis=-1, keepdims=True)


def attend_image(joined_ref, out_ref, rows):
    features = out_ref.shape[1]
    same_crop = crop_of_row(0) == crop_of_row(1)
    first, halves = head_halves(joined_ref.dtype)
    for at in range(0, features, 2 * HD):
        query = joined_ref[rows, at : at + 2 * HD]
        keys = joined_ref[rows, features + at : features + at + 2 * HD]
        values = joined_ref[rows, 2 * features + at : 2 * features + at + 2 * HD]
        mixed = []
        for half in halves:
            prob = head_prob(query * half, keys, same_crop).astype(jnp.bfloat16)
            mixed.append(jnp.dot(prob, values, preferred_element_type=jnp.float32))
        both = mixed[0] * first + mixed[1] * (1.0 - first)
        out_ref[rows, at : at + 2 * HD] = both.astype(out_ref.dtype)


def exchange_plan(crop_ids):
    packs, length = crop_ids.shape
    groups, me = lax.axis_size("tok"), lax.axis_index("tok")
    local = length // groups
    rows = packs * local
    capacity = -(-rows * 13 // (groups * 10) // 16) * 16
    order = crop_ids * length + jnp.arange(length, dtype=jnp.int32)
    rank = jnp.sum((order[:, None, :] < order[:, :, None]).astype(jnp.int32), axis=-1)
    target = rank // local

    def by_source(values):
        return values.reshape(packs, groups, local).transpose(1, 0, 2).reshape(groups, rows)

    target = by_source(target)
    place = by_source(rank % local + local * jnp.arange(packs, dtype=jnp.int32)[:, None])
    number = jnp.arange(rows, dtype=jnp.int32)
    earlier = number[None, :] < number[:, None]
    slot = jnp.sum(
        ((target[:, :, None] == target[:, None, :]) & earlier).astype(jnp.int32), axis=-1
    )
    overflow = jnp.max(slot) >= capacity
    fits = slot < capacity
    own = lax.dynamic_index_in_dim
    send_at = jnp.where(
        own(fits, me, 0, False), (own(target, me, 0, False) ^ me) * capacity + own(slot, me, 0, False), -1
    )
    source = jnp.arange(groups, dtype=jnp.int32)[:, None]
    arrive_at = jnp.where((target == me) & fits, (source ^ me) * capacity + slot + 1, 0)
    hits = (place[None] == number[:, None, None]) & (target == me)[None]
    receive_at = jnp.sum(jnp.where(hits, arrive_at[None], 0), axis=(1, 2)) - 1
    lanes = jnp.arange(groups * capacity, dtype=jnp.int32)
    send, receive = ((at[:, None] == lanes).astype(LOW) for at in (send_at, receive_at))
    send_turned, receive_turned = (
        (lanes[:, None] == at).astype(LOW) for at in (send_at, receive_at)
    )
    return send, receive, send_turned, receive_turned, overflow


def gather_rows(choice, values):
    return jnp.dot(choice, values, preferred_element_type=jnp.float32).astype(jnp.bfloat16)


SLABS = 8
MIB = 1024 * 1024
MICROSECOND = 1000 * 1000 * 1000


def dot(left, right):
    return jnp.dot(left, right, preferred_element_type=jnp.float32)


def dot_back(left, weight):
    return lax.dot_general(
        left, weight, (((1,), (1,)), ((), ())), preferred_element_type=jnp.float32
    )


def gelu_and_slope(z):
    tail = jnp.exp(z * z * -0.5)
    t = 1.0 / (1.0 + (0.3275911 * 0.5**0.5) * jnp.abs(z))
    series = 0.7107068705 + t * (-0.7265760135 + t * 0.5307027145)
    beyond = tail * (t * (0.127414796 + t * (-0.142248368 + t * series)))
    below = jnp.where(z >= 0.0, 1.0 - beyond, beyond)
    return z * below, below + z * tail * 0.3989422804014327


def whole_block(shape):
    return pl.BlockSpec(shape, lambda step, *_: (0,) * len(shape))


def held_block(shape):
    return pl.BlockSpec(
        shape, lambda step, *_: (0,) * len(shape), pipeline_mode=pl.Buffered(1)
    )


UNREAD = pl.BlockSpec(memory_space=pl.ANY)


BIG = 2 * MIB


def place_of(shape, dtype):
    size = dtype.dtype.itemsize
    for extent in shape:
        size *= extent
    return pltpu.HBM(shape, dtype) if size >= BIG else jax.ShapeDtypeStruct(shape, dtype)


def stay(array):
    if array.size * array.dtype.itemsize > BIG:
        return pltpu.with_memory_space_constraint(array, pltpu.HBM)
    return array


def call(
    kernel, name, grid, ins, outs, flops, scratch=(), order=None, after=(), aliases=None, vmem=40
):
    first = 0 if order is None else 1
    given = first + len(ins)

    def body(*refs):
        kernel(*refs[:given], *refs[given + len(after) :])

    return pl.pallas_call(
        body,
        grid_spec=pltpu.PrefetchScalarGridSpec(
            num_scalar_prefetch=first,
            grid=grid,
            in_specs=[spec for _, spec in ins] + [UNREAD] * len(after),
            out_specs=[spec for _, _, spec in outs],
            scratch_shapes=list(scratch),
        ),
        out_shape=[place_of(shape, dtype) for shape, dtype, _ in outs],
        input_output_aliases=aliases or {},
        compiler_params=pltpu.CompilerParams(vmem_limit_bytes=vmem * MIB),
        cost_estimate=pl.CostEstimate(flops=flops, bytes_accessed=0, transcendentals=0),
        name=name,
    )(*([] if order is None else [order]), *[stay(array) for array, _ in ins], *after)


def hold_until(values, after):
    count = len(values)
    held = pl.pallas_call(
        lambda *refs: None,
        in_specs=[UNREAD] * (count + len(after)),
        out_specs=[UNREAD] * count,
        out_shape=[jax.ShapeDtypeStruct(one.shape, one.dtype) for one in values],
        input_output_aliases={i: i for i in range(count)},
        name="hold_until",
    )(*values, *after)
    return list(held)


def front_kernel(
    part0, part1, part2, part3, receive_ref, vec_ref, w_qkv_ref, bias_ref,
    w_out_ref, w1_ref, b1_ref, w2_ref, turn_ref,
    x_ref, normed_ref, joined_ref, att_ref, out0, out1, out2, out3,
    n2t_ref, hat_ref, rstd_ref, hidden_ref, slope_ref,
    parcels, joined_s, n2_s, acc_s, *, projections, images,
):
    step, steps = pl.program_id(0), pl.num_programs(0)
    rows, features = x_ref.shape
    chunk = rows // 4
    size = part0.shape[0]
    block = w_qkv_ref.shape[1]

    @pl.when(step == 0)
    def _():
        for i, ref in enumerate((part0, part1, part2, part3)):
            parcels[i * size : (i + 1) * size, :] = ref[...]

        def part(i, carry):
            at = pl.ds(pl.multiple_of(i * chunk, chunk), chunk)
            x = dot(receive_ref[at, :], parcels[...])
            x_ref[at, :] = x.astype(LOW)
            center = x - jnp.mean(x, axis=-1, keepdims=True)
            rstd = lax.rsqrt(jnp.mean(center * center, axis=-1, keepdims=True) + epsilon)
            normed = center * rstd * vec_ref[4:5, :] + vec_ref[5:6, :]
            normed_ref[at, :] = normed.astype(LOW)
            return carry

        lax.fori_loop(0, rows // chunk, part, 0)

    @pl.when(step < projections)
    def _():
        joined = (dot(normed_ref[...], w_qkv_ref[...]) + bias_ref[...]).astype(LOW)
        joined_ref[...] = joined
        joined_s[:, pl.ds(pl.multiple_of(step * block, block), block)] = joined

    @pl.when((step >= projections) & (step < projections + images))
    def _():
        at = pl.ds(pl.multiple_of((step - projections) * IMAGE, IMAGE), IMAGE)
        attend_image(joined_s, att_ref, at)

    @pl.when(step == projections + images)
    def _():
        def part(i, carry):
            at = pl.ds(pl.multiple_of(i * chunk, chunk), chunk)
            resid = x_ref[at, :].astype(jnp.float32) + dot(att_ref[at, :], w_out_ref[...])
            resid = resid + vec_ref[0:1, :]
            center = resid - jnp.mean(resid, axis=-1, keepdims=True)
            rstd = lax.rsqrt(jnp.mean(center * center, axis=-1, keepdims=True) + epsilon)
            hat = center * rstd
            hat_ref[at, :] = hat.astype(LOW)
            rstd_ref[at, :] = jnp.broadcast_to(rstd, (chunk, rstd_ref.shape[1]))
            acc_s[at, :] = resid + vec_ref[3:4, :]
            n2_s[at, :] = (hat * vec_ref[1:2, :] + vec_ref[2:3, :]).astype(LOW)
            return carry

        lax.fori_loop(0, rows // chunk, part, 0)
        n2t_ref[...] = n2_s[...].T

    @pl.when(step >= projections + images)
    def _():
        act, slope = gelu_and_slope(dot(n2_s[...], w1_ref[...]) + b1_ref[...])
        hidden_ref[...] = act.astype(LOW)
        slope_ref[...] = slope.astype(LOW)
        acc_s[...] += dot(hidden_ref[...], w2_ref[...])

    @pl.when(step == steps - 1)
    def _():
        out = acc_s[...].astype(LOW)
        for i, ref in enumerate((out0, out1, out2, out3)):
            ref[...] = dot(turn_ref[i * size : (i + 1) * size, :], out).astype(LOW)


def parcels_out(turned, features):
    shape = (turned.shape[0] // 4, features)
    return [(shape, LOW, whole_block(shape))] * 4


def front(parts, receive, vectors, w_qkv, bias, w_out, w1, b1, w2, turned):
    rows, features = receive.shape[0], w_qkv.shape[0]
    width = w1.shape[1]
    block = width // SLABS
    projections, images = w_qkv.shape[1] // block, rows // IMAGE

    def early(step):
        return (0, jnp.minimum(step, projections - 1))

    def late(step):
        return (0, jnp.maximum(step - projections - images, 0))

    held = [(part, held_block(part.shape)) for part in parts]
    held += [(receive, held_block(receive.shape)), (vectors, held_block(vectors.shape))]
    tokens = ((rows, features), LOW, whole_block((rows, features)))
    return call(
        functools.partial(front_kernel, projections=projections, images=images),
        "front",
        (projections + images + SLABS,),
        held
        + [
            (w_qkv, pl.BlockSpec((features, block), early)),
            (bias, pl.BlockSpec((1, block), early)),
            (w_out, held_block(w_out.shape)),
            (w1, pl.BlockSpec((features, block), late)),
            (b1, pl.BlockSpec((1, block), late)),
            (w2, pl.BlockSpec((block, features), lambda step: late(step)[::-1])),
            (turned, held_block(turned.shape)),
        ],
        [tokens, tokens, ((rows, w_qkv.shape[1]), LOW, pl.BlockSpec((rows, block), early)), tokens]
        + parcels_out(turned, features)
        + [
            ((features, rows), LOW, whole_block((features, rows))),
            tokens,
            ((rows, 128), jnp.float32, whole_block((rows, 128))),
            ((rows, width), LOW, pl.BlockSpec((rows, block), late)),
            ((rows, width), LOW, pl.BlockSpec((rows, block), late)),
        ],
        flops=44 * MICROSECOND,
        scratch=[
            pltpu.VMEM((4 * parts[0].shape[0], features), LOW),
            pltpu.VMEM((rows, w_qkv.shape[1]), LOW),
            pltpu.VMEM((rows, features), LOW),
            pltpu.VMEM((rows, features), jnp.float32),
        ],
        vmem=56,
    )


def kept(step, order):
    return (jnp.minimum(step, SLABS // 2 - 1), 0, 0)


def sent(step, order):
    return (jnp.maximum(step - SLABS // 2, 0), 0, 0)


def halves_out(extra, rows, width):
    outs = []
    for more in (extra, 0):
        shape = (rows + more, width)
        for place in (kept, sent):
            outs.append(((SLABS // 2,) + shape, LOW, pl.BlockSpec((1,) + shape, place)))
    return outs


def norm_back(grad, gain, hat, rstd):
    scaled = grad * gain
    inner = scaled - jnp.mean(scaled, axis=-1, keepdims=True)
    return (inner - hat * jnp.mean(scaled * hat, axis=-1, keepdims=True)) * rstd


def column_total(values):
    return jnp.sum(values, axis=0, keepdims=True)


def feed_back_kernel(
    order_ref, og_ref, n2t_ref, w1_ref, w2_ref, hidden_ref, slope_ref, *rest, last
):
    if last:
        first_ref, hat_ref, rstd_ref, vec_ref, w_out_ref, *rest = rest
        keep1_ref, send1_ref, keep2_ref, send2_ref, db1_ref, *rest = rest
        branch_ref, att_ref, sums_ref, ogt_s, dn2_ref = rest
    else:
        keep1_ref, send1_ref, keep2_ref, send2_ref, db1_ref, dn2_ref, ogt_s = rest
    step, steps = pl.program_id(0), pl.num_programs(0)
    rows, features = og_ref.shape
    slab, half, chunk = features // SLABS, features // 2, rows // 4

    @pl.when(step == 0)
    def _():
        for p in range(SLABS):
            at = pl.multiple_of(order_ref[1, p] * slab, slab)
            ogt_s[p * slab : (p + 1) * slab, :] = og_ref[:, pl.ds(at, slab)].T
        dn2_ref[...] = first_ref[...] if last else jnp.zeros_like(dn2_ref)

    hidden = hidden_ref[...]
    grad = dot_back(og_ref[...], w2_ref[...]) * slope_ref[...].astype(jnp.float32)
    grad = grad.astype(LOW)
    keep2_ref[0] = dot(ogt_s[:half, :], hidden).astype(LOW)
    send2_ref[0] = dot(ogt_s[half:, :], hidden).astype(LOW)
    db1_ref[...] = column_total(grad.astype(jnp.float32))
    dn2_ref[...] += dot_back(grad, w1_ref[...])
    dw1 = dot(n2t_ref[...], grad).astype(LOW)

    @pl.when(step < steps // 2)
    def _():
        keep1_ref[0] = dw1

    @pl.when(step >= steps // 2)
    def _():
        send1_ref[0] = dw1

    if last:

        @pl.when(step == steps - 1)
        def _():
            sums_ref[...] = jnp.zeros_like(sums_ref)

            def part(i, carry):
                at = pl.ds(pl.multiple_of(i * chunk, chunk), chunk)
                grad, hat = dn2_ref[at, :], hat_ref[at, :].astype(jnp.float32)
                og = og_ref[at, :].astype(jnp.float32)
                resid = og + norm_back(grad, vec_ref[1:2, :], hat, rstd_ref[at, 0:1])
                branch = resid.astype(LOW)
                branch_ref[at, :] = branch
                att_ref[at, :] = dot_back(branch, w_out_ref[...]).astype(LOW)
                sums_ref[0:1, :] += column_total(branch.astype(jnp.float32))
                sums_ref[1:2, :] += column_total(grad * hat)
                sums_ref[2:3, :] += column_total(grad)
                sums_ref[3:4, :] += column_total(og)
                return carry

            lax.fori_loop(0, rows // chunk, part, 0)


def feed_back(order, part, parts, og, n2t, w1, w2, hidden, slope, more, after):
    rows, features = og.shape
    width = w1.shape[1]
    block = width // (SLABS * parts)
    half = SLABS // 2
    last = bool(more)

    def at(step, order):
        return order[0, step] * parts + part

    columns = pl.BlockSpec((rows, block), lambda step, order: (0, at(step, order)))
    turned = pl.BlockSpec(
        (1, features // 2, block), lambda step, order: (order[0, step], 0, 0)
    )
    outs = [
        ((half, features, block), LOW, pl.BlockSpec((1, features, block), kept)),
        ((half, features, block), LOW, pl.BlockSpec((1, features, block), sent)),
        ((SLABS, features // 2, block), LOW, turned),
        ((SLABS, features // 2, block), LOW, turned),
        (
            (1, SLABS * block),
            jnp.float32,
            pl.BlockSpec((1, block), lambda step, order: (0, order[0, step])),
        ),
    ]
    scratch = [pltpu.VMEM((features, rows), LOW)]
    if last:
        outs += [
            (og.shape, LOW, whole_block(og.shape)),
            (og.shape, LOW, whole_block(og.shape)),
            ((8, features), jnp.float32, whole_block((8, features))),
        ]
        scratch.append(pltpu.VMEM(og.shape, jnp.float32))
    else:
        outs.append((og.shape, jnp.float32, whole_block(og.shape)))
    return call(
        functools.partial(feed_back_kernel, last=last),
        "feed_back",
        (SLABS,),
        [
            (og, held_block(og.shape)),
            (n2t, held_block(n2t.shape)),
            (w1, pl.BlockSpec((features, block), lambda step, order: (0, at(step, order)))),
            (w2, pl.BlockSpec((block, features), lambda step, order: (at(step, order), 0))),
            (hidden, columns),
            (slope, columns),
        ]
        + [(each, held_block(each.shape)) for each in more],
        outs,
        flops=18 * MICROSECOND,
        scratch=scratch,
        order=order,
        after=after,
    )


def attend_image_back(joined_ref, grad_ref, out_ref):
    features = grad_ref.shape[1]
    same_crop = crop_of_row(0) == crop_of_row(1)
    first, halves = head_halves(joined_ref.dtype)
    scale = HD ** (-0.5)
    for at in range(0, features, 2 * HD):
        query = joined_ref[:, at : at + 2 * HD]
        keys = joined_ref[:, features + at : features + at + 2 * HD]
        values = joined_ref[:, 2 * features + at : 2 * features + at + 2 * HD]
        grad = grad_ref[:, at : at + 2 * HD]
        terms = []
        for half in halves:
            scores = jnp.where(same_crop, dot_back(keys * half, query) * scale, masked_score)
            expo = jnp.exp(scores - jnp.max(scores, axis=0, keepdims=True))
            prob = expo * (1.0 / jnp.sum(expo, axis=0, keepdims=True))
            grad_prob = dot_back(values * half, grad)
            spread = jnp.sum(prob * grad_prob, axis=0, keepdims=True)
            grad_scores = (prob * (grad_prob - spread)).astype(LOW)
            terms.append(
                (
                    dot(grad_scores.T, keys) * scale,
                    dot(grad_scores, query) * scale,
                    dot(prob.astype(LOW), grad),
                )
            )
        for part in range(3):
            both = terms[0][part] * first + terms[1][part] * (1.0 - first)
            place = part * features + at
            out_ref[:, place : place + 2 * HD] = both.astype(out_ref.dtype)


def image_attention_back(joined, grad, part, parts, earlier, after):
    rows, width = joined.shape
    steps = rows // IMAGE // parts

    def kernel(joined_ref, grad_ref, *rest):
        attend_image_back(joined_ref, grad_ref, rest[-1])

    image = pl.BlockSpec((IMAGE, width), lambda step: (step + part * steps, 0))
    ins = [
        (joined, image),
        (grad, pl.BlockSpec((IMAGE, width // 3), lambda step: (step + part * steps, 0))),
    ]
    if earlier is not None:
        ins.append((earlier, UNREAD))
    return call(
        kernel,
        "attention_back",
        (steps,),
        ins,
        [((rows, width), LOW, image)],
        flops=17 * MICROSECOND,
        after=after,
        aliases=None if earlier is None else {2: 0},
    )[0]


def first_norm_kernel(
    joined_ref, w_ref, x_ref, branch_ref, vec_ref, turn_ref,
    part0, part1, part2, part3, sums_ref, joined_sums_ref, acc_s, out_s,
):
    step, steps = pl.program_id(0), pl.num_programs(0)
    rows = x_ref.shape[0]
    chunk = rows // 4

    @pl.when(step == 0)
    def _():
        acc_s[...] = jnp.zeros_like(acc_s)

    acc_s[...] += dot_back(joined_ref[...], w_ref[...])
    joined_sums_ref[...] = column_total(joined_ref[...].astype(jnp.float32))

    @pl.when(step == steps - 1)
    def _():
        sums_ref[...] = jnp.zeros_like(sums_ref)

        def part(i, carry):
            at = pl.ds(pl.multiple_of(i * chunk, chunk), chunk)
            x = x_ref[at, :].astype(jnp.float32)
            center = x - jnp.mean(x, axis=-1, keepdims=True)
            rstd = lax.rsqrt(jnp.mean(center * center, axis=-1, keepdims=True) + epsilon)
            grad, hat = acc_s[at, :], center * rstd
            term = norm_back(grad, vec_ref[4:5, :], hat, rstd)
            out_s[at, :] = (branch_ref[at, :].astype(jnp.float32) + term).astype(LOW)
            sums_ref[0:1, :] += column_total(grad * hat)
            sums_ref[1:2, :] += column_total(grad)
            return carry

        lax.fori_loop(0, rows // chunk, part, 0)
        size = part0.shape[0]
        for i, ref in enumerate((part0, part1, part2, part3)):
            ref[...] = dot(turn_ref[i * size : (i + 1) * size, :], out_s[...]).astype(LOW)


def first_norm_back(grad_joined, w_qkv, x, branch, vectors, turned, after):
    rows, features = x.shape
    block = features // 2
    return call(
        first_norm_kernel,
        "first_norm_back",
        (w_qkv.shape[1] // block,),
        [
            (grad_joined, pl.BlockSpec((rows, block), lambda step: (0, step))),
            (w_qkv, pl.BlockSpec((features, block), lambda step: (0, step))),
            (x, whole_block(x.shape)),
            (branch, whole_block(x.shape)),
            (vectors, whole_block(vectors.shape)),
            (turned, whole_block(turned.shape)),
        ],
        parcels_out(turned, features)
        + [
            ((8, features), jnp.float32, whole_block((8, features))),
            ((1, w_qkv.shape[1]), jnp.float32, pl.BlockSpec((1, block), lambda step: (0, step))),
        ],
        flops=2 * MICROSECOND,
        scratch=[pltpu.VMEM(x.shape, jnp.float32), pltpu.VMEM(x.shape, LOW)],
        after=after,
    )


def products_kernel(
    order_ref, n1_ref, att_ref, gj_a, gj_b, gb_a, gb_b, short_ref,
    keep_a, send_a, keep_b, send_b, n1t_s, attt_s,
):
    step, steps = pl.program_id(0), pl.num_programs(0)
    half, wide = n1_ref.shape[1] // 2, gj_a.shape[1]

    @pl.when(step == 0)
    def _():
        n1t_s[...] = n1_ref[...].T
        attt_s[...] = att_ref[...].T

    def fill(out_a, out_b):
        out_a[0, :half, :wide] = dot(n1t_s[:half, :], gj_a[...]).astype(LOW)
        out_a[0, :half, wide:] = dot(attt_s[:half, :], gb_a[...]).astype(LOW)
        out_a[0, half:, :] = short_ref[0].astype(LOW)
        out_b[0, :, :wide] = dot(n1t_s[half:, :], gj_b[...]).astype(LOW)
        out_b[0, :, wide:] = dot(attt_s[half:, :], gb_b[...]).astype(LOW)

    @pl.when(step < steps // 2)
    def _():
        fill(keep_a, keep_b)

    @pl.when(step >= steps // 2)
    def _():
        fill(send_a, send_b)


def attention_products(order, normed, attended, joined, branch, short, after):
    rows, features = normed.shape
    wide, narrow = joined.shape[1] // SLABS, branch.shape[1] // SLABS
    return call(
        products_kernel,
        "attention_products",
        (SLABS,),
        [
            (normed, whole_block(normed.shape)),
            (attended, whole_block(attended.shape)),
            (joined, pl.BlockSpec((rows, wide), lambda step, order: (0, order[0, step]))),
            (joined, pl.BlockSpec((rows, wide), lambda step, order: (0, order[1, step]))),
            (branch, pl.BlockSpec((rows, narrow), lambda step, order: (0, order[0, step]))),
            (branch, pl.BlockSpec((rows, narrow), lambda step, order: (0, order[1, step]))),
            (short, pl.BlockSpec((1,) + short.shape[1:], lambda step, order: (order[0, step], 0, 0))),
        ],
        halves_out(short.shape[1], features // 2, wide + narrow),
        flops=15 * MICROSECOND,
        scratch=[pltpu.VMEM((features, rows), LOW), pltpu.VMEM((features, rows), LOW)],
        order=order,
        after=after,
    )


BITS = ((1, 2, 4), (1, 4, 2))


def slab_order():
    place = jnp.arange(SLABS, dtype=jnp.int32)
    if lax.axis_size("batch") != SLABS:
        return jnp.stack([place, place])
    orders = []
    for bits in BITS:
        apart = sum(((place >> (2 - j)) & 1) * bit for j, bit in enumerate(bits))
        orders.append(apart ^ lax.axis_index("batch"))
    return jnp.stack(orders)


class Sums:
    def __init__(self, axes, keep_a, send_a, keep_b, send_b):
        self.axes, self.stage = axes, 0
        self.terms, self.send = ([keep_a], [keep_b]), [send_a, send_b]

    def go(self):
        return [swap(send, "batch", bits[self.stage]) for send, bits in zip(self.send, BITS)]

    def land(self, arrived):
        terms = [own + [other] for own, other in zip(self.terms, arrived)]
        self.stage += 1
        if self.stage == 3:
            return [total(each).reshape(-1, each[0].shape[-1]) for each in terms]
        halves = [
            [jnp.split(one, 2, axis) for one in each] for each, axis in zip(terms, self.axes)
        ]
        self.terms = [[one[0] for one in each] for each in halves]
        self.send = [total([one[1] for one in each]).astype(LOW) for each in halves]
        return self.send


def total(terms):
    return sum(one.astype(jnp.float32) for one in terms)


class TokenSum:
    def __init__(self, values):
        self.low = jnp.where(lax.axis_index("tok") & 1, 1, 0)
        self.high = lax.axis_index("tok") >> 1
        pairs = values.reshape((2, 2) + values.shape[1:])
        self.keep = lax.dynamic_index_in_dim(pairs, self.low, 1, False)
        self.send = [lax.dynamic_index_in_dim(pairs, 1 - self.low, 1, False).astype(LOW)]
        self.stage = 0

    def go(self):
        return [swap(self.send[0], "tok", (1, 2, 2, 1)[self.stage])]

    def land(self, arrived):
        other = arrived[0]
        self.stage += 1
        if self.stage == 1:
            whole = self.keep + other.astype(jnp.float32)
            self.keep = lax.dynamic_index_in_dim(whole, self.high, 0, False)
            self.send = [lax.dynamic_index_in_dim(whole, 1 - self.high, 0, False).astype(LOW)]
        elif self.stage == 2:
            self.send = [(self.keep + other.astype(jnp.float32)).astype(LOW)]
        else:
            own, axis = ((self.high, 0), (self.low, 1))[self.stage - 3]
            mine = self.send[0]
            pair = jnp.stack([mine, other], axis), jnp.stack([other, mine], axis)
            self.send = [jnp.where(own == 0, pair[0], pair[1])]
        if self.stage < 4:
            return self.send
        whole = self.send[0].reshape((4,) + self.send[0].shape[2:])
        return [one.reshape(-1, one.shape[-1]) for one in jnp.split(whole, 2, axis=1)]


def arrive(moves, after):
    flat = hold_until([one for move in moves for one in move], after)
    held, at = [], 0
    for move in moves:
        held.append(flat[at : at + len(move)])
        at += len(move)
    return held


def token_sum(top, bottom):
    parts = [one.reshape(4, -1, one.shape[1]) for one in (top, bottom)]
    return TokenSum(jnp.concatenate(parts, axis=1))


def spread_parts(turned, values):
    parts = [gather_rows(choice, values) for choice in jnp.split(turned, lax.axis_size("tok"))]
    parts[1] = hold_until(parts[1:2], parts[2:])[0]
    return parts


def swap_groups(parts):
    return [parts[0]] + [swap(parts[step], "tok", step) for step in range(1, len(parts))]


def place_rows(choice, parts):
    return gather_rows(choice, jnp.concatenate(parts, axis=0))


def on_device(
    block_input,
    crop_ids,
    ln1_gain,
    ln1_bias,
    w_qkv,
    q_bias,
    v_bias,
    w_out,
    out_bias,
    ln2_gain,
    ln2_bias,
    w_fc1,
    fc1_bias,
    w_fc2,
    fc2_bias,
    out_grad,
):
    packs, local_rows, features = block_input.shape
    rows = packs * local_rows
    shards = lax.axis_size("batch")
    paired = shards == SLABS
    send, receive, send_turned, receive_turned, overflow = exchange_plan(crop_ids)
    arrived = swap_groups(spread_parts(send_turned, block_input.reshape(rows, features)))
    held_back = spread_parts(send_turned, out_grad.reshape(rows, features))
    held_back = hold_until(held_back, arrived[1:])
    vectors = [out_bias, ln2_gain, ln2_bias, fc2_bias, ln1_gain, ln1_bias]
    vectors = jnp.stack(vectors + [jnp.zeros_like(out_bias)] * 2)
    bias = jnp.concatenate([q_bias, jnp.zeros_like(q_bias), v_bias])[None]
    grad_parts = swap_groups(held_back)
    fronts = front(
        arrived, receive, vectors, w_qkv, bias, w_out, w_fc1, fc1_bias[None], w_fc2, receive_turned
    )
    low_input, normed_one, joined, attended, *parts, n2t, hat, rstd, hidden, slope = fronts
    *parts, grad_parts[1], grad_parts[2], grad_parts[3] = hold_until(
        list(parts) + grad_parts[1:], []
    )
    low_grad = place_rows(receive, grad_parts)
    order = slab_order()

    def back(part, more, after):
        return list(
            feed_back(order, part, 2, low_grad, n2t, w_fc1, w_fc2, hidden, slope, more, after)
        )

    size = features // SLABS
    halves = SLABS, SLABS // 2, size, -1

    def slab_sums(back):
        return Sums((0, 1), back[0], back[1], back[2].reshape(halves), back[3].reshape(halves))

    backs = [back(0, [], parts[1:])]
    near = swap(parts[2], "tok", 2)
    backs[0][1], backs[0][3], near = hold_until([backs[0][1], backs[0][3], near], [])
    far = [swap(parts[3], "tok", 3), swap(parts[1], "tok", 1)]
    wait = [backs[0][1]]
    if paired:
        one = slab_sums(backs[0])
        wait = one.land(arrive([one.go()], [])[0])
    backs.append(back(1, [backs[0][5], hat, rstd, vectors, w_out], wait))
    grad_branch, grad_attended, sums_two = backs[1][5:]
    wait = []
    if paired:
        *held, backs[1][1], backs[1][3] = hold_until(
            one.go() + far + [backs[1][1], backs[1][3]], []
        )
        wait, far = one.land(held[:2]), held[2:]
        two = slab_sums(backs[1])
    parts = [parts[0], far[1], near, far[0]]
    grad_joined = image_attention_back(joined, grad_attended, 0, 2, None, wait)
    if paired:
        held = arrive([one.go(), two.go()], [grad_joined])
        left = token_sum(*one.land(held[0]))
        wait = left.send + two.land(held[1])
    grad_joined = image_attention_back(joined, grad_attended, 1, 2, grad_joined, wait)
    if paired:
        moving = two.go()
        wait = left.land(arrive([left.go()], [grad_joined])[0])
    *input_parts, sums_one, joined_sums = first_norm_back(
        grad_joined, w_qkv, low_input, grad_branch, vectors, receive_turned, wait
    )
    wait = []
    if paired:
        *held, sums_one = hold_until(left.go() + moving + input_parts[1:] + [sums_one], [])
        input_parts[1:] = held[3:]
        left.land(held[:1])
        wait = two.land(held[1:3])
    input_parts = swap_groups(input_parts)
    short = [
        sums_one[0],
        sums_one[1],
        joined_sums[0, :features],
        joined_sums[0, 2 * features :],
        sums_two[0],
        sums_two[1],
        sums_two[2],
        sums_two[3],
        jnp.stack([each[4].reshape(SLABS, -1) for each in backs], axis=1).reshape(-1),
        jnp.broadcast_to(overflow.astype(jnp.float32), (SLABS * features // 2,)),
    ]
    short_slabs = jnp.concatenate([each.reshape(SLABS, -1) for each in short], axis=1)
    short_slabs = short_slabs.reshape(SLABS, -1, 4 * size)
    short_slabs = jnp.pad(short_slabs, ((0, 0), (0, 64 - short_slabs.shape[1]), (0, 0)))
    products = attention_products(
        order, normed_one, attended, grad_joined, grad_branch, short_slabs, wait
    )
    output = place_rows(send, parts)

    if paired:
        products = list(products)
        held = hold_until(
            [products[1], products[3]] + two.go() + input_parts[2:3] + left.send, []
        )
        products[1], products[3] = held[:2]
        input_parts[2] = held[4]
        left.send = held[5:]
        three = Sums((0, 0), *products)
        right = token_sum(*two.land(held[2:4]))
        held = arrive([three.go()], right.send)
        three.land(held[0])
        held = arrive([right.go(), left.go()], three.send)
        right.land(held[0])
        left.land(held[1])
        held = arrive([three.go()], right.send + left.send)
        three.land(held[0])
        held = arrive([right.go(), input_parts[3:]], three.send)
        right.land(held[0])
        input_parts[3] = held[1][0]
        held = arrive([three.go()], right.send)
        top, bottom = three.land(held[0])
        last = token_sum(top, jnp.pad(bottom, ((0, top.shape[0] - bottom.shape[0]), (0, 0))))
        held = arrive([left.go(), right.go()], last.send)
        first = left.land(held[0])
        right.land(held[1])
        held = arrive([last.go()], right.send)
        last.land(held[0])
        held = arrive([right.go(), input_parts[1:2]], last.send)
        second = right.land(held[0])
        input_parts[1] = held[1][0]
        for _ in range(3):
            third = last.land(last.go())
        fc1 = jnp.concatenate([first[0], second[0]], axis=1)
        fc2 = [each[1].reshape(SLABS, size, -1) for each in (first, second)]
        grad_fc1 = fc1
        grad_fc2 = jnp.stack(fc2, axis=1).transpose(0, 1, 3, 2).reshape(-1, size)
        halves = [each[: features // 2] for each in third]
        grad_attention = jnp.concatenate(halves, axis=0)
        grad_qkv, grad_out = grad_attention[:, : 3 * size], grad_attention[:, 3 * size :]
        tail = third[0][features // 2 :].reshape(-1).astype(jnp.float32)
        pieces = [tail[i * size : (i + 1) * size] for i in range(8)]
        pieces += [tail[8 * size : 12 * size], tail[12 * size :][:1]]
    else:
        fc1 = jnp.stack([jnp.concatenate(each[:2]) for each in backs], axis=2)
        grad_fc1 = share_columns(fc1.transpose(1, 0, 2, 3).reshape(features, -1))
        fc2 = jnp.stack([jnp.concatenate(each[2:4], axis=1) for each in backs], axis=2)
        fc2 = fc2.transpose(1, 0, 2, 3).reshape(shards, features // shards, -1)
        grad_fc2 = share_slabs(fc2).T
        both = [jnp.concatenate(products[:2])[:, : features // 2], jnp.concatenate(products[2:])]
        both = jnp.concatenate(both, axis=1)
        grad_qkv = share_columns(both[:, :, : 3 * size].transpose(1, 0, 2).reshape(features, -1))
        grad_out = share_columns(both[:, :, 3 * size :].transpose(1, 0, 2).reshape(features, -1))
        widths = [each.shape[0] // shards for each in short]
        packed = jnp.concatenate([each.reshape(shards, -1) for each in short], axis=1)
        packed = share_slabs(packed.astype(LOW)).astype(jnp.float32)
        pieces, at = [], 0
        for width in widths:
            pieces.append(packed[at : at + width])
            at += width
    input_grad = place_rows(send, input_parts)
    fast = (
        output.reshape(block_input.shape),
        input_grad.reshape(block_input.shape),
        pieces[0],
        pieces[1],
        grad_qkv.astype(jnp.float32),
        pieces[2],
        pieces[3],
        grad_out.astype(jnp.float32),
        pieces[4],
        pieces[5],
        pieces[6],
        grad_fc1.astype(jnp.float32),
        pieces[8],
        grad_fc2.astype(jnp.float32),
        pieces[7],
    )

    def unfinished(state):
        return state[0] > 0.5

    def redo(state):
        return (
            jnp.float32(0.0),
            in_place(
                block_input,
                crop_ids,
                ln1_gain,
                ln1_bias,
                w_qkv,
                q_bias,
                v_bias,
                w_out,
                out_bias,
                ln2_gain,
                ln2_bias,
                w_fc1,
                fc1_bias,
                w_fc2,
                fc2_bias,
                out_grad,
            ),
        )

    return lax.while_loop(unfinished, redo, (pieces[9][0], fast))[1]


def solution(mesh):
    in_specs = (
        P("batch", "tok", None),
        P("batch", None),
        P(),
        P(),
        P(),
        P(),
        P(),
        P(),
        P(),
        P(),
        P(),
        P(),
        P(),
        P(),
        P(),
        P("batch", "tok", None),
    )
    out_specs = (
        P("batch", "tok", None),
        P("batch", "tok", None),
        P("batch"),
        P("batch"),
        P(None, "batch"),
        P("batch"),
        P("batch"),
        P(None, "batch"),
        P("batch"),
        P("batch"),
        P("batch"),
        P(None, "batch"),
        P("batch"),
        P(None, "batch"),
        P("batch"),
    )
    return jax.shard_map(
        on_device, mesh=mesh, in_specs=in_specs, out_specs=out_specs, check_vma=False
    )
```

```python
import functools

import jax
import jax.numpy as jnp
from jax import lax
from jax.experimental import pallas as pl
from jax.experimental.pallas import tpu as pltpu
from jax.sharding import PartitionSpec as P

H = 16
HD = 64
IMAGE = 160
LOW = jnp.bfloat16


epsilon = 1e-06
masked_score = -1000000000.0


def layer_norm(values, gain, shift):
    center = values - jnp.mean(values, axis=-1, keepdims=True)
    variance = jnp.mean(center * center, axis=-1, keepdims=True)
    return center * lax.rsqrt(variance + epsilon) * gain + shift


def split_heads(values):
    return values.reshape(values.shape[0], H, HD)


def join_heads(values):
    return values.reshape(values.shape[0], H * HD)


def column_sum(values):
    return jnp.sum(values.astype(jnp.float32), axis=(0, 1))


def project_qkv(inputs, ln1_gain, ln1_bias, w_qkv, q_bias, v_bias):
    normed, norm_back = jax.vjp(layer_norm, inputs, ln1_gain, ln1_bias)
    normed_low = normed.astype(jnp.bfloat16)
    joined = jnp.dot(normed_low, w_qkv, preferred_element_type=jnp.float32)
    features = inputs.shape[-1]
    query_low = (joined[..., :features] + q_bias).astype(jnp.bfloat16)
    key_low = joined[..., features : 2 * features].astype(jnp.bfloat16)
    value_low = (joined[..., 2 * features :] + v_bias).astype(jnp.bfloat16)
    return (normed_low, norm_back, query_low, key_low, value_low)


def pack_scores(query_pack, key_pack, same_pack):
    raw = jnp.einsum(
        "shd,lhd->hsl",
        split_heads(query_pack),
        split_heads(key_pack),
        preferred_element_type=jnp.float32,
    )
    return jnp.where(same_pack[None], raw * HD ** (-0.5), masked_score)


def attend_forward(pieces):
    query_pack, key_pack, value_pack, same_pack = pieces
    scores = pack_scores(query_pack, key_pack, same_pack)
    row_max = jnp.max(scores, axis=-1, keepdims=True)
    expo = jnp.exp(scores - row_max)
    totals = jnp.sum(expo, axis=-1, keepdims=True)
    log_total = row_max + jnp.log(totals)
    prob_low = (expo / totals).astype(jnp.bfloat16)
    mixed = jnp.einsum(
        "hsl,lhd->shd", prob_low, split_heads(value_pack), preferred_element_type=jnp.float32
    )
    return (join_heads(mixed).astype(jnp.bfloat16), log_total)


def attend_backward(pieces):
    query_pack, key_pack, value_pack, same_pack, log_total, grad_pack = pieces
    score_scale = HD ** (-0.5)
    scores_again = pack_scores(query_pack, key_pack, same_pack)
    prob_full = jnp.exp(scores_again - log_total)
    prob_back = prob_full.astype(jnp.bfloat16)
    grad_heads = split_heads(grad_pack)
    grad_prob = jnp.einsum(
        "shd,lhd->hsl", grad_heads, split_heads(value_pack), preferred_element_type=jnp.float32
    )
    spread = jnp.sum(prob_full * grad_prob, axis=-1, keepdims=True)
    grad_scores = (prob_full * (grad_prob - spread)).astype(jnp.bfloat16)
    grad_query = join_heads(
        jnp.einsum(
            "hsl,lhd->shd", grad_scores, split_heads(key_pack), preferred_element_type=jnp.float32
        )
        * score_scale
    ).astype(jnp.bfloat16)
    key_terms = join_heads(
        jnp.einsum(
            "hsl,shd->lhd", grad_scores, split_heads(query_pack), preferred_element_type=jnp.float32
        )
        * score_scale
    )
    value_terms = join_heads(
        jnp.einsum("hsl,shd->lhd", prob_back, grad_heads, preferred_element_type=jnp.float32)
    )
    return (grad_query, key_terms, value_terms)


def swap(values, axis, apart):
    return lax.ppermute(values, axis, [(i, i ^ apart) for i in range(lax.axis_size(axis))])


def gather_tokens(values):
    groups, me = lax.axis_size("tok"), lax.axis_index("tok")
    held = jnp.stack([values] + [swap(values, "tok", step) for step in range(1, groups)])
    return jnp.concatenate(
        [lax.dynamic_index_in_dim(held, me ^ at, 0, False) for at in range(groups)], axis=1
    )


def scatter_tokens(values):
    groups, me = lax.axis_size("tok"), lax.axis_index("tok")
    length = values.shape[1] // groups

    def part(at):
        return lax.dynamic_slice_in_dim(values, at * length, length, 1)

    return part(me) + sum(swap(part(me ^ step), "tok", step) for step in range(1, groups))


def sum_tokens(values):
    groups, me = lax.axis_size("tok"), lax.axis_index("tok")
    held, bits = values, []
    bit = 1
    while bit < groups:
        bits.append(bit)
        pairs = held.reshape((held.shape[0] // 2, 2) + held.shape[1:])
        own = jnp.where(me & bit, 1, 0)
        other = lax.dynamic_index_in_dim(pairs, 1 - own, 1, False).astype(LOW)
        held = lax.dynamic_index_in_dim(pairs, own, 1, False).astype(jnp.float32)
        held = held + swap(other, "tok", bit).astype(jnp.float32)
        bit *= 2
    held = held.astype(LOW)
    for bit in reversed(bits):
        arrived = swap(held, "tok", bit)
        own = (me & bit) > 0
        held = jnp.where(own, jnp.stack([arrived, held], 1), jnp.stack([held, arrived], 1))
        held = held.reshape((-1,) + held.shape[2:])
    return held


def share_slabs(slabs):
    me, held = lax.axis_index("batch"), slabs
    bit = 1
    while bit < lax.axis_size("batch"):
        pairs = held.reshape((held.shape[0] // 2, 2) + held.shape[1:])
        own = jnp.where(me & bit, 1, 0)
        other = lax.dynamic_index_in_dim(pairs, 1 - own, 1, False).astype(LOW)
        held = lax.dynamic_index_in_dim(pairs, own, 1, False).astype(jnp.float32)
        held = held + swap(other, "batch", bit).astype(jnp.float32)
        bit *= 2
    flat = held[0].reshape(-1)
    groups = lax.axis_size("tok")
    padded = jnp.pad(flat, (0, -flat.size % groups)).astype(LOW).reshape(groups, -1)
    return sum_tokens(padded).reshape(-1)[: flat.size].reshape(slabs.shape[1:])


def share_columns(grad):
    shards = lax.axis_size("batch")
    if grad.ndim == 1:
        return share_slabs(grad.astype(LOW).reshape(shards, -1)).astype(jnp.float32)
    slabs = grad.astype(LOW).reshape(grad.shape[0], shards, -1).transpose(1, 0, 2)
    return share_slabs(slabs).astype(jnp.float32)


def in_place(
    block_input,
    crop_ids,
    ln1_gain,
    ln1_bias,
    w_qkv,
    q_bias,
    v_bias,
    w_out,
    out_bias,
    ln2_gain,
    ln2_bias,
    w_fc1,
    fc1_bias,
    w_fc2,
    fc2_bias,
    out_grad,
):
    packs, local_rows, features = block_input.shape
    offset = lax.axis_index("tok") * local_rows
    own_crop = lax.dynamic_slice_in_dim(crop_ids, offset, local_rows, 1)
    same_crop = own_crop[:, :, None] == crop_ids[:, None, :]
    inputs = block_input.astype(jnp.float32)
    normed_one, norm_one_back, query_low, key_low, value_low = project_qkv(
        inputs, ln1_gain, ln1_bias, w_qkv, q_bias, v_bias
    )
    key_all, value_all = (
        gather_tokens(key_low),
        gather_tokens(value_low),
    )
    attended, log_total = lax.map(attend_forward, (query_low, key_all, value_all, same_crop))
    resid = inputs + jnp.dot(attended, w_out, preferred_element_type=jnp.float32) + out_bias
    normed_two, norm_two_back = jax.vjp(layer_norm, resid, ln2_gain, ln2_bias)
    normed_two_low = normed_two.astype(jnp.bfloat16)
    pre_act = jnp.dot(normed_two_low, w_fc1, preferred_element_type=jnp.float32) + fc1_bias

    def gelu_exact(values):
        return jax.nn.gelu(values, approximate=False)

    activated, gelu_back = jax.vjp(gelu_exact, pre_act)
    hidden = activated.astype(jnp.bfloat16)
    output = resid + jnp.dot(hidden, w_fc2, preferred_element_type=jnp.float32) + fc2_bias
    out_grad_full = out_grad.astype(jnp.float32)
    grad_fc2 = jnp.einsum("bsf,bsd->fd", hidden, out_grad, preferred_element_type=jnp.float32)
    grad_fc2_bias = column_sum(out_grad)
    grad_hidden = jnp.einsum("bsd,fd->bsf", out_grad, w_fc2, preferred_element_type=jnp.float32)
    grad_pre = gelu_back(grad_hidden)[0].astype(jnp.bfloat16)
    grad_fc1 = jnp.einsum(
        "bsd,bsf->df", normed_two_low, grad_pre, preferred_element_type=jnp.float32
    )
    grad_fc1_bias = column_sum(grad_pre)
    grad_normed_two = jnp.einsum("bsf,df->bsd", grad_pre, w_fc1, preferred_element_type=jnp.float32)
    resid_term, grad_ln2_gain, grad_ln2_bias = norm_two_back(grad_normed_two)
    grad_resid = out_grad_full + resid_term
    grad_branch = grad_resid.astype(jnp.bfloat16)
    grad_out = jnp.einsum("bsd,bse->de", attended, grad_branch, preferred_element_type=jnp.float32)
    grad_out_bias = column_sum(grad_branch)
    grad_attended = jnp.einsum(
        "bse,de->bsd", grad_branch, w_out, preferred_element_type=jnp.float32
    ).astype(jnp.bfloat16)
    normed_one, norm_one_back, query_low, key_low, value_low = project_qkv(
        inputs, ln1_gain, ln1_bias, w_qkv, q_bias, v_bias
    )
    key_all, value_all = (
        gather_tokens(key_low),
        gather_tokens(value_low),
    )
    grad_query, key_terms, value_terms = lax.map(
        attend_backward, (query_low, key_all, value_all, same_crop, log_total, grad_attended)
    )
    grad_key_sum, grad_value_sum = (
        scatter_tokens(key_terms),
        scatter_tokens(value_terms),
    )
    grad_key = grad_key_sum.astype(jnp.bfloat16)
    grad_value = grad_value_sum.astype(jnp.bfloat16)
    grad_joined = jnp.concatenate([grad_query, grad_key, grad_value], axis=-1)
    grad_qkv = jnp.einsum(
        "bsd,bse->de", normed_one, grad_joined, preferred_element_type=jnp.float32
    )
    grad_q_bias = column_sum(grad_query)
    grad_v_bias = column_sum(grad_value)
    grad_normed_one = jnp.einsum(
        "bse,de->bsd", grad_joined, w_qkv, preferred_element_type=jnp.float32
    )
    input_term, grad_ln1_gain, grad_ln1_bias = norm_one_back(grad_normed_one)
    input_grad = (grad_resid + input_term).astype(jnp.bfloat16)
    summed = [
        share_columns(grad)
        for grad in (
            grad_ln1_gain,
            grad_ln1_bias,
            grad_qkv,
            grad_q_bias,
            grad_v_bias,
            grad_out,
            grad_out_bias,
            grad_ln2_gain,
            grad_ln2_bias,
            grad_fc1,
            grad_fc1_bias,
            grad_fc2,
            grad_fc2_bias,
        )
    ]
    return (
        output.astype(jnp.bfloat16),
        input_grad,
        summed[0],
        summed[1],
        summed[2],
        summed[3],
        summed[4],
        summed[5],
        summed[6],
        summed[7],
        summed[8],
        summed[9],
        summed[10],
        summed[11],
        summed[12],
    )


def crop_of_row(axis):
    row = lax.broadcasted_iota(jnp.int32, (IMAGE, IMAGE), axis)
    return jnp.where(row < 50, 0, jnp.where(row < 100, 1, 2 + (row - 100) // 10))


def head_halves(dtype):
    lane = lax.broadcasted_iota(jnp.int32, (1, 2 * HD), 1)
    first = (lane < HD).astype(jnp.float32)
    return first, (first.astype(dtype), (1.0 - first).astype(dtype))


def head_prob(query_half, keys, same_crop):
    raw = lax.dot_general(
        query_half, keys, (((1,), (1,)), ((), ())), preferred_element_type=jnp.float32
    )
    scores = jnp.where(same_crop, raw * HD ** (-0.5), masked_score)
    expo = jnp.exp(scores - jnp.max(scores, axis=-1, keepdims=True))
    return expo / jnp.sum(expo, axis=-1, keepdims=True)


def attend_image(joined_ref, out_ref, rows):
    features = out_ref.shape[1]
    same_crop = crop_of_row(0) == crop_of_row(1)
    first, halves = head_halves(joined_ref.dtype)
    for at in range(0, features, 2 * HD):
        query = joined_ref[rows, at : at + 2 * HD]
        keys = joined_ref[rows, features + at : features + at + 2 * HD]
        values = joined_ref[rows, 2 * features + at : 2 * features + at + 2 * HD]
        mixed = []
        for half in halves:
            prob = head_prob(query * half, keys, same_crop).astype(jnp.bfloat16)
            mixed.append(jnp.dot(prob, values, preferred_element_type=jnp.float32))
        both = mixed[0] * first + mixed[1] * (1.0 - first)
        out_ref[rows, at : at + 2 * HD] = both.astype(out_ref.dtype)


def exchange_plan(crop_ids):
    packs, length = crop_ids.shape
    groups, me = lax.axis_size("tok"), lax.axis_index("tok")
    local = length // groups
    rows = packs * local
    capacity = -(-rows * 13 // (groups * 10) // 16) * 16
    order = crop_ids * length + jnp.arange(length, dtype=jnp.int32)
    rank = jnp.sum((order[:, None, :] < order[:, :, None]).astype(jnp.int32), axis=-1)
    target = rank // local

    def by_source(values):
        return values.reshape(packs, groups, local).transpose(1, 0, 2).reshape(groups, rows)

    target = by_source(target)
    place = by_source(rank % local + local * jnp.arange(packs, dtype=jnp.int32)[:, None])
    number = jnp.arange(rows, dtype=jnp.int32)
    earlier = number[None, :] < number[:, None]
    slot = jnp.sum(
        ((target[:, :, None] == target[:, None, :]) & earlier).astype(jnp.int32), axis=-1
    )
    overflow = jnp.max(slot) >= capacity
    fits = slot < capacity
    own = lax.dynamic_index_in_dim
    send_at = jnp.where(
        own(fits, me, 0, False), (own(target, me, 0, False) ^ me) * capacity + own(slot, me, 0, False), -1
    )
    source = jnp.arange(groups, dtype=jnp.int32)[:, None]
    arrive_at = jnp.where((target == me) & fits, (source ^ me) * capacity + slot + 1, 0)
    hits = (place[None] == number[:, None, None]) & (target == me)[None]
    receive_at = jnp.sum(jnp.where(hits, arrive_at[None], 0), axis=(1, 2)) - 1
    lanes = jnp.arange(groups * capacity, dtype=jnp.int32)
    send, receive = ((at[:, None] == lanes).astype(LOW) for at in (send_at, receive_at))
    send_turned, receive_turned = (
        (lanes[:, None] == at).astype(LOW) for at in (send_at, receive_at)
    )
    return send, receive, send_turned, receive_turned, overflow


def gather_rows(choice, values):
    return jnp.dot(choice, values, preferred_element_type=jnp.float32).astype(jnp.bfloat16)


SLABS = 8
MIB = 1024 * 1024
MICROSECOND = 1000 * 1000 * 1000


def dot(left, right):
    return jnp.dot(left, right, preferred_element_type=jnp.float32)


def dot_back(left, weight):
    return lax.dot_general(
        left, weight, (((1,), (1,)), ((), ())), preferred_element_type=jnp.float32
    )


def gelu_and_slope(z):
    tail = jnp.exp(z * z * -0.5)
    t = 1.0 / (1.0 + (0.3275911 * 0.5**0.5) * jnp.abs(z))
    series = 0.7107068705 + t * (-0.7265760135 + t * 0.5307027145)
    beyond = tail * (t * (0.127414796 + t * (-0.142248368 + t * series)))
    below = jnp.where(z >= 0.0, 1.0 - beyond, beyond)
    return z * below, below + z * tail * 0.3989422804014327


def whole_block(shape):
    return pl.BlockSpec(shape, lambda step, *_: (0,) * len(shape))


def held_block(shape):
    return pl.BlockSpec(
        shape, lambda step, *_: (0,) * len(shape), pipeline_mode=pl.Buffered(1)
    )


UNREAD = pl.BlockSpec(memory_space=pl.ANY)


BIG = 2 * MIB


def place_of(shape, dtype, far):
    size = dtype.dtype.itemsize
    for extent in shape:
        size *= extent
    return pltpu.HBM(shape, dtype) if far or size >= BIG else jax.ShapeDtypeStruct(shape, dtype)


def stay(array, limit=BIG):
    if array.size * array.dtype.itemsize > limit:
        return pltpu.with_memory_space_constraint(array, pltpu.HBM)
    return array


def call(
    kernel, name, grid, ins, outs, flops, scratch=(), order=None, after=(), aliases=None, vmem=40, far=(),
):
    first = 0 if order is None else 1
    given = first + len(ins)

    def body(*refs):
        kernel(*refs[:given], *refs[given + len(after) :])

    return pl.pallas_call(
        body,
        grid_spec=pltpu.PrefetchScalarGridSpec(
            num_scalar_prefetch=first,
            grid=grid,
            in_specs=[spec for _, spec in ins] + [UNREAD] * len(after),
            out_specs=[spec for _, _, spec in outs],
            scratch_shapes=list(scratch),
        ),
        out_shape=[
            place_of(shape, dtype, i in far) for i, (shape, dtype, _) in enumerate(outs)
        ],
        input_output_aliases=aliases or {},
        compiler_params=pltpu.CompilerParams(vmem_limit_bytes=vmem * MIB),
        cost_estimate=pl.CostEstimate(flops=flops, bytes_accessed=0, transcendentals=0),
        name=name,
    )(*([] if order is None else [order]), *[stay(array) for array, _ in ins], *after)


def hold_until(values, after, wait=0):
    count = len(values)
    held = pl.pallas_call(
        lambda *refs: None,
        in_specs=[UNREAD] * (count + len(after)),
        out_specs=[UNREAD] * count,
        out_shape=[jax.ShapeDtypeStruct(one.shape, one.dtype) for one in values],
        input_output_aliases={i: i for i in range(count)},
        cost_estimate=pl.CostEstimate(
            flops=wait * MICROSECOND, bytes_accessed=0, transcendentals=0
        ),
        name="hold_until",
    )(*values, *after)
    return list(held)


def front_kernel(
    part0, part1, part2, part3, receive_ref, vec_ref, w_qkv_ref, bias_ref,
    w_out_ref, w1_ref, b1_ref, w2_ref, turn_ref,
    x_ref, normed_ref, joined_ref, att_ref, out0, out1, out2, out3,
    n2t_ref, hat_ref, rstd_ref, hidden_ref, slope_ref,
    parcels, joined_s, n2_s, acc_s, *, projections, images,
):
    step, steps = pl.program_id(0), pl.num_programs(0)
    rows, features = x_ref.shape
    chunk = rows // 4
    size = part0.shape[0]
    block = w_qkv_ref.shape[1]

    @pl.when(step == 0)
    def _():
        for i, ref in enumerate((part0, part1, part2, part3)):
            parcels[i * size : (i + 1) * size, :] = ref[...]

        def part(i, carry):
            at = pl.ds(pl.multiple_of(i * chunk, chunk), chunk)
            x = dot(receive_ref[at, :], parcels[...])
            x_ref[at, :] = x.astype(LOW)
            center = x - jnp.mean(x, axis=-1, keepdims=True)
            rstd = lax.rsqrt(jnp.mean(center * center, axis=-1, keepdims=True) + epsilon)
            normed = center * rstd * vec_ref[4:5, :] + vec_ref[5:6, :]
            normed_ref[at, :] = normed.astype(LOW)
            return carry

        lax.fori_loop(0, rows // chunk, part, 0)

    @pl.when(step < projections)
    def _():
        joined = (dot(normed_ref[...], w_qkv_ref[...]) + bias_ref[...]).astype(LOW)
        joined_ref[...] = joined
        joined_s[:, pl.ds(pl.multiple_of(step * block, block), block)] = joined

    @pl.when((step >= projections) & (step < projections + images))
    def _():
        at = pl.ds(pl.multiple_of((step - projections) * IMAGE, IMAGE), IMAGE)
        attend_image(joined_s, att_ref, at)

    @pl.when(step == projections + images)
    def _():
        def part(i, carry):
            at = pl.ds(pl.multiple_of(i * chunk, chunk), chunk)
            resid = x_ref[at, :].astype(jnp.float32) + dot(att_ref[at, :], w_out_ref[...])
            resid = resid + vec_ref[0:1, :]
            center = resid - jnp.mean(resid, axis=-1, keepdims=True)
            rstd = lax.rsqrt(jnp.mean(center * center, axis=-1, keepdims=True) + epsilon)
            hat = center * rstd
            hat_ref[at, :] = hat.astype(LOW)
            rstd_ref[at, :] = jnp.broadcast_to(rstd, (chunk, rstd_ref.shape[1]))
            acc_s[at, :] = resid + vec_ref[3:4, :]
            n2_s[at, :] = (hat * vec_ref[1:2, :] + vec_ref[2:3, :]).astype(LOW)
            return carry

        lax.fori_loop(0, rows // chunk, part, 0)
        n2t_ref[...] = n2_s[...].T

    @pl.when(step >= projections + images)
    def _():
        act, slope = gelu_and_slope(dot(n2_s[...], w1_ref[...]) + b1_ref[...])
        hidden_ref[...] = act.astype(LOW)
        slope_ref[...] = slope.astype(LOW)
        acc_s[...] += dot(hidden_ref[...], w2_ref[...])

    @pl.when(step == steps - 1)
    def _():
        out = acc_s[...].astype(LOW)
        for i, ref in enumerate((out0, out1, out2, out3)):
            ref[...] = dot(turn_ref[i * size : (i + 1) * size, :], out).astype(LOW)


def parcels_out(turned, features):
    shape = (turned.shape[0] // 4, features)
    return [(shape, LOW, whole_block(shape))] * 4


def front(parts, receive, vectors, w_qkv, bias, w_out, w1, b1, w2, turned):
    rows, features = receive.shape[0], w_qkv.shape[0]
    width = w1.shape[1]
    block = width // SLABS
    projections, images = w_qkv.shape[1] // block, rows // IMAGE

    def early(step):
        return (0, jnp.minimum(step, projections - 1))

    def late(step):
        return (0, jnp.maximum(step - projections - images, 0))

    held = [(part, held_block(part.shape)) for part in parts]
    held += [(receive, held_block(receive.shape)), (vectors, held_block(vectors.shape))]
    tokens = ((rows, features), LOW, whole_block((rows, features)))
    return call(
        functools.partial(front_kernel, projections=projections, images=images),
        "front",
        (projections + images + SLABS,),
        held
        + [
            (w_qkv, pl.BlockSpec((features, block), early)),
            (bias, pl.BlockSpec((1, block), early)),
            (w_out, held_block(w_out.shape)),
            (w1, pl.BlockSpec((features, block), late)),
            (b1, pl.BlockSpec((1, block), late)),
            (w2, pl.BlockSpec((block, features), lambda step: late(step)[::-1])),
            (turned, held_block(turned.shape)),
        ],
        [tokens, tokens, ((rows, w_qkv.shape[1]), LOW, pl.BlockSpec((rows, block), early)), tokens]
        + parcels_out(turned, features)
        + [
            ((features, rows), LOW, whole_block((features, rows))),
            tokens,
            ((rows, 128), jnp.float32, whole_block((rows, 128))),
            ((rows, width), LOW, pl.BlockSpec((rows, block), late)),
            ((rows, width), LOW, pl.BlockSpec((rows, block), late)),
        ],
        flops=44 * MICROSECOND,
        scratch=[
            pltpu.VMEM((4 * parts[0].shape[0], features), LOW),
            pltpu.VMEM((rows, w_qkv.shape[1]), LOW),
            pltpu.VMEM((rows, features), LOW),
            pltpu.VMEM((rows, features), jnp.float32),
        ],
        vmem=56,
    )


def kept(step, order):
    return (jnp.minimum(step, SLABS // 2 - 1), 0, 0)


def sent(step, order):
    return (jnp.maximum(step - SLABS // 2, 0), 0, 0)


def halves_out(extra, rows, width):
    outs = []
    for more in (extra, 0):
        shape = (rows + more, width)
        for place in (kept, sent):
            outs.append(((SLABS // 2,) + shape, LOW, pl.BlockSpec((1,) + shape, place)))
    return outs


def norm_back(grad, gain, hat, rstd):
    scaled = grad * gain
    inner = scaled - jnp.mean(scaled, axis=-1, keepdims=True)
    return (inner - hat * jnp.mean(scaled * hat, axis=-1, keepdims=True)) * rstd


def column_total(values):
    return jnp.sum(values, axis=0, keepdims=True)


def feed_back_kernel(
    order_ref, og_ref, n2t_ref, w1_ref, w2_ref, hidden_ref, slope_ref, *rest, last
):
    if last:
        first_ref, hat_ref, rstd_ref, vec_ref, w_out_ref, *rest = rest
        keep1_ref, send1_ref, keep2_ref, send2_ref, db1_ref, *rest = rest
        branch_ref, att_ref, sums_ref, ogt_s, dn2_ref = rest
    else:
        keep1_ref, send1_ref, keep2_ref, send2_ref, db1_ref, dn2_ref, ogt_s = rest
    step, steps = pl.program_id(0), pl.num_programs(0)
    rows, features = og_ref.shape
    slab, half, chunk = features // SLABS, features // 2, rows // 4

    @pl.when(step == 0)
    def _():
        for p in range(SLABS):
            at = pl.multiple_of(order_ref[1, p] * slab, slab)
            ogt_s[p * slab : (p + 1) * slab, :] = og_ref[:, pl.ds(at, slab)].T
        dn2_ref[...] = first_ref[...] if last else jnp.zeros_like(dn2_ref)

    hidden = hidden_ref[...]
    grad = dot_back(og_ref[...], w2_ref[...]) * slope_ref[...].astype(jnp.float32)
    grad = grad.astype(LOW)
    keep2_ref[0] = dot(ogt_s[:half, :], hidden).astype(LOW)
    send2_ref[0] = dot(ogt_s[half:, :], hidden).astype(LOW)
    db1_ref[...] = column_total(grad.astype(jnp.float32))
    dn2_ref[...] += dot_back(grad, w1_ref[...])
    dw1 = dot(n2t_ref[...], grad).astype(LOW)

    @pl.when(step < steps // 2)
    def _():
        keep1_ref[0] = dw1

    @pl.when(step >= steps // 2)
    def _():
        send1_ref[0] = dw1

    if last:

        @pl.when(step == steps - 1)
        def _():
            sums_ref[...] = jnp.zeros_like(sums_ref)

            def part(i, carry):
                at = pl.ds(pl.multiple_of(i * chunk, chunk), chunk)
                grad, hat = dn2_ref[at, :], hat_ref[at, :].astype(jnp.float32)
                og = og_ref[at, :].astype(jnp.float32)
                resid = og + norm_back(grad, vec_ref[1:2, :], hat, rstd_ref[at, 0:1])
                branch = resid.astype(LOW)
                branch_ref[at, :] = branch
                att_ref[at, :] = dot_back(branch, w_out_ref[...]).astype(LOW)
                sums_ref[0:1, :] += column_total(branch.astype(jnp.float32))
                sums_ref[1:2, :] += column_total(grad * hat)
                sums_ref[2:3, :] += column_total(grad)
                sums_ref[3:4, :] += column_total(og)
                return carry

            lax.fori_loop(0, rows // chunk, part, 0)


def feed_back(order, part, parts, og, n2t, w1, w2, hidden, slope, more, after):
    rows, features = og.shape
    width = w1.shape[1]
    block = width // (SLABS * parts)
    half = SLABS // 2
    last = bool(more)

    def at(step, order):
        return order[0, step] * parts + part

    columns = pl.BlockSpec((rows, block), lambda step, order: (0, at(step, order)))
    turned = pl.BlockSpec(
        (1, features // 2, block), lambda step, order: (order[0, step], 0, 0)
    )
    outs = [
        ((half, features, block), LOW, pl.BlockSpec((1, features, block), kept)),
        ((half, features, block), LOW, pl.BlockSpec((1, features, block), sent)),
        ((SLABS, features // 2, block), LOW, turned),
        ((SLABS, features // 2, block), LOW, turned),
        (
            (1, SLABS * block),
            jnp.float32,
            pl.BlockSpec((1, block), lambda step, order: (0, order[0, step])),
        ),
    ]
    scratch = [pltpu.VMEM((features, rows), LOW)]
    if last:
        outs += [
            (og.shape, LOW, whole_block(og.shape)),
            (og.shape, LOW, whole_block(og.shape)),
            ((8, features), jnp.float32, whole_block((8, features))),
        ]
        scratch.append(pltpu.VMEM(og.shape, jnp.float32))
    else:
        outs.append((og.shape, jnp.float32, whole_block(og.shape)))
    return call(
        functools.partial(feed_back_kernel, last=last),
        "feed_back",
        (SLABS,),
        [
            (og, held_block(og.shape)),
            (n2t, held_block(n2t.shape)),
            (w1, pl.BlockSpec((features, block), lambda step, order: (0, at(step, order)))),
            (w2, pl.BlockSpec((block, features), lambda step, order: (at(step, order), 0))),
            (hidden, columns),
            (slope, columns),
        ]
        + [(each, held_block(each.shape)) for each in more],
        outs,
        flops=18 * MICROSECOND,
        scratch=scratch,
        order=order,
        after=after,
    )


def attend_image_back(joined_ref, grad_ref, out_ref):
    features = grad_ref.shape[1]
    same_crop = crop_of_row(0) == crop_of_row(1)
    first, halves = head_halves(joined_ref.dtype)
    scale = HD ** (-0.5)
    for at in range(0, features, 2 * HD):
        query = joined_ref[:, at : at + 2 * HD]
        keys = joined_ref[:, features + at : features + at + 2 * HD]
        values = joined_ref[:, 2 * features + at : 2 * features + at + 2 * HD]
        grad = grad_ref[:, at : at + 2 * HD]
        terms = []
        for half in halves:
            scores = jnp.where(same_crop, dot_back(keys * half, query) * scale, masked_score)
            expo = jnp.exp(scores - jnp.max(scores, axis=0, keepdims=True))
            prob = expo * (1.0 / jnp.sum(expo, axis=0, keepdims=True))
            grad_prob = dot_back(values * half, grad)
            spread = jnp.sum(prob * grad_prob, axis=0, keepdims=True)
            grad_scores = (prob * (grad_prob - spread)).astype(LOW)
            terms.append(
                (
                    dot(grad_scores.T, keys) * scale,
                    dot(grad_scores, query) * scale,
                    dot(prob.astype(LOW), grad),
                )
            )
        for part in range(3):
            both = terms[0][part] * first + terms[1][part] * (1.0 - first)
            place = part * features + at
            out_ref[:, place : place + 2 * HD] = both.astype(out_ref.dtype)


def image_attention_back(joined, grad, part, parts, earlier, after):
    rows, width = joined.shape
    steps = rows // IMAGE // parts

    def kernel(joined_ref, grad_ref, *rest):
        attend_image_back(joined_ref, grad_ref, rest[-1])

    image = pl.BlockSpec((IMAGE, width), lambda step: (step + part * steps, 0))
    ins = [
        (joined, image),
        (grad, pl.BlockSpec((IMAGE, width // 3), lambda step: (step + part * steps, 0))),
    ]
    if earlier is not None:
        ins.append((earlier, UNREAD))
    return call(
        kernel,
        "attention_back",
        (steps,),
        ins,
        [((rows, width), LOW, image)],
        flops=17 * MICROSECOND,
        after=after,
        aliases=None if earlier is None else {2: 0},
    )[0]


def first_norm_kernel(
    joined_ref, w_ref, x_ref, branch_ref, vec_ref, turn_ref,
    part0, part1, part2, part3, sums_ref, joined_sums_ref, acc_s, out_s,
):
    step, steps = pl.program_id(0), pl.num_programs(0)
    rows = x_ref.shape[0]
    chunk = rows // 4

    @pl.when(step == 0)
    def _():
        acc_s[...] = jnp.zeros_like(acc_s)

    acc_s[...] += dot_back(joined_ref[...], w_ref[...])
    joined_sums_ref[...] = column_total(joined_ref[...].astype(jnp.float32))

    @pl.when(step == steps - 1)
    def _():
        sums_ref[...] = jnp.zeros_like(sums_ref)

        def part(i, carry):
            at = pl.ds(pl.multiple_of(i * chunk, chunk), chunk)
            x = x_ref[at, :].astype(jnp.float32)
            center = x - jnp.mean(x, axis=-1, keepdims=True)
            rstd = lax.rsqrt(jnp.mean(center * center, axis=-1, keepdims=True) + epsilon)
            grad, hat = acc_s[at, :], center * rstd
            term = norm_back(grad, vec_ref[4:5, :], hat, rstd)
            out_s[at, :] = (branch_ref[at, :].astype(jnp.float32) + term).astype(LOW)
            sums_ref[0:1, :] += column_total(grad * hat)
            sums_ref[1:2, :] += column_total(grad)
            return carry

        lax.fori_loop(0, rows // chunk, part, 0)
        size = part0.shape[0]
        for i, ref in enumerate((part0, part1, part2, part3)):
            ref[...] = dot(turn_ref[i * size : (i + 1) * size, :], out_s[...]).astype(LOW)


def first_norm_back(grad_joined, w_qkv, x, branch, vectors, turned, after):
    rows, features = x.shape
    block = features // 2
    return call(
        first_norm_kernel,
        "first_norm_back",
        (w_qkv.shape[1] // block,),
        [
            (grad_joined, pl.BlockSpec((rows, block), lambda step: (0, step))),
            (w_qkv, pl.BlockSpec((features, block), lambda step: (0, step))),
            (x, whole_block(x.shape)),
            (branch, whole_block(x.shape)),
            (vectors, whole_block(vectors.shape)),
            (turned, whole_block(turned.shape)),
        ],
        parcels_out(turned, features)
        + [
            ((8, features), jnp.float32, whole_block((8, features))),
            ((1, w_qkv.shape[1]), jnp.float32, pl.BlockSpec((1, block), lambda step: (0, step))),
        ],
        flops=2 * MICROSECOND,
        far=range(5),
        scratch=[pltpu.VMEM(x.shape, jnp.float32), pltpu.VMEM(x.shape, LOW)],
        after=after,
    )


def products_kernel(
    order_ref, n1_ref, att_ref, gj_a, gj_b, gb_a, gb_b, short_ref,
    keep_a, send_a, keep_b, send_b, n1t_s, attt_s,
):
    step, steps = pl.program_id(0), pl.num_programs(0)
    half, wide = n1_ref.shape[1] // 2, gj_a.shape[1]

    @pl.when(step == 0)
    def _():
        n1t_s[...] = n1_ref[...].T
        attt_s[...] = att_ref[...].T

    def fill(out_a, out_b):
        out_a[0, :half, :wide] = dot(n1t_s[:half, :], gj_a[...]).astype(LOW)
        out_a[0, :half, wide:] = dot(attt_s[:half, :], gb_a[...]).astype(LOW)
        out_a[0, half:, :] = short_ref[0].astype(LOW)
        out_b[0, :, :wide] = dot(n1t_s[half:, :], gj_b[...]).astype(LOW)
        out_b[0, :, wide:] = dot(attt_s[half:, :], gb_b[...]).astype(LOW)

    @pl.when(step < steps // 2)
    def _():
        fill(keep_a, keep_b)

    @pl.when(step >= steps // 2)
    def _():
        fill(send_a, send_b)


def attention_products(order, normed, attended, joined, branch, short, after):
    rows, features = normed.shape
    wide, narrow = joined.shape[1] // SLABS, branch.shape[1] // SLABS
    return call(
        products_kernel,
        "attention_products",
        (SLABS,),
        [
            (stay(normed, MIB), whole_block(normed.shape)),
            (stay(attended, MIB), whole_block(attended.shape)),
            (joined, pl.BlockSpec((rows, wide), lambda step, order: (0, order[0, step]))),
            (joined, pl.BlockSpec((rows, wide), lambda step, order: (0, order[1, step]))),
            (branch, pl.BlockSpec((rows, narrow), lambda step, order: (0, order[0, step]))),
            (branch, pl.BlockSpec((rows, narrow), lambda step, order: (0, order[1, step]))),
            (short, pl.BlockSpec((1,) + short.shape[1:], lambda step, order: (order[0, step], 0, 0))),
        ],
        halves_out(short.shape[1], features // 2, wide + narrow),
        flops=15 * MICROSECOND,
        scratch=[pltpu.VMEM((features, rows), LOW), pltpu.VMEM((features, rows), LOW)],
        order=order,
        after=after,
    )


BITS = ((1, 2, 4), (1, 4, 2))


def slab_order():
    place = jnp.arange(SLABS, dtype=jnp.int32)
    if lax.axis_size("batch") != SLABS:
        return jnp.stack([place, place])
    orders = []
    for bits in BITS:
        apart = sum(((place >> (2 - j)) & 1) * bit for j, bit in enumerate(bits))
        orders.append(apart ^ lax.axis_index("batch"))
    return jnp.stack(orders)


class Sums:
    def __init__(self, axes, keep_a, send_a, keep_b, send_b):
        self.axes, self.stage = axes, 0
        self.terms, self.send = ([keep_a], [keep_b]), [send_a, send_b]

    def go(self):
        return [swap(send, "batch", bits[self.stage]) for send, bits in zip(self.send, BITS)]

    def land(self, arrived):
        terms = [own + [other] for own, other in zip(self.terms, arrived)]
        self.stage += 1
        if self.stage == 3:
            return [total(each).reshape(-1, each[0].shape[-1]) for each in terms]
        halves = [
            [jnp.split(one, 2, axis) for one in each] for each, axis in zip(terms, self.axes)
        ]
        self.terms = [[one[0] for one in each] for each in halves]
        self.send = [total([one[1] for one in each]).astype(LOW) for each in halves]
        return self.send


def total(terms):
    return sum(one.astype(jnp.float32) for one in terms)


class TokenSum:
    def __init__(self, values):
        self.low = jnp.where(lax.axis_index("tok") & 1, 1, 0)
        self.high = lax.axis_index("tok") >> 1
        pairs = values.reshape((2, 2) + values.shape[1:])
        self.keep = lax.dynamic_index_in_dim(pairs, self.low, 1, False)
        self.send = [lax.dynamic_index_in_dim(pairs, 1 - self.low, 1, False).astype(LOW)]
        self.stage = 0

    def go(self):
        return [swap(self.send[0], "tok", (1, 2, 2, 1)[self.stage])]

    def land(self, arrived):
        other = arrived[0]
        self.stage += 1
        if self.stage == 1:
            whole = self.keep + other.astype(jnp.float32)
            self.keep = lax.dynamic_index_in_dim(whole, self.high, 0, False)
            self.send = [lax.dynamic_index_in_dim(whole, 1 - self.high, 0, False).astype(LOW)]
        elif self.stage == 2:
            self.send = [(self.keep + other.astype(jnp.float32)).astype(LOW)]
        else:
            own, axis = ((self.high, 0), (self.low, 1))[self.stage - 3]
            mine = self.send[0]
            pair = jnp.stack([mine, other], axis), jnp.stack([other, mine], axis)
            self.send = [jnp.where(own == 0, pair[0], pair[1])]
        if self.stage < 4:
            return self.send
        whole = self.send[0].reshape((4,) + self.send[0].shape[2:])
        return [one.reshape(-1, one.shape[-1]) for one in jnp.split(whole, 2, axis=1)]


def arrive(moves, after, wait=0):
    flat = hold_until([one for move in moves for one in move], after, wait)
    held, at = [], 0
    for move in moves:
        held.append(flat[at : at + len(move)])
        at += len(move)
    return held


class DirectSum:
    def __init__(self, values):
        self.me, self.whole = lax.axis_index("tok"), None

        def quarter(at):
            return lax.dynamic_index_in_dim(values, at, 0, False)

        self.own = quarter(self.me)
        self.send = [quarter(self.me ^ step).astype(LOW) for step in (1, 2, 3)]

    def go(self):
        return [swap(one, "tok", step) for step, one in zip((1, 2, 3), self.send)]

    def land(self, arrived):
        if self.whole is None:
            self.whole = total([self.own] + arrived).astype(LOW)
            self.send = [self.whole] * 3
            return self.send[:1]
        one, two, three = arrived
        rows = [jnp.stack([self.whole, one]), jnp.stack([two, three])]
        rows = [jnp.where(self.me & 1, row[::-1], row) for row in rows]
        upper = self.me >> 1
        rows = jnp.where(upper == 0, rows[0], rows[1]), jnp.where(upper == 0, rows[1], rows[0])
        whole = jnp.concatenate(rows)
        return [each.reshape(-1, each.shape[-1]) for each in jnp.split(whole, 2, axis=1)]


def token_sum(top, bottom, kind=TokenSum):
    parts = [one.reshape(4, -1, one.shape[1]) for one in (top, bottom)]
    return kind(jnp.concatenate(parts, axis=1))


def spread_parts(turned, values):
    parts = [gather_rows(choice, values) for choice in jnp.split(turned, lax.axis_size("tok"))]
    parts[1] = hold_until(parts[1:2], parts[2:])[0]
    return parts


def swap_groups(parts):
    return [parts[0]] + [swap(parts[step], "tok", step) for step in range(1, len(parts))]


def place_rows(choice, parts):
    return gather_rows(choice, jnp.concatenate(parts, axis=0))


def on_device(
    block_input,
    crop_ids,
    ln1_gain,
    ln1_bias,
    w_qkv,
    q_bias,
    v_bias,
    w_out,
    out_bias,
    ln2_gain,
    ln2_bias,
    w_fc1,
    fc1_bias,
    w_fc2,
    fc2_bias,
    out_grad,
):
    packs, local_rows, features = block_input.shape
    rows = packs * local_rows
    shards = lax.axis_size("batch")
    paired = shards == SLABS
    send, receive, send_turned, receive_turned, overflow = exchange_plan(crop_ids)
    arrived = swap_groups(spread_parts(send_turned, block_input.reshape(rows, features)))
    held_back = spread_parts(send_turned, out_grad.reshape(rows, features))
    held_back = hold_until(held_back, arrived[1:])
    vectors = [out_bias, ln2_gain, ln2_bias, fc2_bias, ln1_gain, ln1_bias]
    vectors = jnp.stack(vectors + [jnp.zeros_like(out_bias)] * 2)
    bias = jnp.concatenate([q_bias, jnp.zeros_like(q_bias), v_bias])[None]
    grad_parts = swap_groups(held_back)
    fronts = front(
        arrived, receive, vectors, w_qkv, bias, w_out, w_fc1, fc1_bias[None], w_fc2, receive_turned
    )
    low_input, normed_one, joined, attended, *parts, n2t, hat, rstd, hidden, slope = fronts
    *parts, grad_parts[1], grad_parts[2], grad_parts[3] = hold_until(
        list(parts) + grad_parts[1:], []
    )
    low_grad = place_rows(receive, grad_parts)
    order = slab_order()

    def back(part, more, after):
        return list(
            feed_back(order, part, 2, low_grad, n2t, w_fc1, w_fc2, hidden, slope, more, after)
        )

    size = features // SLABS
    halves = SLABS, SLABS // 2, size, -1

    def slab_sums(back):
        return Sums((0, 1), back[0], back[1], back[2].reshape(halves), back[3].reshape(halves))

    backs = [back(0, [], parts[1:])]
    near = swap(parts[2], "tok", 2)
    backs[0][1], backs[0][3], near = hold_until([backs[0][1], backs[0][3], near], [])
    far = [swap(parts[3], "tok", 3), swap(parts[1], "tok", 1)]
    wait = [backs[0][1]]
    if paired:
        one = slab_sums(backs[0])
        wait = one.land(arrive([one.go()], [], 5)[0])
    backs.append(back(1, [backs[0][5], hat, rstd, vectors, w_out], wait))
    grad_branch, grad_attended, sums_two = backs[1][5:]
    wait = []
    if paired:
        *held, backs[1][1], backs[1][3] = hold_until(
            one.go() + far + [backs[1][1], backs[1][3]], []
        )
        wait, far = one.land(held[:2]), held[2:]
        two = slab_sums(backs[1])
    parts = [parts[0], far[1], near, far[0]]
    grad_joined = image_attention_back(joined, grad_attended, 0, 2, None, wait)
    if paired:
        held = arrive([one.go(), two.go()], [grad_joined])
        left = token_sum(*one.land(held[0]))
        wait = left.send + two.land(held[1])
    grad_joined = image_attention_back(joined, grad_attended, 1, 2, grad_joined, wait)
    if paired:
        moving = two.go()
        wait = left.land(arrive([left.go()], [grad_joined])[0])
    *input_parts, sums_one, joined_sums = first_norm_back(
        grad_joined, w_qkv, low_input, grad_branch, vectors, receive_turned, wait
    )
    wait = []
    if paired:
        *held, sums_one = hold_until(left.go() + moving + input_parts[1:] + [sums_one], [])
        input_parts[1:] = held[3:]
        left.land(held[:1])
        wait = two.land(held[1:3])
    input_parts = swap_groups(input_parts)
    short = [
        sums_one[0],
        sums_one[1],
        joined_sums[0, :features],
        joined_sums[0, 2 * features :],
        sums_two[0],
        sums_two[1],
        sums_two[2],
        sums_two[3],
        jnp.stack([each[4].reshape(SLABS, -1) for each in backs], axis=1).reshape(-1),
        jnp.broadcast_to(overflow.astype(jnp.float32), (SLABS * features // 2,)),
    ]
    short_slabs = jnp.concatenate([each.reshape(SLABS, -1) for each in short], axis=1)
    short_slabs = short_slabs.reshape(SLABS, -1, 4 * size)
    short_slabs = jnp.pad(short_slabs, ((0, 0), (0, 64 - short_slabs.shape[1]), (0, 0)))
    products = attention_products(
        order, normed_one, attended, grad_joined, grad_branch, short_slabs, wait
    )
    output = place_rows(send, parts)

    if paired:
        products = list(products)
        held = hold_until(
            [products[1], products[3]] + two.go() + input_parts[2:3] + left.send, []
        )
        products[1], products[3] = held[:2]
        input_parts[2] = held[4]
        left.send = held[5:]
        three = Sums((0, 0), *products)
        right = token_sum(*two.land(held[2:4]))
        three.land(arrive([three.go()], right.send, 6)[0])
        three.land(arrive([three.go()], three.send + [output], 24)[0])
        held = arrive([right.go(), left.go(), input_parts[1:2]], three.send, 2)
        right.land(held[0])
        left.land(held[1])
        input_parts[1] = held[2][0]
        top, bottom = three.land(arrive([three.go()], right.send + left.send, 14)[0])
        bottom = jnp.pad(bottom, ((0, top.shape[0] - bottom.shape[0]), (0, 0)))
        last = token_sum(top, bottom, DirectSum)
        held = arrive([right.go(), input_parts[3:]], last.send, 2)
        right.land(held[0])
        input_parts[3] = held[1][0]
        held = arrive([right.go(), left.go()], last.send, 12)
        right.land(held[0])
        first = left.land(held[1])
        last.land(arrive([last.go()], right.send, 12)[0])
        second = right.land(arrive([right.go()], last.send[:1], 8)[0])
        input_grad = place_rows(send, input_parts)
        grad_fc1 = jnp.concatenate([first[0], second[0]], axis=1).astype(jnp.float32)
        fc2 = [each[1].reshape(SLABS, size, -1) for each in (first, second)]
        fc2 = jnp.stack(fc2, axis=1).transpose(0, 1, 3, 2).reshape(-1, size)
        grad_fc2 = fc2.astype(jnp.float32)
        third = last.land(arrive([last.go()], [input_grad, grad_fc1, grad_fc2], 8)[0])
        halves = [each[: features // 2] for each in third]
        grad_attention = jnp.concatenate(halves, axis=0)
        grad_qkv, grad_out = grad_attention[:, : 3 * size], grad_attention[:, 3 * size :]
        tail = third[0][features // 2 :].reshape(-1).astype(jnp.float32)
        pieces = [tail[i * size : (i + 1) * size] for i in range(8)]
        pieces += [tail[8 * size : 12 * size], tail[12 * size :][:1]]
    else:
        input_grad = place_rows(send, input_parts)
        fc1 = jnp.stack([jnp.concatenate(each[:2]) for each in backs], axis=2)
        grad_fc1 = share_columns(fc1.transpose(1, 0, 2, 3).reshape(features, -1))
        fc2 = jnp.stack([jnp.concatenate(each[2:4], axis=1) for each in backs], axis=2)
        fc2 = fc2.transpose(1, 0, 2, 3).reshape(shards, features // shards, -1)
        grad_fc2 = share_slabs(fc2).T
        both = [jnp.concatenate(products[:2])[:, : features // 2], jnp.concatenate(products[2:])]
        both = jnp.concatenate(both, axis=1)
        grad_qkv = share_columns(both[:, :, : 3 * size].transpose(1, 0, 2).reshape(features, -1))
        grad_out = share_columns(both[:, :, 3 * size :].transpose(1, 0, 2).reshape(features, -1))
        widths = [each.shape[0] // shards for each in short]
        packed = jnp.concatenate([each.reshape(shards, -1) for each in short], axis=1)
        packed = share_slabs(packed.astype(LOW)).astype(jnp.float32)
        pieces, at = [], 0
        for width in widths:
            pieces.append(packed[at : at + width])
            at += width
    fast = (
        output.reshape(block_input.shape),
        input_grad.reshape(block_input.shape),
        pieces[0],
        pieces[1],
        grad_qkv.astype(jnp.float32),
        pieces[2],
        pieces[3],
        grad_out.astype(jnp.float32),
        pieces[4],
        pieces[5],
        pieces[6],
        grad_fc1.astype(jnp.float32),
        pieces[8],
        grad_fc2.astype(jnp.float32),
        pieces[7],
    )

    def unfinished(state):
        return state[0] > 0.5

    def redo(state):
        return (
            jnp.float32(0.0),
            in_place(
                block_input,
                crop_ids,
                ln1_gain,
                ln1_bias,
                w_qkv,
                q_bias,
                v_bias,
                w_out,
                out_bias,
                ln2_gain,
                ln2_bias,
                w_fc1,
                fc1_bias,
                w_fc2,
                fc2_bias,
                out_grad,
            ),
        )

    return lax.while_loop(unfinished, redo, (pieces[9][0], fast))[1]


def solution(mesh):
    in_specs = (
        P("batch", "tok", None),
        P("batch", None),
        P(),
        P(),
        P(),
        P(),
        P(),
        P(),
        P(),
        P(),
        P(),
        P(),
        P(),
        P(),
        P(),
        P("batch", "tok", None),
    )
    out_specs = (
        P("batch", "tok", None),
        P("batch", "tok", None),
        P("batch"),
        P("batch"),
        P(None, "batch"),
        P("batch"),
        P("batch"),
        P(None, "batch"),
        P("batch"),
        P("batch"),
        P("batch"),
        P(None, "batch"),
        P("batch"),
        P(None, "batch"),
        P("batch"),
    )
    return jax.shard_map(
        on_device, mesh=mesh, in_specs=in_specs, out_specs=out_specs, check_vma=False
    )
```

```python
import functools

import jax
import jax.numpy as jnp
from jax import lax
from jax.experimental import pallas as pl
from jax.experimental.pallas import tpu as pltpu
from jax.sharding import PartitionSpec as P

H = 16
HD = 64
IMAGE = 160
LOW = jnp.bfloat16


epsilon = 1e-06
masked_score = -1000000000.0


def layer_norm(values, gain, shift):
    center = values - jnp.mean(values, axis=-1, keepdims=True)
    variance = jnp.mean(center * center, axis=-1, keepdims=True)
    return center * lax.rsqrt(variance + epsilon) * gain + shift


def split_heads(values):
    return values.reshape(values.shape[0], H, HD)


def join_heads(values):
    return values.reshape(values.shape[0], H * HD)


def column_sum(values):
    return jnp.sum(values.astype(jnp.float32), axis=(0, 1))


def project_qkv(inputs, ln1_gain, ln1_bias, w_qkv, q_bias, v_bias):
    normed, norm_back = jax.vjp(layer_norm, inputs, ln1_gain, ln1_bias)
    normed_low = normed.astype(jnp.bfloat16)
    joined = jnp.dot(normed_low, w_qkv, preferred_element_type=jnp.float32)
    features = inputs.shape[-1]
    query_low = (joined[..., :features] + q_bias).astype(jnp.bfloat16)
    key_low = joined[..., features : 2 * features].astype(jnp.bfloat16)
    value_low = (joined[..., 2 * features :] + v_bias).astype(jnp.bfloat16)
    return (normed_low, norm_back, query_low, key_low, value_low)


def pack_scores(query_pack, key_pack, same_pack):
    raw = jnp.einsum(
        "shd,lhd->hsl",
        split_heads(query_pack),
        split_heads(key_pack),
        preferred_element_type=jnp.float32,
    )
    return jnp.where(same_pack[None], raw * HD ** (-0.5), masked_score)


def attend_forward(pieces):
    query_pack, key_pack, value_pack, same_pack = pieces
    scores = pack_scores(query_pack, key_pack, same_pack)
    row_max = jnp.max(scores, axis=-1, keepdims=True)
    expo = jnp.exp(scores - row_max)
    totals = jnp.sum(expo, axis=-1, keepdims=True)
    log_total = row_max + jnp.log(totals)
    prob_low = (expo / totals).astype(jnp.bfloat16)
    mixed = jnp.einsum(
        "hsl,lhd->shd", prob_low, split_heads(value_pack), preferred_element_type=jnp.float32
    )
    return (join_heads(mixed).astype(jnp.bfloat16), log_total)


def attend_backward(pieces):
    query_pack, key_pack, value_pack, same_pack, log_total, grad_pack = pieces
    score_scale = HD ** (-0.5)
    scores_again = pack_scores(query_pack, key_pack, same_pack)
    prob_full = jnp.exp(scores_again - log_total)
    prob_back = prob_full.astype(jnp.bfloat16)
    grad_heads = split_heads(grad_pack)
    grad_prob = jnp.einsum(
        "shd,lhd->hsl", grad_heads, split_heads(value_pack), preferred_element_type=jnp.float32
    )
    spread = jnp.sum(prob_full * grad_prob, axis=-1, keepdims=True)
    grad_scores = (prob_full * (grad_prob - spread)).astype(jnp.bfloat16)
    grad_query = join_heads(
        jnp.einsum(
            "hsl,lhd->shd", grad_scores, split_heads(key_pack), preferred_element_type=jnp.float32
        )
        * score_scale
    ).astype(jnp.bfloat16)
    key_terms = join_heads(
        jnp.einsum(
            "hsl,shd->lhd", grad_scores, split_heads(query_pack), preferred_element_type=jnp.float32
        )
        * score_scale
    )
    value_terms = join_heads(
        jnp.einsum("hsl,shd->lhd", prob_back, grad_heads, preferred_element_type=jnp.float32)
    )
    return (grad_query, key_terms, value_terms)


def swap(values, axis, apart):
    return lax.ppermute(values, axis, [(i, i ^ apart) for i in range(lax.axis_size(axis))])


def gather_tokens(values):
    groups, me = lax.axis_size("tok"), lax.axis_index("tok")
    held = jnp.stack([values] + [swap(values, "tok", step) for step in range(1, groups)])
    return jnp.concatenate(
        [lax.dynamic_index_in_dim(held, me ^ at, 0, False) for at in range(groups)], axis=1
    )


def scatter_tokens(values):
    groups, me = lax.axis_size("tok"), lax.axis_index("tok")
    length = values.shape[1] // groups

    def part(at):
        return lax.dynamic_slice_in_dim(values, at * length, length, 1)

    return part(me) + sum(swap(part(me ^ step), "tok", step) for step in range(1, groups))


def sum_tokens(values):
    groups, me = lax.axis_size("tok"), lax.axis_index("tok")
    held, bits = values, []
    bit = 1
    while bit < groups:
        bits.append(bit)
        pairs = held.reshape((held.shape[0] // 2, 2) + held.shape[1:])
        own = jnp.where(me & bit, 1, 0)
        other = lax.dynamic_index_in_dim(pairs, 1 - own, 1, False).astype(LOW)
        held = lax.dynamic_index_in_dim(pairs, own, 1, False).astype(jnp.float32)
        held = held + swap(other, "tok", bit).astype(jnp.float32)
        bit *= 2
    held = held.astype(LOW)
    for bit in reversed(bits):
        arrived = swap(held, "tok", bit)
        own = (me & bit) > 0
        held = jnp.where(own, jnp.stack([arrived, held], 1), jnp.stack([held, arrived], 1))
        held = held.reshape((-1,) + held.shape[2:])
    return held


def share_slabs(slabs):
    me, held = lax.axis_index("batch"), slabs
    bit = 1
    while bit < lax.axis_size("batch"):
        pairs = held.reshape((held.shape[0] // 2, 2) + held.shape[1:])
        own = jnp.where(me & bit, 1, 0)
        other = lax.dynamic_index_in_dim(pairs, 1 - own, 1, False).astype(LOW)
        held = lax.dynamic_index_in_dim(pairs, own, 1, False).astype(jnp.float32)
        held = held + swap(other, "batch", bit).astype(jnp.float32)
        bit *= 2
    flat = held[0].reshape(-1)
    groups = lax.axis_size("tok")
    padded = jnp.pad(flat, (0, -flat.size % groups)).astype(LOW).reshape(groups, -1)
    return sum_tokens(padded).reshape(-1)[: flat.size].reshape(slabs.shape[1:])


def share_columns(grad):
    shards = lax.axis_size("batch")
    if grad.ndim == 1:
        return share_slabs(grad.astype(LOW).reshape(shards, -1)).astype(jnp.float32)
    slabs = grad.astype(LOW).reshape(grad.shape[0], shards, -1).transpose(1, 0, 2)
    return share_slabs(slabs).astype(jnp.float32)


def in_place(
    block_input,
    crop_ids,
    ln1_gain,
    ln1_bias,
    w_qkv,
    q_bias,
    v_bias,
    w_out,
    out_bias,
    ln2_gain,
    ln2_bias,
    w_fc1,
    fc1_bias,
    w_fc2,
    fc2_bias,
    out_grad,
):
    packs, local_rows, features = block_input.shape
    offset = lax.axis_index("tok") * local_rows
    own_crop = lax.dynamic_slice_in_dim(crop_ids, offset, local_rows, 1)
    same_crop = own_crop[:, :, None] == crop_ids[:, None, :]
    inputs = block_input.astype(jnp.float32)
    normed_one, norm_one_back, query_low, key_low, value_low = project_qkv(
        inputs, ln1_gain, ln1_bias, w_qkv, q_bias, v_bias
    )
    key_all, value_all = (
        gather_tokens(key_low),
        gather_tokens(value_low),
    )
    attended, log_total = lax.map(attend_forward, (query_low, key_all, value_all, same_crop))
    resid = inputs + jnp.dot(attended, w_out, preferred_element_type=jnp.float32) + out_bias
    normed_two, norm_two_back = jax.vjp(layer_norm, resid, ln2_gain, ln2_bias)
    normed_two_low = normed_two.astype(jnp.bfloat16)
    pre_act = jnp.dot(normed_two_low, w_fc1, preferred_element_type=jnp.float32) + fc1_bias

    def gelu_exact(values):
        return jax.nn.gelu(values, approximate=False)

    activated, gelu_back = jax.vjp(gelu_exact, pre_act)
    hidden = activated.astype(jnp.bfloat16)
    output = resid + jnp.dot(hidden, w_fc2, preferred_element_type=jnp.float32) + fc2_bias
    out_grad_full = out_grad.astype(jnp.float32)
    grad_fc2 = jnp.einsum("bsf,bsd->fd", hidden, out_grad, preferred_element_type=jnp.float32)
    grad_fc2_bias = column_sum(out_grad)
    grad_hidden = jnp.einsum("bsd,fd->bsf", out_grad, w_fc2, preferred_element_type=jnp.float32)
    grad_pre = gelu_back(grad_hidden)[0].astype(jnp.bfloat16)
    grad_fc1 = jnp.einsum(
        "bsd,bsf->df", normed_two_low, grad_pre, preferred_element_type=jnp.float32
    )
    grad_fc1_bias = column_sum(grad_pre)
    grad_normed_two = jnp.einsum("bsf,df->bsd", grad_pre, w_fc1, preferred_element_type=jnp.float32)
    resid_term, grad_ln2_gain, grad_ln2_bias = norm_two_back(grad_normed_two)
    grad_resid = out_grad_full + resid_term
    grad_branch = grad_resid.astype(jnp.bfloat16)
    grad_out = jnp.einsum("bsd,bse->de", attended, grad_branch, preferred_element_type=jnp.float32)
    grad_out_bias = column_sum(grad_branch)
    grad_attended = jnp.einsum(
        "bse,de->bsd", grad_branch, w_out, preferred_element_type=jnp.float32
    ).astype(jnp.bfloat16)
    normed_one, norm_one_back, query_low, key_low, value_low = project_qkv(
        inputs, ln1_gain, ln1_bias, w_qkv, q_bias, v_bias
    )
    key_all, value_all = (
        gather_tokens(key_low),
        gather_tokens(value_low),
    )
    grad_query, key_terms, value_terms = lax.map(
        attend_backward, (query_low, key_all, value_all, same_crop, log_total, grad_attended)
    )
    grad_key_sum, grad_value_sum = (
        scatter_tokens(key_terms),
        scatter_tokens(value_terms),
    )
    grad_key = grad_key_sum.astype(jnp.bfloat16)
    grad_value = grad_value_sum.astype(jnp.bfloat16)
    grad_joined = jnp.concatenate([grad_query, grad_key, grad_value], axis=-1)
    grad_qkv = jnp.einsum(
        "bsd,bse->de", normed_one, grad_joined, preferred_element_type=jnp.float32
    )
    grad_q_bias = column_sum(grad_query)
    grad_v_bias = column_sum(grad_value)
    grad_normed_one = jnp.einsum(
        "bse,de->bsd", grad_joined, w_qkv, preferred_element_type=jnp.float32
    )
    input_term, grad_ln1_gain, grad_ln1_bias = norm_one_back(grad_normed_one)
    input_grad = (grad_resid + input_term).astype(jnp.bfloat16)
    summed = [
        share_columns(grad)
        for grad in (
            grad_ln1_gain,
            grad_ln1_bias,
            grad_qkv,
            grad_q_bias,
            grad_v_bias,
            grad_out,
            grad_out_bias,
            grad_ln2_gain,
            grad_ln2_bias,
            grad_fc1,
            grad_fc1_bias,
            grad_fc2,
            grad_fc2_bias,
        )
    ]
    return (
        output.astype(jnp.bfloat16),
        input_grad,
        summed[0],
        summed[1],
        summed[2],
        summed[3],
        summed[4],
        summed[5],
        summed[6],
        summed[7],
        summed[8],
        summed[9],
        summed[10],
        summed[11],
        summed[12],
    )


def crop_of_row(axis):
    row = lax.broadcasted_iota(jnp.int32, (IMAGE, IMAGE), axis)
    return jnp.where(row < 50, 0, jnp.where(row < 100, 1, 2 + (row - 100) // 10))


def head_halves(dtype):
    lane = lax.broadcasted_iota(jnp.int32, (1, 2 * HD), 1)
    first = (lane < HD).astype(jnp.float32)
    return first, (first.astype(dtype), (1.0 - first).astype(dtype))


def head_prob(query_half, keys, same_crop):
    raw = lax.dot_general(
        query_half, keys, (((1,), (1,)), ((), ())), preferred_element_type=jnp.float32
    )
    scores = jnp.where(same_crop, raw * HD ** (-0.5), masked_score)
    expo = jnp.exp(scores - jnp.max(scores, axis=-1, keepdims=True))
    return expo / jnp.sum(expo, axis=-1, keepdims=True)


def attend_image(joined_ref, out_ref, rows):
    features = out_ref.shape[1]
    same_crop = crop_of_row(0) == crop_of_row(1)
    first, halves = head_halves(joined_ref.dtype)
    for at in range(0, features, 2 * HD):
        query = joined_ref[rows, at : at + 2 * HD]
        keys = joined_ref[rows, features + at : features + at + 2 * HD]
        values = joined_ref[rows, 2 * features + at : 2 * features + at + 2 * HD]
        mixed = []
        for half in halves:
            prob = head_prob(query * half, keys, same_crop).astype(jnp.bfloat16)
            mixed.append(jnp.dot(prob, values, preferred_element_type=jnp.float32))
        both = mixed[0] * first + mixed[1] * (1.0 - first)
        out_ref[rows, at : at + 2 * HD] = both.astype(out_ref.dtype)


def exchange_plan(crop_ids):
    packs, length = crop_ids.shape
    groups, me = lax.axis_size("tok"), lax.axis_index("tok")
    local = length // groups
    rows = packs * local
    capacity = -(-rows * 13 // (groups * 10) // 16) * 16
    order = crop_ids * length + jnp.arange(length, dtype=jnp.int32)
    number = jnp.arange(rows, dtype=jnp.int32)
    earlier = number[None, :] < number[:, None]

    def rank_of(some):
        return jnp.sum((order[:, None, :] < some[:, :, None]).astype(jnp.int32), axis=-1)

    def slot_of(target):
        same = target[..., :, None] == target[..., None, :]
        return jnp.sum((same & earlier).astype(jnp.int32), axis=-1)

    own = rank_of(lax.dynamic_slice_in_dim(order, me * local, local, 1)) // local
    own = own.reshape(rows)
    own_slot = slot_of(own)
    send_at = jnp.where(own_slot < capacity, (own ^ me) * capacity + own_slot, -1)

    def by_source(values):
        return values.reshape(packs, groups, local).transpose(1, 0, 2).reshape(groups, rows)

    rank = rank_of(order)
    target = by_source(rank // local)
    place = by_source(rank % local + local * jnp.arange(packs, dtype=jnp.int32)[:, None])
    slot = slot_of(target)
    overflow = jnp.max(slot) >= capacity
    source = jnp.arange(groups, dtype=jnp.int32)[:, None]
    arrive_at = (target == me) & (slot < capacity)
    arrive_at = jnp.where(arrive_at, (source ^ me) * capacity + slot + 1, 0)
    hits = (place[None] == number[:, None, None]) & (target == me)[None]
    receive_at = jnp.sum(jnp.where(hits, arrive_at[None], 0), axis=(1, 2)) - 1
    lanes = jnp.arange(groups * capacity, dtype=jnp.int32)
    send, receive = ((at[:, None] == lanes).astype(LOW) for at in (send_at, receive_at))
    send_turned, receive_turned = (
        (lanes[:, None] == at).astype(LOW) for at in (send_at, receive_at)
    )
    return send, receive, send_turned, receive_turned, overflow


def gather_rows(choice, values):
    return jnp.dot(choice, values, preferred_element_type=jnp.float32).astype(jnp.bfloat16)


SLABS = 8
MIB = 1024 * 1024
MICROSECOND = 1000 * 1000 * 1000


def dot(left, right):
    return jnp.dot(left, right, preferred_element_type=jnp.float32)


def dot_back(left, weight):
    return lax.dot_general(
        left, weight, (((1,), (1,)), ((), ())), preferred_element_type=jnp.float32
    )


def gelu_and_slope(z):
    tail = jnp.exp(z * z * -0.5)
    t = 1.0 / (1.0 + (0.3275911 * 0.5**0.5) * jnp.abs(z))
    series = 0.7107068705 + t * (-0.7265760135 + t * 0.5307027145)
    beyond = tail * (t * (0.127414796 + t * (-0.142248368 + t * series)))
    below = jnp.where(z >= 0.0, 1.0 - beyond, beyond)
    return z * below, below + z * tail * 0.3989422804014327


def whole_block(shape):
    return pl.BlockSpec(shape, lambda step, *_: (0,) * len(shape))


def held_block(shape):
    return pl.BlockSpec(
        shape, lambda step, *_: (0,) * len(shape), pipeline_mode=pl.Buffered(1)
    )


UNREAD = pl.BlockSpec(memory_space=pl.ANY)


BIG = 2 * MIB


def place_of(shape, dtype, far):
    size = dtype.dtype.itemsize
    for extent in shape:
        size *= extent
    return pltpu.HBM(shape, dtype) if far or size >= BIG else jax.ShapeDtypeStruct(shape, dtype)


def stay(array, limit=BIG):
    if array.size * array.dtype.itemsize > limit:
        return pltpu.with_memory_space_constraint(array, pltpu.HBM)
    return array


def call(
    kernel, name, grid, ins, outs, flops, scratch=(), order=None, after=(), aliases=None, vmem=40, far=(),
):
    first = 0 if order is None else 1
    given = first + len(ins)

    def body(*refs):
        kernel(*refs[:given], *refs[given + len(after) :])

    return pl.pallas_call(
        body,
        grid_spec=pltpu.PrefetchScalarGridSpec(
            num_scalar_prefetch=first,
            grid=grid,
            in_specs=[spec for _, spec in ins] + [UNREAD] * len(after),
            out_specs=[spec for _, _, spec in outs],
            scratch_shapes=list(scratch),
        ),
        out_shape=[
            place_of(shape, dtype, i in far) for i, (shape, dtype, _) in enumerate(outs)
        ],
        input_output_aliases=aliases or {},
        compiler_params=pltpu.CompilerParams(vmem_limit_bytes=vmem * MIB),
        cost_estimate=pl.CostEstimate(flops=flops, bytes_accessed=0, transcendentals=0),
        name=name,
    )(*([] if order is None else [order]), *[stay(array) for array, _ in ins], *after)


def hold_until(values, after, wait=0):
    count = len(values)
    held = pl.pallas_call(
        lambda *refs: None,
        in_specs=[UNREAD] * (count + len(after)),
        out_specs=[UNREAD] * count,
        out_shape=[jax.ShapeDtypeStruct(one.shape, one.dtype) for one in values],
        input_output_aliases={i: i for i in range(count)},
        cost_estimate=pl.CostEstimate(
            flops=wait * MICROSECOND, bytes_accessed=0, transcendentals=0
        ),
        name="hold_until",
    )(*values, *after)
    return list(held)


def front_kernel(
    part0, part1, part2, part3, receive_ref, vec_ref, w_qkv_ref, bias_ref,
    w_out_ref, w1_ref, b1_ref, w2_ref, turn_ref,
    x_ref, normed_ref, joined_ref, att_ref, out0, out1, out2, out3,
    n2t_ref, hat_ref, rstd_ref, hidden_ref, slope_ref,
    parcels, joined_s, n2_s, acc_s, *, projections, images,
):
    step, steps = pl.program_id(0), pl.num_programs(0)
    rows, features = x_ref.shape
    chunk = rows // 4
    size = part0.shape[0]
    block = w_qkv_ref.shape[1]

    @pl.when(step == 0)
    def _():
        for i, ref in enumerate((part0, part1, part2, part3)):
            parcels[i * size : (i + 1) * size, :] = ref[...]

        def part(i, carry):
            at = pl.ds(pl.multiple_of(i * chunk, chunk), chunk)
            x = dot(receive_ref[at, :], parcels[...])
            x_ref[at, :] = x.astype(LOW)
            center = x - jnp.mean(x, axis=-1, keepdims=True)
            rstd = lax.rsqrt(jnp.mean(center * center, axis=-1, keepdims=True) + epsilon)
            normed = center * rstd * vec_ref[4:5, :] + vec_ref[5:6, :]
            normed_ref[at, :] = normed.astype(LOW)
            return carry

        lax.fori_loop(0, rows // chunk, part, 0)

    @pl.when(step < projections)
    def _():
        joined = (dot(normed_ref[...], w_qkv_ref[...]) + bias_ref[...]).astype(LOW)
        joined_ref[...] = joined
        joined_s[:, pl.ds(pl.multiple_of(step * block, block), block)] = joined

    @pl.when((step >= projections) & (step < projections + images))
    def _():
        at = pl.ds(pl.multiple_of((step - projections) * IMAGE, IMAGE), IMAGE)
        attend_image(joined_s, att_ref, at)

    @pl.when(step == projections + images)
    def _():
        def part(i, carry):
            at = pl.ds(pl.multiple_of(i * chunk, chunk), chunk)
            resid = x_ref[at, :].astype(jnp.float32) + dot(att_ref[at, :], w_out_ref[...])
            resid = resid + vec_ref[0:1, :]
            center = resid - jnp.mean(resid, axis=-1, keepdims=True)
            rstd = lax.rsqrt(jnp.mean(center * center, axis=-1, keepdims=True) + epsilon)
            hat = center * rstd
            hat_ref[at, :] = hat.astype(LOW)
            rstd_ref[at, :] = jnp.broadcast_to(rstd, (chunk, rstd_ref.shape[1]))
            acc_s[at, :] = resid + vec_ref[3:4, :]
            n2_s[at, :] = (hat * vec_ref[1:2, :] + vec_ref[2:3, :]).astype(LOW)
            return carry

        lax.fori_loop(0, rows // chunk, part, 0)
        n2t_ref[...] = n2_s[...].T

    @pl.when(step >= projections + images)
    def _():
        act, slope = gelu_and_slope(dot(n2_s[...], w1_ref[...]) + b1_ref[...])
        hidden_ref[...] = act.astype(LOW)
        slope_ref[...] = slope.astype(LOW)
        acc_s[...] += dot(hidden_ref[...], w2_ref[...])

    @pl.when(step == steps - 1)
    def _():
        out = acc_s[...].astype(LOW)
        for i, ref in enumerate((out0, out1, out2, out3)):
            ref[...] = dot(turn_ref[i * size : (i + 1) * size, :], out).astype(LOW)


def parcels_out(turned, features):
    shape = (turned.shape[0] // 4, features)
    return [(shape, LOW, whole_block(shape))] * 4


def front(parts, receive, vectors, w_qkv, bias, w_out, w1, b1, w2, turned):
    rows, features = receive.shape[0], w_qkv.shape[0]
    width = w1.shape[1]
    block = width // SLABS
    projections, images = w_qkv.shape[1] // block, rows // IMAGE

    def early(step):
        return (0, jnp.minimum(step, projections - 1))

    def late(step):
        return (0, jnp.maximum(step - projections - images, 0))

    held = [(part, held_block(part.shape)) for part in parts]
    held += [(receive, held_block(receive.shape)), (vectors, held_block(vectors.shape))]
    tokens = ((rows, features), LOW, whole_block((rows, features)))
    return call(
        functools.partial(front_kernel, projections=projections, images=images),
        "front",
        (projections + images + SLABS,),
        held
        + [
            (w_qkv, pl.BlockSpec((features, block), early)),
            (bias, pl.BlockSpec((1, block), early)),
            (w_out, held_block(w_out.shape)),
            (w1, pl.BlockSpec((features, block), late)),
            (b1, pl.BlockSpec((1, block), late)),
            (w2, pl.BlockSpec((block, features), lambda step: late(step)[::-1])),
            (turned, held_block(turned.shape)),
        ],
        [tokens, tokens, ((rows, w_qkv.shape[1]), LOW, pl.BlockSpec((rows, block), early)), tokens]
        + parcels_out(turned, features)
        + [
            ((features, rows), LOW, whole_block((features, rows))),
            tokens,
            ((rows, 128), jnp.float32, whole_block((rows, 128))),
            ((rows, width), LOW, pl.BlockSpec((rows, block), late)),
            ((rows, width), LOW, pl.BlockSpec((rows, block), late)),
        ],
        flops=44 * MICROSECOND,
        scratch=[
            pltpu.VMEM((4 * parts[0].shape[0], features), LOW),
            pltpu.VMEM((rows, w_qkv.shape[1]), LOW),
            pltpu.VMEM((rows, features), LOW),
            pltpu.VMEM((rows, features), jnp.float32),
        ],
        vmem=56,
    )


def kept(step, order):
    return (jnp.minimum(step, SLABS // 2 - 1), 0, 0)


def sent(step, order):
    return (jnp.maximum(step - SLABS // 2, 0), 0, 0)


def halves_out(extra, rows, width):
    outs = []
    for more in (extra, 0):
        shape = (rows + more, width)
        for place in (kept, sent):
            outs.append(((SLABS // 2,) + shape, LOW, pl.BlockSpec((1,) + shape, place)))
    return outs


def norm_back(grad, gain, hat, rstd):
    scaled = grad * gain
    inner = scaled - jnp.mean(scaled, axis=-1, keepdims=True)
    return (inner - hat * jnp.mean(scaled * hat, axis=-1, keepdims=True)) * rstd


def column_total(values):
    return jnp.sum(values, axis=0, keepdims=True)


def feed_back_kernel(
    order_ref, og_ref, n2t_ref, w1_ref, w2_ref, hidden_ref, slope_ref, *rest, last
):
    if last:
        first_ref, hat_ref, rstd_ref, vec_ref, w_out_ref, *rest = rest
        keep1_ref, send1_ref, keep2_ref, send2_ref, db1_ref, *rest = rest
        branch_ref, att_ref, sums_ref, ogt_s, dn2_ref = rest
    else:
        keep1_ref, send1_ref, keep2_ref, send2_ref, db1_ref, dn2_ref, ogt_s = rest
    step, steps = pl.program_id(0), pl.num_programs(0)
    rows, features = og_ref.shape
    slab, half, chunk = features // SLABS, features // 2, rows // 4

    @pl.when(step == 0)
    def _():
        for p in range(SLABS):
            at = pl.multiple_of(order_ref[1, p] * slab, slab)
            ogt_s[p * slab : (p + 1) * slab, :] = og_ref[:, pl.ds(at, slab)].T
        dn2_ref[...] = first_ref[...] if last else jnp.zeros_like(dn2_ref)

    hidden = hidden_ref[...]
    grad = dot_back(og_ref[...], w2_ref[...]) * slope_ref[...].astype(jnp.float32)
    grad = grad.astype(LOW)
    keep2_ref[0] = dot(ogt_s[:half, :], hidden).astype(LOW)
    send2_ref[0] = dot(ogt_s[half:, :], hidden).astype(LOW)
    db1_ref[...] = column_total(grad.astype(jnp.float32))
    dn2_ref[...] += dot_back(grad, w1_ref[...])
    dw1 = dot(n2t_ref[...], grad).astype(LOW)

    @pl.when(step < steps // 2)
    def _():
        keep1_ref[0] = dw1

    @pl.when(step >= steps // 2)
    def _():
        send1_ref[0] = dw1

    if last:

        @pl.when(step == steps - 1)
        def _():
            sums_ref[...] = jnp.zeros_like(sums_ref)

            def part(i, carry):
                at = pl.ds(pl.multiple_of(i * chunk, chunk), chunk)
                grad, hat = dn2_ref[at, :], hat_ref[at, :].astype(jnp.float32)
                og = og_ref[at, :].astype(jnp.float32)
                resid = og + norm_back(grad, vec_ref[1:2, :], hat, rstd_ref[at, 0:1])
                branch = resid.astype(LOW)
                branch_ref[at, :] = branch
                att_ref[at, :] = dot_back(branch, w_out_ref[...]).astype(LOW)
                sums_ref[0:1, :] += column_total(branch.astype(jnp.float32))
                sums_ref[1:2, :] += column_total(grad * hat)
                sums_ref[2:3, :] += column_total(grad)
                sums_ref[3:4, :] += column_total(og)
                return carry

            lax.fori_loop(0, rows // chunk, part, 0)


def feed_back(order, part, parts, og, n2t, w1, w2, hidden, slope, more, after):
    rows, features = og.shape
    width = w1.shape[1]
    block = width // (SLABS * parts)
    half = SLABS // 2
    last = bool(more)

    def at(step, order):
        return order[0, step] * parts + part

    columns = pl.BlockSpec((rows, block), lambda step, order: (0, at(step, order)))
    turned = pl.BlockSpec(
        (1, features // 2, block), lambda step, order: (order[0, step], 0, 0)
    )
    outs = [
        ((half, features, block), LOW, pl.BlockSpec((1, features, block), kept)),
        ((half, features, block), LOW, pl.BlockSpec((1, features, block), sent)),
        ((SLABS, features // 2, block), LOW, turned),
        ((SLABS, features // 2, block), LOW, turned),
        (
            (1, SLABS * block),
            jnp.float32,
            pl.BlockSpec((1, block), lambda step, order: (0, order[0, step])),
        ),
    ]
    scratch = [pltpu.VMEM((features, rows), LOW)]
    if last:
        outs += [
            (og.shape, LOW, whole_block(og.shape)),
            (og.shape, LOW, whole_block(og.shape)),
            ((8, features), jnp.float32, whole_block((8, features))),
        ]
        scratch.append(pltpu.VMEM(og.shape, jnp.float32))
    else:
        outs.append((og.shape, jnp.float32, whole_block(og.shape)))
    return call(
        functools.partial(feed_back_kernel, last=last),
        "feed_back",
        (SLABS,),
        [
            (og, held_block(og.shape)),
            (n2t, held_block(n2t.shape)),
            (w1, pl.BlockSpec((features, block), lambda step, order: (0, at(step, order)))),
            (w2, pl.BlockSpec((block, features), lambda step, order: (at(step, order), 0))),
            (hidden, columns),
            (slope, columns),
        ]
        + [(each, held_block(each.shape)) for each in more],
        outs,
        flops=18 * MICROSECOND,
        scratch=scratch,
        order=order,
        after=after,
    )


def attend_image_back(joined_ref, grad_ref, out_ref):
    features = grad_ref.shape[1]
    same_crop = crop_of_row(0) == crop_of_row(1)
    first, halves = head_halves(joined_ref.dtype)
    scale = HD ** (-0.5)
    for at in range(0, features, 2 * HD):
        query = joined_ref[:, at : at + 2 * HD]
        keys = joined_ref[:, features + at : features + at + 2 * HD]
        values = joined_ref[:, 2 * features + at : 2 * features + at + 2 * HD]
        grad = grad_ref[:, at : at + 2 * HD]
        terms = []
        for half in halves:
            scores = jnp.where(same_crop, dot_back(keys * half, query) * scale, masked_score)
            expo = jnp.exp(scores - jnp.max(scores, axis=0, keepdims=True))
            prob = expo * (1.0 / jnp.sum(expo, axis=0, keepdims=True))
            grad_prob = dot_back(values * half, grad)
            spread = jnp.sum(prob * grad_prob, axis=0, keepdims=True)
            grad_scores = (prob * (grad_prob - spread)).astype(LOW)
            terms.append(
                (
                    dot(grad_scores.T, keys) * scale,
                    dot(grad_scores, query) * scale,
                    dot(prob.astype(LOW), grad),
                )
            )
        for part in range(3):
            both = terms[0][part] * first + terms[1][part] * (1.0 - first)
            place = part * features + at
            out_ref[:, place : place + 2 * HD] = both.astype(out_ref.dtype)


def image_attention_back(joined, grad, part, parts, earlier, after):
    rows, width = joined.shape
    steps = rows // IMAGE // parts

    def kernel(joined_ref, grad_ref, *rest):
        attend_image_back(joined_ref, grad_ref, rest[-1])

    image = pl.BlockSpec((IMAGE, width), lambda step: (step + part * steps, 0))
    ins = [
        (joined, image),
        (grad, pl.BlockSpec((IMAGE, width // 3), lambda step: (step + part * steps, 0))),
    ]
    if earlier is not None:
        ins.append((earlier, UNREAD))
    return call(
        kernel,
        "attention_back",
        (steps,),
        ins,
        [((rows, width), LOW, image)],
        flops=17 * MICROSECOND,
        after=after,
        aliases=None if earlier is None else {2: 0},
    )[0]


def first_norm_kernel(
    joined_ref, w_ref, x_ref, branch_ref, vec_ref, turn_ref,
    part0, part1, part2, part3, sums_ref, joined_sums_ref, acc_s, out_s,
):
    step, steps = pl.program_id(0), pl.num_programs(0)
    rows = x_ref.shape[0]
    chunk = rows // 4

    @pl.when(step == 0)
    def _():
        acc_s[...] = jnp.zeros_like(acc_s)

    acc_s[...] += dot_back(joined_ref[...], w_ref[...])
    joined_sums_ref[...] = column_total(joined_ref[...].astype(jnp.float32))

    @pl.when(step == steps - 1)
    def _():
        sums_ref[...] = jnp.zeros_like(sums_ref)

        def part(i, carry):
            at = pl.ds(pl.multiple_of(i * chunk, chunk), chunk)
            x = x_ref[at, :].astype(jnp.float32)
            center = x - jnp.mean(x, axis=-1, keepdims=True)
            rstd = lax.rsqrt(jnp.mean(center * center, axis=-1, keepdims=True) + epsilon)
            grad, hat = acc_s[at, :], center * rstd
            term = norm_back(grad, vec_ref[4:5, :], hat, rstd)
            out_s[at, :] = (branch_ref[at, :].astype(jnp.float32) + term).astype(LOW)
            sums_ref[0:1, :] += column_total(grad * hat)
            sums_ref[1:2, :] += column_total(grad)
            return carry

        lax.fori_loop(0, rows // chunk, part, 0)
        size = part0.shape[0]
        for i, ref in enumerate((part0, part1, part2, part3)):
            ref[...] = dot(turn_ref[i * size : (i + 1) * size, :], out_s[...]).astype(LOW)


def first_norm_back(grad_joined, w_qkv, x, branch, vectors, turned, after):
    rows, features = x.shape
    block = features // 2
    return call(
        first_norm_kernel,
        "first_norm_back",
        (w_qkv.shape[1] // block,),
        [
            (grad_joined, pl.BlockSpec((rows, block), lambda step: (0, step))),
            (w_qkv, pl.BlockSpec((features, block), lambda step: (0, step))),
            (x, whole_block(x.shape)),
            (branch, whole_block(x.shape)),
            (vectors, whole_block(vectors.shape)),
            (turned, whole_block(turned.shape)),
        ],
        parcels_out(turned, features)
        + [
            ((8, features), jnp.float32, whole_block((8, features))),
            ((1, w_qkv.shape[1]), jnp.float32, pl.BlockSpec((1, block), lambda step: (0, step))),
        ],
        flops=2 * MICROSECOND,
        far=range(5),
        scratch=[pltpu.VMEM(x.shape, jnp.float32), pltpu.VMEM(x.shape, LOW)],
        after=after,
    )


def products_kernel(
    order_ref, n1_ref, att_ref, gj_a, gj_b, gb_a, gb_b, short_ref,
    keep_a, send_a, keep_b, send_b, n1t_s, attt_s,
):
    step, steps = pl.program_id(0), pl.num_programs(0)
    half, wide = n1_ref.shape[1] // 2, gj_a.shape[1]

    @pl.when(step == 0)
    def _():
        n1t_s[...] = n1_ref[...].T
        attt_s[...] = att_ref[...].T

    def fill(out_a, out_b):
        out_a[0, :half, :wide] = dot(n1t_s[:half, :], gj_a[...]).astype(LOW)
        out_a[0, :half, wide:] = dot(attt_s[:half, :], gb_a[...]).astype(LOW)
        out_a[0, half:, :] = short_ref[0].astype(LOW)
        out_b[0, :, :wide] = dot(n1t_s[half:, :], gj_b[...]).astype(LOW)
        out_b[0, :, wide:] = dot(attt_s[half:, :], gb_b[...]).astype(LOW)

    @pl.when(step < steps // 2)
    def _():
        fill(keep_a, keep_b)

    @pl.when(step >= steps // 2)
    def _():
        fill(send_a, send_b)


def attention_products(order, normed, attended, joined, branch, short, after):
    rows, features = normed.shape
    wide, narrow = joined.shape[1] // SLABS, branch.shape[1] // SLABS
    return call(
        products_kernel,
        "attention_products",
        (SLABS,),
        [
            (stay(normed, MIB), whole_block(normed.shape)),
            (stay(attended, MIB), whole_block(attended.shape)),
            (joined, pl.BlockSpec((rows, wide), lambda step, order: (0, order[0, step]))),
            (joined, pl.BlockSpec((rows, wide), lambda step, order: (0, order[1, step]))),
            (branch, pl.BlockSpec((rows, narrow), lambda step, order: (0, order[0, step]))),
            (branch, pl.BlockSpec((rows, narrow), lambda step, order: (0, order[1, step]))),
            (short, pl.BlockSpec((1,) + short.shape[1:], lambda step, order: (order[0, step], 0, 0))),
        ],
        halves_out(short.shape[1], features // 2, wide + narrow),
        flops=15 * MICROSECOND,
        scratch=[pltpu.VMEM((features, rows), LOW), pltpu.VMEM((features, rows), LOW)],
        order=order,
        after=after,
    )


BITS = ((1, 2, 4), (1, 4, 2))


def slab_order():
    place = jnp.arange(SLABS, dtype=jnp.int32)
    if lax.axis_size("batch") != SLABS:
        return jnp.stack([place, place])
    orders = []
    for bits in BITS:
        apart = sum(((place >> (2 - j)) & 1) * bit for j, bit in enumerate(bits))
        orders.append(apart ^ lax.axis_index("batch"))
    return jnp.stack(orders)


class Sums:
    def __init__(self, axes, keep_a, send_a, keep_b, send_b):
        self.axes, self.stage = axes, 0
        self.terms, self.send = ([keep_a], [keep_b]), [send_a, send_b]

    def go(self):
        return [swap(send, "batch", bits[self.stage]) for send, bits in zip(self.send, BITS)]

    def land(self, arrived):
        terms = [own + [other] for own, other in zip(self.terms, arrived)]
        self.stage += 1
        if self.stage == 3:
            return [total(each).reshape(-1, each[0].shape[-1]) for each in terms]
        halves = [
            [jnp.split(one, 2, axis) for one in each] for each, axis in zip(terms, self.axes)
        ]
        self.terms = [[one[0] for one in each] for each in halves]
        self.send = [total([one[1] for one in each]).astype(LOW) for each in halves]
        return self.send


def total(terms):
    return sum(one.astype(jnp.float32) for one in terms)


class TokenSum:
    def __init__(self, values):
        self.low = jnp.where(lax.axis_index("tok") & 1, 1, 0)
        self.high = lax.axis_index("tok") >> 1
        pairs = values.reshape((2, 2) + values.shape[1:])
        self.keep = lax.dynamic_index_in_dim(pairs, self.low, 1, False)
        self.send = [lax.dynamic_index_in_dim(pairs, 1 - self.low, 1, False).astype(LOW)]
        self.stage = 0

    def go(self):
        return [swap(self.send[0], "tok", (1, 2, 2, 1)[self.stage])]

    def land(self, arrived):
        other = arrived[0]
        self.stage += 1
        if self.stage == 1:
            whole = self.keep + other.astype(jnp.float32)
            self.keep = lax.dynamic_index_in_dim(whole, self.high, 0, False)
            self.send = [lax.dynamic_index_in_dim(whole, 1 - self.high, 0, False).astype(LOW)]
        elif self.stage == 2:
            self.send = [(self.keep + other.astype(jnp.float32)).astype(LOW)]
        else:
            own, axis = ((self.high, 0), (self.low, 1))[self.stage - 3]
            mine = self.send[0]
            pair = jnp.stack([mine, other], axis), jnp.stack([other, mine], axis)
            self.send = [jnp.where(own == 0, pair[0], pair[1])]
        if self.stage < 4:
            return self.send
        whole = self.send[0].reshape((4,) + self.send[0].shape[2:])
        return [one.reshape(-1, one.shape[-1]) for one in jnp.split(whole, 2, axis=1)]


def arrive(moves, after, wait=0):
    flat = hold_until([one for move in moves for one in move], after, wait)
    held, at = [], 0
    for move in moves:
        held.append(flat[at : at + len(move)])
        at += len(move)
    return held


class DirectSum:
    def __init__(self, values):
        self.me, self.whole = lax.axis_index("tok"), None

        def quarter(at):
            return lax.dynamic_index_in_dim(values, at, 0, False)

        self.own = quarter(self.me)
        self.send = [quarter(self.me ^ step).astype(LOW) for step in (1, 2, 3)]

    def go(self):
        return [swap(one, "tok", step) for step, one in zip((1, 2, 3), self.send)]

    def land(self, arrived):
        if self.whole is None:
            self.whole = total([self.own] + arrived).astype(LOW)
            self.send = [self.whole] * 3
            return self.send[:1]
        one, two, three = arrived
        rows = [jnp.stack([self.whole, one]), jnp.stack([two, three])]
        rows = [jnp.where(self.me & 1, row[::-1], row) for row in rows]
        upper = self.me >> 1
        rows = jnp.where(upper == 0, rows[0], rows[1]), jnp.where(upper == 0, rows[1], rows[0])
        whole = jnp.concatenate(rows)
        return [each.reshape(-1, each.shape[-1]) for each in jnp.split(whole, 2, axis=1)]


def token_sum(top, bottom, kind=TokenSum):
    parts = [one.reshape(4, -1, one.shape[1]) for one in (top, bottom)]
    return kind(jnp.concatenate(parts, axis=1))


def spread_parts(turned, values):
    parts = [gather_rows(choice, values) for choice in jnp.split(turned, lax.axis_size("tok"))]
    parts[1] = hold_until(parts[1:2], parts[2:])[0]
    return parts


def swap_groups(parts):
    return [parts[0]] + [swap(parts[step], "tok", step) for step in range(1, len(parts))]


def place_rows(choice, parts):
    return gather_rows(choice, jnp.concatenate(parts, axis=0))


def on_device(
    block_input,
    crop_ids,
    ln1_gain,
    ln1_bias,
    w_qkv,
    q_bias,
    v_bias,
    w_out,
    out_bias,
    ln2_gain,
    ln2_bias,
    w_fc1,
    fc1_bias,
    w_fc2,
    fc2_bias,
    out_grad,
):
    packs, local_rows, features = block_input.shape
    rows = packs * local_rows
    shards = lax.axis_size("batch")
    paired = shards == SLABS
    send, receive, send_turned, receive_turned, overflow = exchange_plan(crop_ids)
    arrived = swap_groups(spread_parts(send_turned, block_input.reshape(rows, features)))
    held_back = spread_parts(send_turned, out_grad.reshape(rows, features))
    held_back = hold_until(held_back, arrived[1:])
    vectors = [out_bias, ln2_gain, ln2_bias, fc2_bias, ln1_gain, ln1_bias]
    vectors = jnp.stack(vectors + [jnp.zeros_like(out_bias)] * 2)
    bias = jnp.concatenate([q_bias, jnp.zeros_like(q_bias), v_bias])[None]
    grad_parts = swap_groups(held_back)
    fronts = front(
        arrived, receive, vectors, w_qkv, bias, w_out, w_fc1, fc1_bias[None], w_fc2, receive_turned
    )
    low_input, normed_one, joined, attended, *parts, n2t, hat, rstd, hidden, slope = fronts
    *parts, grad_parts[1], grad_parts[2], grad_parts[3] = hold_until(
        list(parts) + grad_parts[1:], []
    )
    low_grad = place_rows(receive, grad_parts)
    order = slab_order()

    def back(part, more, after):
        return list(
            feed_back(order, part, 2, low_grad, n2t, w_fc1, w_fc2, hidden, slope, more, after)
        )

    size = features // SLABS
    halves = SLABS, SLABS // 2, size, -1

    def slab_sums(back):
        return Sums((0, 1), back[0], back[1], back[2].reshape(halves), back[3].reshape(halves))

    backs = [back(0, [], parts[1:])]
    near = swap(parts[2], "tok", 2)
    backs[0][1], backs[0][3], near = hold_until([backs[0][1], backs[0][3], near], [])
    far = [swap(parts[3], "tok", 3), swap(parts[1], "tok", 1)]
    wait = [backs[0][1]]
    if paired:
        one = slab_sums(backs[0])
        wait = one.land(arrive([one.go()], [], 5)[0])
    backs.append(back(1, [backs[0][5], hat, rstd, vectors, w_out], wait))
    grad_branch, grad_attended, sums_two = backs[1][5:]
    wait = []
    if paired:
        *held, backs[1][1], backs[1][3] = hold_until(
            one.go() + far + [backs[1][1], backs[1][3]], []
        )
        wait, far = one.land(held[:2]), held[2:]
        two = slab_sums(backs[1])
    parts = [parts[0], far[1], near, far[0]]
    grad_joined = image_attention_back(joined, grad_attended, 0, 2, None, wait)
    if paired:
        held = arrive([one.go(), two.go()], [grad_joined])
        left = token_sum(*one.land(held[0]))
        wait = left.send + two.land(held[1])
    grad_joined = image_attention_back(joined, grad_attended, 1, 2, grad_joined, wait)
    if paired:
        moving = two.go()
        wait = left.land(arrive([left.go()], [grad_joined])[0])
    *input_parts, sums_one, joined_sums = first_norm_back(
        grad_joined, w_qkv, low_input, grad_branch, vectors, receive_turned, wait
    )
    wait = []
    if paired:
        *held, sums_one = hold_until(left.go() + moving + input_parts[1:] + [sums_one], [])
        input_parts[1:] = held[3:]
        left.land(held[:1])
        wait = two.land(held[1:3])
    input_parts = swap_groups(input_parts)
    short = [
        sums_one[0],
        sums_one[1],
        joined_sums[0, :features],
        joined_sums[0, 2 * features :],
        sums_two[0],
        sums_two[1],
        sums_two[2],
        sums_two[3],
        jnp.stack([each[4].reshape(SLABS, -1) for each in backs], axis=1).reshape(-1),
        jnp.broadcast_to(overflow.astype(jnp.float32), (SLABS * features // 2,)),
    ]
    short_slabs = jnp.concatenate([each.reshape(SLABS, -1) for each in short], axis=1)
    short_slabs = short_slabs.reshape(SLABS, -1, 4 * size)
    short_slabs = jnp.pad(short_slabs, ((0, 0), (0, 64 - short_slabs.shape[1]), (0, 0)))
    products = attention_products(
        order, normed_one, attended, grad_joined, grad_branch, short_slabs, wait
    )
    output = place_rows(send, parts)

    if paired:
        products = list(products)
        held = hold_until(
            [products[1], products[3]] + two.go() + input_parts[2:3] + left.send, []
        )
        products[1], products[3] = held[:2]
        input_parts[2] = held[4]
        left.send = held[5:]
        three = Sums((0, 0), *products)
        right = token_sum(*two.land(held[2:4]))
        three.land(arrive([three.go()], right.send, 6)[0])
        held = arrive([three.go(), left.go()], three.send + [output], 24)
        three.land(held[0])
        held = arrive([right.go(), held[1], input_parts[1:2]], three.send, 2)
        right.land(held[0])
        left.land(held[1])
        input_parts[1] = held[2][0]
        top, bottom = three.land(arrive([three.go()], right.send + left.send, 14)[0])
        bottom = jnp.pad(bottom, ((0, top.shape[0] - bottom.shape[0]), (0, 0)))
        last = token_sum(top, bottom, DirectSum)
        held = arrive([right.go(), input_parts[3:]], last.send, 2)
        right.land(held[0])
        input_parts[3] = held[1][0]
        held = arrive([right.go(), left.go()], last.send, 12)
        right.land(held[0])
        first = left.land(held[1])
        last.land(arrive([last.go()], right.send, 12)[0])
        second = right.land(arrive([right.go()], last.send[:1], 8)[0])
        input_grad = place_rows(send, input_parts)
        grad_fc1 = jnp.concatenate([first[0], second[0]], axis=1).astype(jnp.float32)
        fc2 = [each[1].reshape(SLABS, size, -1) for each in (first, second)]
        fc2 = jnp.stack(fc2, axis=1).transpose(0, 1, 3, 2).reshape(-1, size)
        grad_fc2 = fc2.astype(jnp.float32)
        third = last.land(arrive([last.go()], [input_grad, grad_fc1, grad_fc2], 8)[0])
        halves = [each[: features // 2] for each in third]
        grad_attention = jnp.concatenate(halves, axis=0)
        grad_qkv, grad_out = grad_attention[:, : 3 * size], grad_attention[:, 3 * size :]
        tail = third[0][features // 2 :].reshape(-1).astype(jnp.float32)
        pieces = [tail[i * size : (i + 1) * size] for i in range(8)]
        pieces += [tail[8 * size : 12 * size], tail[12 * size :][:1]]
    else:
        input_grad = place_rows(send, input_parts)
        fc1 = jnp.stack([jnp.concatenate(each[:2]) for each in backs], axis=2)
        grad_fc1 = share_columns(fc1.transpose(1, 0, 2, 3).reshape(features, -1))
        fc2 = jnp.stack([jnp.concatenate(each[2:4], axis=1) for each in backs], axis=2)
        fc2 = fc2.transpose(1, 0, 2, 3).reshape(shards, features // shards, -1)
        grad_fc2 = share_slabs(fc2).T
        both = [jnp.concatenate(products[:2])[:, : features // 2], jnp.concatenate(products[2:])]
        both = jnp.concatenate(both, axis=1)
        grad_qkv = share_columns(both[:, :, : 3 * size].transpose(1, 0, 2).reshape(features, -1))
        grad_out = share_columns(both[:, :, 3 * size :].transpose(1, 0, 2).reshape(features, -1))
        widths = [each.shape[0] // shards for each in short]
        packed = jnp.concatenate([each.reshape(shards, -1) for each in short], axis=1)
        packed = share_slabs(packed.astype(LOW)).astype(jnp.float32)
        pieces, at = [], 0
        for width in widths:
            pieces.append(packed[at : at + width])
            at += width
    fast = (
        output.reshape(block_input.shape),
        input_grad.reshape(block_input.shape),
        pieces[0],
        pieces[1],
        grad_qkv.astype(jnp.float32),
        pieces[2],
        pieces[3],
        grad_out.astype(jnp.float32),
        pieces[4],
        pieces[5],
        pieces[6],
        grad_fc1.astype(jnp.float32),
        pieces[8],
        grad_fc2.astype(jnp.float32),
        pieces[7],
    )

    def unfinished(state):
        return state[0] > 0.5

    def redo(state):
        return (
            jnp.float32(0.0),
            in_place(
                block_input,
                crop_ids,
                ln1_gain,
                ln1_bias,
                w_qkv,
                q_bias,
                v_bias,
                w_out,
                out_bias,
                ln2_gain,
                ln2_bias,
                w_fc1,
                fc1_bias,
                w_fc2,
                fc2_bias,
                out_grad,
            ),
        )

    return lax.while_loop(unfinished, redo, (pieces[9][0], fast))[1]


def solution(mesh):
    in_specs = (
        P("batch", "tok", None),
        P("batch", None),
        P(),
        P(),
        P(),
        P(),
        P(),
        P(),
        P(),
        P(),
        P(),
        P(),
        P(),
        P(),
        P(),
        P("batch", "tok", None),
    )
    out_specs = (
        P("batch", "tok", None),
        P("batch", "tok", None),
        P("batch"),
        P("batch"),
        P(None, "batch"),
        P("batch"),
        P("batch"),
        P(None, "batch"),
        P("batch"),
        P("batch"),
        P("batch"),
        P(None, "batch"),
        P("batch"),
        P(None, "batch"),
        P("batch"),
    )
    return jax.shard_map(
        on_device, mesh=mesh, in_specs=in_specs, out_specs=out_specs, check_vma=False
    )
```

```python
import functools

import jax
import jax.numpy as jnp
from jax import lax
from jax.experimental import pallas as pl
from jax.experimental.pallas import tpu as pltpu
from jax.sharding import PartitionSpec as P

H = 16
HD = 64
IMAGE = 160
LOW = jnp.bfloat16


epsilon = 1e-06
masked_score = -1000000000.0


def layer_norm(values, gain, shift):
    center = values - jnp.mean(values, axis=-1, keepdims=True)
    variance = jnp.mean(center * center, axis=-1, keepdims=True)
    return center * lax.rsqrt(variance + epsilon) * gain + shift


def split_heads(values):
    return values.reshape(values.shape[0], H, HD)


def join_heads(values):
    return values.reshape(values.shape[0], H * HD)


def column_sum(values):
    return jnp.sum(values.astype(jnp.float32), axis=(0, 1))


def project_qkv(inputs, ln1_gain, ln1_bias, w_qkv, q_bias, v_bias):
    normed, norm_back = jax.vjp(layer_norm, inputs, ln1_gain, ln1_bias)
    normed_low = normed.astype(jnp.bfloat16)
    joined = jnp.dot(normed_low, w_qkv, preferred_element_type=jnp.float32)
    features = inputs.shape[-1]
    query_low = (joined[..., :features] + q_bias).astype(jnp.bfloat16)
    key_low = joined[..., features : 2 * features].astype(jnp.bfloat16)
    value_low = (joined[..., 2 * features :] + v_bias).astype(jnp.bfloat16)
    return (normed_low, norm_back, query_low, key_low, value_low)


def pack_scores(query_pack, key_pack, same_pack):
    raw = jnp.einsum(
        "shd,lhd->hsl",
        split_heads(query_pack),
        split_heads(key_pack),
        preferred_element_type=jnp.float32,
    )
    return jnp.where(same_pack[None], raw * HD ** (-0.5), masked_score)


def attend_forward(pieces):
    query_pack, key_pack, value_pack, same_pack = pieces
    scores = pack_scores(query_pack, key_pack, same_pack)
    row_max = jnp.max(scores, axis=-1, keepdims=True)
    expo = jnp.exp(scores - row_max)
    totals = jnp.sum(expo, axis=-1, keepdims=True)
    log_total = row_max + jnp.log(totals)
    prob_low = (expo / totals).astype(jnp.bfloat16)
    mixed = jnp.einsum(
        "hsl,lhd->shd", prob_low, split_heads(value_pack), preferred_element_type=jnp.float32
    )
    return (join_heads(mixed).astype(jnp.bfloat16), log_total)


def attend_backward(pieces):
    query_pack, key_pack, value_pack, same_pack, log_total, grad_pack = pieces
    score_scale = HD ** (-0.5)
    scores_again = pack_scores(query_pack, key_pack, same_pack)
    prob_full = jnp.exp(scores_again - log_total)
    prob_back = prob_full.astype(jnp.bfloat16)
    grad_heads = split_heads(grad_pack)
    grad_prob = jnp.einsum(
        "shd,lhd->hsl", grad_heads, split_heads(value_pack), preferred_element_type=jnp.float32
    )
    spread = jnp.sum(prob_full * grad_prob, axis=-1, keepdims=True)
    grad_scores = (prob_full * (grad_prob - spread)).astype(jnp.bfloat16)
    grad_query = join_heads(
        jnp.einsum(
            "hsl,lhd->shd", grad_scores, split_heads(key_pack), preferred_element_type=jnp.float32
        )
        * score_scale
    ).astype(jnp.bfloat16)
    key_terms = join_heads(
        jnp.einsum(
            "hsl,shd->lhd", grad_scores, split_heads(query_pack), preferred_element_type=jnp.float32
        )
        * score_scale
    )
    value_terms = join_heads(
        jnp.einsum("hsl,shd->lhd", prob_back, grad_heads, preferred_element_type=jnp.float32)
    )
    return (grad_query, key_terms, value_terms)


def swap(values, axis, apart):
    return lax.ppermute(values, axis, [(i, i ^ apart) for i in range(lax.axis_size(axis))])


def gather_tokens(values):
    groups, me = lax.axis_size("tok"), lax.axis_index("tok")
    held = jnp.stack([values] + [swap(values, "tok", step) for step in range(1, groups)])
    return jnp.concatenate(
        [lax.dynamic_index_in_dim(held, me ^ at, 0, False) for at in range(groups)], axis=1
    )


def scatter_tokens(values):
    groups, me = lax.axis_size("tok"), lax.axis_index("tok")
    length = values.shape[1] // groups

    def part(at):
        return lax.dynamic_slice_in_dim(values, at * length, length, 1)

    return part(me) + sum(swap(part(me ^ step), "tok", step) for step in range(1, groups))


def sum_tokens(values):
    groups, me = lax.axis_size("tok"), lax.axis_index("tok")
    held, bits = values, []
    bit = 1
    while bit < groups:
        bits.append(bit)
        pairs = held.reshape((held.shape[0] // 2, 2) + held.shape[1:])
        own = jnp.where(me & bit, 1, 0)
        other = lax.dynamic_index_in_dim(pairs, 1 - own, 1, False).astype(LOW)
        held = lax.dynamic_index_in_dim(pairs, own, 1, False).astype(jnp.float32)
        held = held + swap(other, "tok", bit).astype(jnp.float32)
        bit *= 2
    held = held.astype(LOW)
    for bit in reversed(bits):
        arrived = swap(held, "tok", bit)
        own = (me & bit) > 0
        held = jnp.where(own, jnp.stack([arrived, held], 1), jnp.stack([held, arrived], 1))
        held = held.reshape((-1,) + held.shape[2:])
    return held


def share_slabs(slabs):
    me, held = lax.axis_index("batch"), slabs
    bit = 1
    while bit < lax.axis_size("batch"):
        pairs = held.reshape((held.shape[0] // 2, 2) + held.shape[1:])
        own = jnp.where(me & bit, 1, 0)
        other = lax.dynamic_index_in_dim(pairs, 1 - own, 1, False).astype(LOW)
        held = lax.dynamic_index_in_dim(pairs, own, 1, False).astype(jnp.float32)
        held = held + swap(other, "batch", bit).astype(jnp.float32)
        bit *= 2
    flat = held[0].reshape(-1)
    groups = lax.axis_size("tok")
    padded = jnp.pad(flat, (0, -flat.size % groups)).astype(LOW).reshape(groups, -1)
    return sum_tokens(padded).reshape(-1)[: flat.size].reshape(slabs.shape[1:])


def share_columns(grad):
    shards = lax.axis_size("batch")
    if grad.ndim == 1:
        return share_slabs(grad.astype(LOW).reshape(shards, -1)).astype(jnp.float32)
    slabs = grad.astype(LOW).reshape(grad.shape[0], shards, -1).transpose(1, 0, 2)
    return share_slabs(slabs).astype(jnp.float32)


def in_place(
    block_input,
    crop_ids,
    ln1_gain,
    ln1_bias,
    w_qkv,
    q_bias,
    v_bias,
    w_out,
    out_bias,
    ln2_gain,
    ln2_bias,
    w_fc1,
    fc1_bias,
    w_fc2,
    fc2_bias,
    out_grad,
):
    packs, local_rows, features = block_input.shape
    offset = lax.axis_index("tok") * local_rows
    own_crop = lax.dynamic_slice_in_dim(crop_ids, offset, local_rows, 1)
    same_crop = own_crop[:, :, None] == crop_ids[:, None, :]
    inputs = block_input.astype(jnp.float32)
    normed_one, norm_one_back, query_low, key_low, value_low = project_qkv(
        inputs, ln1_gain, ln1_bias, w_qkv, q_bias, v_bias
    )
    key_all, value_all = (
        gather_tokens(key_low),
        gather_tokens(value_low),
    )
    attended, log_total = lax.map(attend_forward, (query_low, key_all, value_all, same_crop))
    resid = inputs + jnp.dot(attended, w_out, preferred_element_type=jnp.float32) + out_bias
    normed_two, norm_two_back = jax.vjp(layer_norm, resid, ln2_gain, ln2_bias)
    normed_two_low = normed_two.astype(jnp.bfloat16)
    pre_act = jnp.dot(normed_two_low, w_fc1, preferred_element_type=jnp.float32) + fc1_bias

    def gelu_exact(values):
        return jax.nn.gelu(values, approximate=False)

    activated, gelu_back = jax.vjp(gelu_exact, pre_act)
    hidden = activated.astype(jnp.bfloat16)
    output = resid + jnp.dot(hidden, w_fc2, preferred_element_type=jnp.float32) + fc2_bias
    out_grad_full = out_grad.astype(jnp.float32)
    grad_fc2 = jnp.einsum("bsf,bsd->fd", hidden, out_grad, preferred_element_type=jnp.float32)
    grad_fc2_bias = column_sum(out_grad)
    grad_hidden = jnp.einsum("bsd,fd->bsf", out_grad, w_fc2, preferred_element_type=jnp.float32)
    grad_pre = gelu_back(grad_hidden)[0].astype(jnp.bfloat16)
    grad_fc1 = jnp.einsum(
        "bsd,bsf->df", normed_two_low, grad_pre, preferred_element_type=jnp.float32
    )
    grad_fc1_bias = column_sum(grad_pre)
    grad_normed_two = jnp.einsum("bsf,df->bsd", grad_pre, w_fc1, preferred_element_type=jnp.float32)
    resid_term, grad_ln2_gain, grad_ln2_bias = norm_two_back(grad_normed_two)
    grad_resid = out_grad_full + resid_term
    grad_branch = grad_resid.astype(jnp.bfloat16)
    grad_out = jnp.einsum("bsd,bse->de", attended, grad_branch, preferred_element_type=jnp.float32)
    grad_out_bias = column_sum(grad_branch)
    grad_attended = jnp.einsum(
        "bse,de->bsd", grad_branch, w_out, preferred_element_type=jnp.float32
    ).astype(jnp.bfloat16)
    normed_one, norm_one_back, query_low, key_low, value_low = project_qkv(
        inputs, ln1_gain, ln1_bias, w_qkv, q_bias, v_bias
    )
    key_all, value_all = (
        gather_tokens(key_low),
        gather_tokens(value_low),
    )
    grad_query, key_terms, value_terms = lax.map(
        attend_backward, (query_low, key_all, value_all, same_crop, log_total, grad_attended)
    )
    grad_key_sum, grad_value_sum = (
        scatter_tokens(key_terms),
        scatter_tokens(value_terms),
    )
    grad_key = grad_key_sum.astype(jnp.bfloat16)
    grad_value = grad_value_sum.astype(jnp.bfloat16)
    grad_joined = jnp.concatenate([grad_query, grad_key, grad_value], axis=-1)
    grad_qkv = jnp.einsum(
        "bsd,bse->de", normed_one, grad_joined, preferred_element_type=jnp.float32
    )
    grad_q_bias = column_sum(grad_query)
    grad_v_bias = column_sum(grad_value)
    grad_normed_one = jnp.einsum(
        "bse,de->bsd", grad_joined, w_qkv, preferred_element_type=jnp.float32
    )
    input_term, grad_ln1_gain, grad_ln1_bias = norm_one_back(grad_normed_one)
    input_grad = (grad_resid + input_term).astype(jnp.bfloat16)
    summed = [
        share_columns(grad)
        for grad in (
            grad_ln1_gain,
            grad_ln1_bias,
            grad_qkv,
            grad_q_bias,
            grad_v_bias,
            grad_out,
            grad_out_bias,
            grad_ln2_gain,
            grad_ln2_bias,
            grad_fc1,
            grad_fc1_bias,
            grad_fc2,
            grad_fc2_bias,
        )
    ]
    return (
        output.astype(jnp.bfloat16),
        input_grad,
        summed[0],
        summed[1],
        summed[2],
        summed[3],
        summed[4],
        summed[5],
        summed[6],
        summed[7],
        summed[8],
        summed[9],
        summed[10],
        summed[11],
        summed[12],
    )


def crop_of_row(axis):
    row = lax.broadcasted_iota(jnp.int32, (IMAGE, IMAGE), axis)
    return jnp.where(row < 50, 0, jnp.where(row < 100, 1, 2 + (row - 100) // 10))


def head_halves(dtype):
    lane = lax.broadcasted_iota(jnp.int32, (1, 2 * HD), 1)
    first = (lane < HD).astype(jnp.float32)
    return first, (first.astype(dtype), (1.0 - first).astype(dtype))


def head_prob(query_half, keys, same_crop):
    raw = lax.dot_general(
        query_half, keys, (((1,), (1,)), ((), ())), preferred_element_type=jnp.float32
    )
    scores = jnp.where(same_crop, raw * HD ** (-0.5), masked_score)
    expo = jnp.exp(scores - jnp.max(scores, axis=-1, keepdims=True))
    return expo / jnp.sum(expo, axis=-1, keepdims=True)


def attend_image(joined_ref, out_ref, rows):
    features = out_ref.shape[1]
    same_crop = crop_of_row(0) == crop_of_row(1)
    first, halves = head_halves(joined_ref.dtype)
    for at in range(0, features, 2 * HD):
        query = joined_ref[rows, at : at + 2 * HD]
        keys = joined_ref[rows, features + at : features + at + 2 * HD]
        values = joined_ref[rows, 2 * features + at : 2 * features + at + 2 * HD]
        mixed = []
        for half in halves:
            prob = head_prob(query * half, keys, same_crop).astype(jnp.bfloat16)
            mixed.append(jnp.dot(prob, values, preferred_element_type=jnp.float32))
        both = mixed[0] * first + mixed[1] * (1.0 - first)
        out_ref[rows, at : at + 2 * HD] = both.astype(out_ref.dtype)


def exchange_plan(crop_ids):
    packs, length = crop_ids.shape
    groups, me = lax.axis_size("tok"), lax.axis_index("tok")
    local = length // groups
    rows = packs * local
    capacity = -(-rows * 13 // (groups * 10) // 16) * 16
    order = crop_ids * length + jnp.arange(length, dtype=jnp.int32)
    number = jnp.arange(rows, dtype=jnp.int32)
    earlier = number[None, :] < number[:, None]

    def rank_of(some):
        return jnp.sum((order[:, None, :] < some[:, :, None]).astype(jnp.int32), axis=-1)

    def slot_of(target):
        same = target[..., :, None] == target[..., None, :]
        return jnp.sum((same & earlier).astype(jnp.int32), axis=-1)

    own = rank_of(lax.dynamic_slice_in_dim(order, me * local, local, 1)) // local
    own = own.reshape(rows)
    own_slot = slot_of(own)
    send_at = jnp.where(own_slot < capacity, (own ^ me) * capacity + own_slot, -1)

    def by_source(values):
        return values.reshape(packs, groups, local).transpose(1, 0, 2).reshape(groups, rows)

    rank = rank_of(order)
    target = by_source(rank // local)
    place = by_source(rank % local + local * jnp.arange(packs, dtype=jnp.int32)[:, None])
    slot = slot_of(target)
    overflow = jnp.max(slot) >= capacity
    source = jnp.arange(groups, dtype=jnp.int32)[:, None]
    arrive_at = (target == me) & (slot < capacity)
    arrive_at = jnp.where(arrive_at, (source ^ me) * capacity + slot + 1, 0)
    hits = (place[None] == number[:, None, None]) & (target == me)[None]
    receive_at = jnp.sum(jnp.where(hits, arrive_at[None], 0), axis=(1, 2)) - 1
    lanes = jnp.arange(groups * capacity, dtype=jnp.int32)
    send, receive = ((at[:, None] == lanes).astype(LOW) for at in (send_at, receive_at))
    send_turned, receive_turned = (
        (lanes[:, None] == at).astype(LOW) for at in (send_at, receive_at)
    )
    return send, receive, send_turned, receive_turned, overflow


def gather_rows(choice, values):
    return jnp.dot(choice, values, preferred_element_type=jnp.float32).astype(jnp.bfloat16)


SLABS = 8
MIB = 1024 * 1024
MICROSECOND = 1000 * 1000 * 1000


def dot(left, right):
    return jnp.dot(left, right, preferred_element_type=jnp.float32)


def dot_back(left, weight):
    return lax.dot_general(
        left, weight, (((1,), (1,)), ((), ())), preferred_element_type=jnp.float32
    )


def gelu_and_slope(z):
    tail = jnp.exp(z * z * -0.5)
    t = 1.0 / (1.0 + (0.3275911 * 0.5**0.5) * jnp.abs(z))
    series = 0.7107068705 + t * (-0.7265760135 + t * 0.5307027145)
    beyond = tail * (t * (0.127414796 + t * (-0.142248368 + t * series)))
    below = jnp.where(z >= 0.0, 1.0 - beyond, beyond)
    return z * below, below + z * tail * 0.3989422804014327


def whole_block(shape):
    return pl.BlockSpec(shape, lambda step, *_: (0,) * len(shape))


def held_block(shape):
    return pl.BlockSpec(
        shape, lambda step, *_: (0,) * len(shape), pipeline_mode=pl.Buffered(1)
    )


UNREAD = pl.BlockSpec(memory_space=pl.ANY)


BIG = 2 * MIB


def place_of(shape, dtype, far):
    size = dtype.dtype.itemsize
    for extent in shape:
        size *= extent
    return pltpu.HBM(shape, dtype) if far or size >= BIG else jax.ShapeDtypeStruct(shape, dtype)


def stay(array, limit=BIG):
    if array.size * array.dtype.itemsize > limit:
        return pltpu.with_memory_space_constraint(array, pltpu.HBM)
    return array


def call(
    kernel, name, grid, ins, outs, flops, scratch=(), order=None, after=(), aliases=None, vmem=40, far=(),
):
    first = 0 if order is None else 1
    given = first + len(ins)

    def body(*refs):
        kernel(*refs[:given], *refs[given + len(after) :])

    return pl.pallas_call(
        body,
        grid_spec=pltpu.PrefetchScalarGridSpec(
            num_scalar_prefetch=first,
            grid=grid,
            in_specs=[spec for _, spec in ins] + [UNREAD] * len(after),
            out_specs=[spec for _, _, spec in outs],
            scratch_shapes=list(scratch),
        ),
        out_shape=[
            place_of(shape, dtype, i in far) for i, (shape, dtype, _) in enumerate(outs)
        ],
        input_output_aliases=aliases or {},
        compiler_params=pltpu.CompilerParams(vmem_limit_bytes=vmem * MIB),
        cost_estimate=pl.CostEstimate(flops=flops, bytes_accessed=0, transcendentals=0),
        name=name,
    )(*([] if order is None else [order]), *[stay(array) for array, _ in ins], *after)


def hold_until(values, after, wait=0):
    count = len(values)
    held = pl.pallas_call(
        lambda *refs: None,
        in_specs=[UNREAD] * (count + len(after)),
        out_specs=[UNREAD] * count,
        out_shape=[jax.ShapeDtypeStruct(one.shape, one.dtype) for one in values],
        input_output_aliases={i: i for i in range(count)},
        cost_estimate=pl.CostEstimate(
            flops=wait * MICROSECOND, bytes_accessed=0, transcendentals=0
        ),
        name="hold_until",
    )(*values, *after)
    return list(held)


def front_kernel(
    part0, part1, part2, part3, receive_ref, vec_ref, w_qkv_ref, bias_ref,
    w_out_ref, w1_ref, b1_ref, w2_ref, turn_ref,
    x_ref, normed_ref, joined_ref, att_ref, out0, out1, out2, out3,
    n2t_ref, hat_ref, rstd_ref, hidden_ref, slope_ref,
    parcels, joined_s, n2_s, acc_s, *, projections, images,
):
    step, steps = pl.program_id(0), pl.num_programs(0)
    rows, features = x_ref.shape
    chunk = rows // 4
    size = part0.shape[0]
    block = w_qkv_ref.shape[1]

    @pl.when(step == 0)
    def _():
        for i, ref in enumerate((part0, part1, part2, part3)):
            parcels[i * size : (i + 1) * size, :] = ref[...]

        def part(i, carry):
            at = pl.ds(pl.multiple_of(i * chunk, chunk), chunk)
            x = dot(receive_ref[at, :], parcels[...])
            x_ref[at, :] = x.astype(LOW)
            center = x - jnp.mean(x, axis=-1, keepdims=True)
            rstd = lax.rsqrt(jnp.mean(center * center, axis=-1, keepdims=True) + epsilon)
            normed = center * rstd * vec_ref[4:5, :] + vec_ref[5:6, :]
            normed_ref[at, :] = normed.astype(LOW)
            return carry

        lax.fori_loop(0, rows // chunk, part, 0)

    @pl.when(step < projections)
    def _():
        joined = (dot(normed_ref[...], w_qkv_ref[...]) + bias_ref[...]).astype(LOW)
        joined_ref[...] = joined
        joined_s[:, pl.ds(pl.multiple_of(step * block, block), block)] = joined

    @pl.when((step >= projections) & (step < projections + images))
    def _():
        at = pl.ds(pl.multiple_of((step - projections) * IMAGE, IMAGE), IMAGE)
        attend_image(joined_s, att_ref, at)

    @pl.when(step == projections + images)
    def _():
        def part(i, carry):
            at = pl.ds(pl.multiple_of(i * chunk, chunk), chunk)
            resid = x_ref[at, :].astype(jnp.float32) + dot(att_ref[at, :], w_out_ref[...])
            resid = resid + vec_ref[0:1, :]
            center = resid - jnp.mean(resid, axis=-1, keepdims=True)
            rstd = lax.rsqrt(jnp.mean(center * center, axis=-1, keepdims=True) + epsilon)
            hat = center * rstd
            hat_ref[at, :] = hat.astype(LOW)
            rstd_ref[at, :] = jnp.broadcast_to(rstd, (chunk, rstd_ref.shape[1]))
            acc_s[at, :] = resid + vec_ref[3:4, :]
            n2_s[at, :] = (hat * vec_ref[1:2, :] + vec_ref[2:3, :]).astype(LOW)
            return carry

        lax.fori_loop(0, rows // chunk, part, 0)
        n2t_ref[...] = n2_s[...].T

    @pl.when(step >= projections + images)
    def _():
        act, slope = gelu_and_slope(dot(n2_s[...], w1_ref[...]) + b1_ref[...])
        hidden_ref[...] = act.astype(LOW)
        slope_ref[...] = slope.astype(LOW)
        acc_s[...] += dot(hidden_ref[...], w2_ref[...])

    @pl.when(step == steps - 1)
    def _():
        out = acc_s[...].astype(LOW)
        for i, ref in enumerate((out0, out1, out2, out3)):
            ref[...] = dot(turn_ref[i * size : (i + 1) * size, :], out).astype(LOW)


def parcels_out(turned, features):
    shape = (turned.shape[0] // 4, features)
    return [(shape, LOW, whole_block(shape))] * 4


def front(parts, receive, vectors, w_qkv, bias, w_out, w1, b1, w2, turned):
    rows, features = receive.shape[0], w_qkv.shape[0]
    width = w1.shape[1]
    block = width // SLABS
    projections, images = w_qkv.shape[1] // block, rows // IMAGE

    def early(step):
        return (0, jnp.minimum(step, projections - 1))

    def late(step):
        return (0, jnp.maximum(step - projections - images, 0))

    held = [(part, held_block(part.shape)) for part in parts]
    held += [(receive, held_block(receive.shape)), (vectors, held_block(vectors.shape))]
    tokens = ((rows, features), LOW, whole_block((rows, features)))
    return call(
        functools.partial(front_kernel, projections=projections, images=images),
        "front",
        (projections + images + SLABS,),
        held
        + [
            (w_qkv, pl.BlockSpec((features, block), early)),
            (bias, pl.BlockSpec((1, block), early)),
            (w_out, held_block(w_out.shape)),
            (w1, pl.BlockSpec((features, block), late)),
            (b1, pl.BlockSpec((1, block), late)),
            (w2, pl.BlockSpec((block, features), lambda step: late(step)[::-1])),
            (turned, held_block(turned.shape)),
        ],
        [tokens, tokens, ((rows, w_qkv.shape[1]), LOW, pl.BlockSpec((rows, block), early)), tokens]
        + parcels_out(turned, features)
        + [
            ((features, rows), LOW, whole_block((features, rows))),
            tokens,
            ((rows, 128), jnp.float32, whole_block((rows, 128))),
            ((rows, width), LOW, pl.BlockSpec((rows, block), late)),
            ((rows, width), LOW, pl.BlockSpec((rows, block), late)),
        ],
        flops=44 * MICROSECOND,
        scratch=[
            pltpu.VMEM((4 * parts[0].shape[0], features), LOW),
            pltpu.VMEM((rows, w_qkv.shape[1]), LOW),
            pltpu.VMEM((rows, features), LOW),
            pltpu.VMEM((rows, features), jnp.float32),
        ],
        vmem=56,
    )


def kept(step, order):
    return (jnp.minimum(step, SLABS // 2 - 1), 0, 0)


def sent(step, order):
    return (jnp.maximum(step - SLABS // 2, 0), 0, 0)


def halves_out(extra, rows, width):
    outs = []
    for more in (extra, 0):
        shape = (rows + more, width)
        for place in (kept, sent):
            outs.append(((SLABS // 2,) + shape, LOW, pl.BlockSpec((1,) + shape, place)))
    return outs


def norm_back(grad, gain, hat, rstd):
    scaled = grad * gain
    inner = scaled - jnp.mean(scaled, axis=-1, keepdims=True)
    return (inner - hat * jnp.mean(scaled * hat, axis=-1, keepdims=True)) * rstd


def column_total(values):
    return jnp.sum(values, axis=0, keepdims=True)


def feed_back_kernel(
    order_ref, og_ref, n2t_ref, w1_ref, w2_ref, hidden_ref, slope_ref, *rest, last
):
    if last:
        first_ref, hat_ref, rstd_ref, vec_ref, w_out_ref, *rest = rest
        keep1_ref, send1_ref, keep2_ref, send2_ref, db1_ref, *rest = rest
        branch_ref, att_ref, sums_ref, ogt_s, dn2_ref = rest
    else:
        keep1_ref, send1_ref, keep2_ref, send2_ref, db1_ref, dn2_ref, ogt_s = rest
    step, steps = pl.program_id(0), pl.num_programs(0)
    rows, features = og_ref.shape
    slab, half, chunk = features // SLABS, features // 2, rows // 4

    @pl.when(step == 0)
    def _():
        for p in range(SLABS):
            at = pl.multiple_of(order_ref[1, p] * slab, slab)
            ogt_s[p * slab : (p + 1) * slab, :] = og_ref[:, pl.ds(at, slab)].T
        dn2_ref[...] = first_ref[...] if last else jnp.zeros_like(dn2_ref)

    hidden = hidden_ref[...]
    grad = dot_back(og_ref[...], w2_ref[...]) * slope_ref[...].astype(jnp.float32)
    grad = grad.astype(LOW)
    keep2_ref[0] = dot(ogt_s[:half, :], hidden).astype(LOW)
    send2_ref[0] = dot(ogt_s[half:, :], hidden).astype(LOW)
    db1_ref[...] = column_total(grad.astype(jnp.float32))
    dn2_ref[...] += dot_back(grad, w1_ref[...])
    dw1 = dot(n2t_ref[...], grad).astype(LOW)

    @pl.when(step < steps // 2)
    def _():
        keep1_ref[0] = dw1

    @pl.when(step >= steps // 2)
    def _():
        send1_ref[0] = dw1

    if last:

        @pl.when(step == steps - 1)
        def _():
            sums_ref[...] = jnp.zeros_like(sums_ref)

            def part(i, carry):
                at = pl.ds(pl.multiple_of(i * chunk, chunk), chunk)
                grad, hat = dn2_ref[at, :], hat_ref[at, :].astype(jnp.float32)
                og = og_ref[at, :].astype(jnp.float32)
                resid = og + norm_back(grad, vec_ref[1:2, :], hat, rstd_ref[at, 0:1])
                branch = resid.astype(LOW)
                branch_ref[at, :] = branch
                att_ref[at, :] = dot_back(branch, w_out_ref[...]).astype(LOW)
                sums_ref[0:1, :] += column_total(branch.astype(jnp.float32))
                sums_ref[1:2, :] += column_total(grad * hat)
                sums_ref[2:3, :] += column_total(grad)
                sums_ref[3:4, :] += column_total(og)
                return carry

            lax.fori_loop(0, rows // chunk, part, 0)


def feed_back(order, part, parts, og, n2t, w1, w2, hidden, slope, more, after):
    rows, features = og.shape
    width = w1.shape[1]
    block = width // (SLABS * parts)
    half = SLABS // 2
    last = bool(more)

    def at(step, order):
        return order[0, step] * parts + part

    columns = pl.BlockSpec((rows, block), lambda step, order: (0, at(step, order)))
    turned = pl.BlockSpec(
        (1, features // 2, block), lambda step, order: (order[0, step], 0, 0)
    )
    outs = [
        ((half, features, block), LOW, pl.BlockSpec((1, features, block), kept)),
        ((half, features, block), LOW, pl.BlockSpec((1, features, block), sent)),
        ((SLABS, features // 2, block), LOW, turned),
        ((SLABS, features // 2, block), LOW, turned),
        (
            (1, SLABS * block),
            jnp.float32,
            pl.BlockSpec((1, block), lambda step, order: (0, order[0, step])),
        ),
    ]
    scratch = [pltpu.VMEM((features, rows), LOW)]
    if last:
        outs += [
            (og.shape, LOW, whole_block(og.shape)),
            (og.shape, LOW, whole_block(og.shape)),
            ((8, features), jnp.float32, whole_block((8, features))),
        ]
        scratch.append(pltpu.VMEM(og.shape, jnp.float32))
    else:
        outs.append((og.shape, jnp.float32, whole_block(og.shape)))
    return call(
        functools.partial(feed_back_kernel, last=last),
        "feed_back",
        (SLABS,),
        [
            (og, held_block(og.shape)),
            (n2t, held_block(n2t.shape)),
            (w1, pl.BlockSpec((features, block), lambda step, order: (0, at(step, order)))),
            (w2, pl.BlockSpec((block, features), lambda step, order: (at(step, order), 0))),
            (hidden, columns),
            (slope, columns),
        ]
        + [(each, held_block(each.shape)) for each in more],
        outs,
        flops=18 * MICROSECOND,
        scratch=scratch,
        order=order,
        after=after,
    )


def attend_image_back(joined_ref, grad_ref, out_ref):
    features = grad_ref.shape[1]
    same_crop = crop_of_row(0) == crop_of_row(1)
    first, halves = head_halves(joined_ref.dtype)
    scale = HD ** (-0.5)
    for at in range(0, features, 2 * HD):
        query = joined_ref[:, at : at + 2 * HD]
        keys = joined_ref[:, features + at : features + at + 2 * HD]
        values = joined_ref[:, 2 * features + at : 2 * features + at + 2 * HD]
        grad = grad_ref[:, at : at + 2 * HD]
        terms = []
        for half in halves:
            scores = jnp.where(same_crop, dot_back(keys * half, query) * scale, masked_score)
            expo = jnp.exp(scores - jnp.max(scores, axis=0, keepdims=True))
            prob = expo * (1.0 / jnp.sum(expo, axis=0, keepdims=True))
            grad_prob = dot_back(values * half, grad)
            spread = jnp.sum(prob * grad_prob, axis=0, keepdims=True)
            grad_scores = (prob * (grad_prob - spread)).astype(LOW)
            terms.append(
                (
                    dot(grad_scores.T, keys) * scale,
                    dot(grad_scores, query) * scale,
                    dot(prob.astype(LOW), grad),
                )
            )
        for part in range(3):
            both = terms[0][part] * first + terms[1][part] * (1.0 - first)
            place = part * features + at
            out_ref[:, place : place + 2 * HD] = both.astype(out_ref.dtype)


def image_attention_back(joined, grad, part, parts, earlier, after):
    rows, width = joined.shape
    steps = rows // IMAGE // parts

    def kernel(joined_ref, grad_ref, *rest):
        attend_image_back(joined_ref, grad_ref, rest[-1])

    image = pl.BlockSpec((IMAGE, width), lambda step: (step + part * steps, 0))
    ins = [
        (joined, image),
        (grad, pl.BlockSpec((IMAGE, width // 3), lambda step: (step + part * steps, 0))),
    ]
    if earlier is not None:
        ins.append((earlier, UNREAD))
    return call(
        kernel,
        "attention_back",
        (steps,),
        ins,
        [((rows, width), LOW, image)],
        flops=17 * MICROSECOND,
        after=after,
        aliases=None if earlier is None else {2: 0},
    )[0]


def first_norm_kernel(
    joined_ref, w_ref, x_ref, branch_ref, vec_ref, turn_ref,
    part0, part1, part2, part3, sums_ref, joined_sums_ref, acc_s, out_s,
):
    step, steps = pl.program_id(0), pl.num_programs(0)
    rows = x_ref.shape[0]
    chunk = rows // 4

    @pl.when(step == 0)
    def _():
        acc_s[...] = jnp.zeros_like(acc_s)

    acc_s[...] += dot_back(joined_ref[...], w_ref[...])
    joined_sums_ref[...] = column_total(joined_ref[...].astype(jnp.float32))

    @pl.when(step == steps - 1)
    def _():
        sums_ref[...] = jnp.zeros_like(sums_ref)

        def part(i, carry):
            at = pl.ds(pl.multiple_of(i * chunk, chunk), chunk)
            x = x_ref[at, :].astype(jnp.float32)
            center = x - jnp.mean(x, axis=-1, keepdims=True)
            rstd = lax.rsqrt(jnp.mean(center * center, axis=-1, keepdims=True) + epsilon)
            grad, hat = acc_s[at, :], center * rstd
            term = norm_back(grad, vec_ref[4:5, :], hat, rstd)
            out_s[at, :] = (branch_ref[at, :].astype(jnp.float32) + term).astype(LOW)
            sums_ref[0:1, :] += column_total(grad * hat)
            sums_ref[1:2, :] += column_total(grad)
            return carry

        lax.fori_loop(0, rows // chunk, part, 0)
        size = part0.shape[0]
        for i, ref in enumerate((part0, part1, part2, part3)):
            ref[...] = dot(turn_ref[i * size : (i + 1) * size, :], out_s[...]).astype(LOW)


def first_norm_back(grad_joined, w_qkv, x, branch, vectors, turned, after):
    rows, features = x.shape
    block = features // 2
    return call(
        first_norm_kernel,
        "first_norm_back",
        (w_qkv.shape[1] // block,),
        [
            (grad_joined, pl.BlockSpec((rows, block), lambda step: (0, step))),
            (w_qkv, pl.BlockSpec((features, block), lambda step: (0, step))),
            (x, whole_block(x.shape)),
            (branch, whole_block(x.shape)),
            (vectors, whole_block(vectors.shape)),
            (turned, whole_block(turned.shape)),
        ],
        parcels_out(turned, features)
        + [
            ((8, features), jnp.float32, whole_block((8, features))),
            ((1, w_qkv.shape[1]), jnp.float32, pl.BlockSpec((1, block), lambda step: (0, step))),
        ],
        flops=2 * MICROSECOND,
        far=range(5),
        scratch=[pltpu.VMEM(x.shape, jnp.float32), pltpu.VMEM(x.shape, LOW)],
        after=after,
    )


def products_kernel(
    order_ref, n1_ref, att_ref, gj_a, gj_b, gb_a, gb_b, short_ref,
    keep_a, send_a, keep_b, send_b, n1t_s, attt_s,
):
    step, steps = pl.program_id(0), pl.num_programs(0)
    half, wide = n1_ref.shape[1] // 2, gj_a.shape[1]

    @pl.when(step == 0)
    def _():
        n1t_s[...] = n1_ref[...].T
        attt_s[...] = att_ref[...].T

    def fill(out_a, out_b):
        out_a[0, :half, :wide] = dot(n1t_s[:half, :], gj_a[...]).astype(LOW)
        out_a[0, :half, wide:] = dot(attt_s[:half, :], gb_a[...]).astype(LOW)
        out_a[0, half:, :] = short_ref[0].astype(LOW)
        out_b[0, :, :wide] = dot(n1t_s[half:, :], gj_b[...]).astype(LOW)
        out_b[0, :, wide:] = dot(attt_s[half:, :], gb_b[...]).astype(LOW)

    @pl.when(step < steps // 2)
    def _():
        fill(keep_a, keep_b)

    @pl.when(step >= steps // 2)
    def _():
        fill(send_a, send_b)


def attention_products(order, normed, attended, joined, branch, short, after):
    rows, features = normed.shape
    wide, narrow = joined.shape[1] // SLABS, branch.shape[1] // SLABS
    return call(
        products_kernel,
        "attention_products",
        (SLABS,),
        [
            (stay(normed, MIB), whole_block(normed.shape)),
            (stay(attended, MIB), whole_block(attended.shape)),
            (joined, pl.BlockSpec((rows, wide), lambda step, order: (0, order[0, step]))),
            (joined, pl.BlockSpec((rows, wide), lambda step, order: (0, order[1, step]))),
            (branch, pl.BlockSpec((rows, narrow), lambda step, order: (0, order[0, step]))),
            (branch, pl.BlockSpec((rows, narrow), lambda step, order: (0, order[1, step]))),
            (short, pl.BlockSpec((1,) + short.shape[1:], lambda step, order: (order[0, step], 0, 0))),
        ],
        halves_out(short.shape[1], features // 2, wide + narrow),
        flops=15 * MICROSECOND,
        scratch=[pltpu.VMEM((features, rows), LOW), pltpu.VMEM((features, rows), LOW)],
        order=order,
        after=after,
    )


BITS = ((1, 2, 4), (1, 4, 2))


def slab_order():
    place = jnp.arange(SLABS, dtype=jnp.int32)
    if lax.axis_size("batch") != SLABS:
        return jnp.stack([place, place])
    orders = []
    for bits in BITS:
        apart = sum(((place >> (2 - j)) & 1) * bit for j, bit in enumerate(bits))
        orders.append(apart ^ lax.axis_index("batch"))
    return jnp.stack(orders)


class Sums:
    def __init__(self, axes, keep_a, send_a, keep_b, send_b):
        self.axes, self.stage = axes, 0
        self.terms, self.send = ([keep_a], [keep_b]), [send_a, send_b]

    def go(self):
        return [swap(send, "batch", bits[self.stage]) for send, bits in zip(self.send, BITS)]

    def land(self, arrived):
        terms = [own + [other] for own, other in zip(self.terms, arrived)]
        self.stage += 1
        if self.stage == 3:
            return [total(each).reshape(-1, each[0].shape[-1]) for each in terms]
        halves = [
            [jnp.split(one, 2, axis) for one in each] for each, axis in zip(terms, self.axes)
        ]
        self.terms = [[one[0] for one in each] for each in halves]
        self.send = [total([one[1] for one in each]).astype(LOW) for each in halves]
        return self.send


def total(terms):
    return sum(one.astype(jnp.float32) for one in terms)


class TokenSum:
    def __init__(self, values):
        self.low = jnp.where(lax.axis_index("tok") & 1, 1, 0)
        self.high = lax.axis_index("tok") >> 1
        pairs = values.reshape((2, 2) + values.shape[1:])
        self.keep = lax.dynamic_index_in_dim(pairs, self.low, 1, False)
        self.send = [lax.dynamic_index_in_dim(pairs, 1 - self.low, 1, False).astype(LOW)]
        self.stage = 0

    def go(self):
        return [swap(self.send[0], "tok", (1, 2, 2, 1)[self.stage])]

    def land(self, arrived):
        other = arrived[0]
        self.stage += 1
        if self.stage == 1:
            whole = self.keep + other.astype(jnp.float32)
            self.keep = lax.dynamic_index_in_dim(whole, self.high, 0, False)
            self.send = [lax.dynamic_index_in_dim(whole, 1 - self.high, 0, False).astype(LOW)]
        elif self.stage == 2:
            self.send = [(self.keep + other.astype(jnp.float32)).astype(LOW)]
        else:
            own, axis = ((self.high, 0), (self.low, 1))[self.stage - 3]
            mine = self.send[0]
            pair = jnp.stack([mine, other], axis), jnp.stack([other, mine], axis)
            self.send = [jnp.where(own == 0, pair[0], pair[1])]
        if self.stage < 4:
            return self.send
        whole = self.send[0].reshape((4,) + self.send[0].shape[2:])
        return [one.reshape(-1, one.shape[-1]) for one in jnp.split(whole, 2, axis=1)]


def arrive(moves, after, wait=0):
    flat = hold_until([one for move in moves for one in move], after, wait)
    held, at = [], 0
    for move in moves:
        held.append(flat[at : at + len(move)])
        at += len(move)
    return held


class DirectSum:
    def __init__(self, values):
        self.me, self.whole = lax.axis_index("tok"), None

        def quarter(at):
            return lax.dynamic_index_in_dim(values, at, 0, False)

        self.own = quarter(self.me)
        self.send = [quarter(self.me ^ step).astype(LOW) for step in (1, 2, 3)]

    def go(self):
        return [swap(one, "tok", step) for step, one in zip((1, 2, 3), self.send)]

    def land(self, arrived):
        if self.whole is None:
            self.whole = total([self.own] + arrived).astype(LOW)
            self.send = [self.whole] * 3
            return self.send[:1]
        one, two, three = arrived
        rows = [jnp.stack([self.whole, one]), jnp.stack([two, three])]
        rows = [jnp.where(self.me & 1, row[::-1], row) for row in rows]
        upper = self.me >> 1
        rows = jnp.where(upper == 0, rows[0], rows[1]), jnp.where(upper == 0, rows[1], rows[0])
        whole = jnp.concatenate(rows)
        return [each.reshape(-1, each.shape[-1]) for each in jnp.split(whole, 2, axis=1)]


def token_sum(top, bottom, kind=TokenSum):
    parts = [one.reshape(4, -1, one.shape[1]) for one in (top, bottom)]
    return kind(jnp.concatenate(parts, axis=1))


def spread_parts(turned, values):
    parts = [gather_rows(choice, values) for choice in jnp.split(turned, lax.axis_size("tok"))]
    parts[1] = hold_until(parts[1:2], parts[2:])[0]
    return parts


def swap_groups(parts):
    return [parts[0]] + [swap(parts[step], "tok", step) for step in range(1, len(parts))]


def place_rows(choice, parts):
    return gather_rows(choice, jnp.concatenate(parts, axis=0))


def on_device(
    block_input,
    crop_ids,
    ln1_gain,
    ln1_bias,
    w_qkv,
    q_bias,
    v_bias,
    w_out,
    out_bias,
    ln2_gain,
    ln2_bias,
    w_fc1,
    fc1_bias,
    w_fc2,
    fc2_bias,
    out_grad,
):
    packs, local_rows, features = block_input.shape
    rows = packs * local_rows
    shards = lax.axis_size("batch")
    paired = shards == SLABS
    send, receive, send_turned, receive_turned, overflow = exchange_plan(crop_ids)
    arrived = swap_groups(spread_parts(send_turned, block_input.reshape(rows, features)))
    held_back = spread_parts(send_turned, out_grad.reshape(rows, features))
    held_back = hold_until(held_back, arrived[1:])
    vectors = [out_bias, ln2_gain, ln2_bias, fc2_bias, ln1_gain, ln1_bias]
    vectors = jnp.stack(vectors + [jnp.zeros_like(out_bias)] * 2)
    bias = jnp.concatenate([q_bias, jnp.zeros_like(q_bias), v_bias])[None]
    grad_parts = swap_groups(held_back)
    fronts = front(
        arrived, receive, vectors, w_qkv, bias, w_out, w_fc1, fc1_bias[None], w_fc2, receive_turned
    )
    low_input, normed_one, joined, attended, *parts, n2t, hat, rstd, hidden, slope = fronts
    *parts, grad_parts[1], grad_parts[2], grad_parts[3] = hold_until(
        list(parts) + grad_parts[1:], []
    )
    low_grad = place_rows(receive, grad_parts)
    order = slab_order()

    def back(part, more, after):
        return list(
            feed_back(order, part, 2, low_grad, n2t, w_fc1, w_fc2, hidden, slope, more, after)
        )

    size = features // SLABS
    halves = SLABS, SLABS // 2, size, -1

    def slab_sums(back):
        return Sums((0, 1), back[0], back[1], back[2].reshape(halves), back[3].reshape(halves))

    backs = [back(0, [], parts[1:])]
    near = swap(parts[2], "tok", 2)
    backs[0][1], backs[0][3], near = hold_until([backs[0][1], backs[0][3], near], [])
    far = [swap(parts[3], "tok", 3), swap(parts[1], "tok", 1)]
    wait = [backs[0][1]]
    if paired:
        one = slab_sums(backs[0])
        wait = one.land(arrive([one.go()], [], 5)[0])
    backs.append(back(1, [backs[0][5], hat, rstd, vectors, w_out], wait))
    grad_branch, grad_attended, sums_two = backs[1][5:]
    wait = []
    if paired:
        *held, backs[1][1], backs[1][3] = hold_until(
            one.go() + far + [backs[1][1], backs[1][3]], []
        )
        wait, far = one.land(held[:2]), held[2:]
        two = slab_sums(backs[1])
    parts = [parts[0], far[1], near, far[0]]
    grad_joined = image_attention_back(joined, grad_attended, 0, 2, None, wait)
    if paired:
        held = arrive([one.go(), two.go()], [grad_joined])
        left = token_sum(*one.land(held[0]))
        wait = left.send + two.land(held[1])
    grad_joined = image_attention_back(joined, grad_attended, 1, 2, grad_joined, wait)
    if paired:
        moving = two.go()
        wait = left.land(arrive([left.go()], [grad_joined])[0])
    *input_parts, sums_one, joined_sums = first_norm_back(
        grad_joined, w_qkv, low_input, grad_branch, vectors, receive_turned, wait
    )
    wait = []
    if paired:
        *held, sums_one = hold_until(left.go() + moving + input_parts[1:] + [sums_one], [])
        input_parts[1:] = held[3:]
        left.land(held[:1])
        wait = two.land(held[1:3])
    input_parts = swap_groups(input_parts)
    short = [
        sums_one[0],
        sums_one[1],
        joined_sums[0, :features],
        joined_sums[0, 2 * features :],
        sums_two[0],
        sums_two[1],
        sums_two[2],
        sums_two[3],
        jnp.stack([each[4].reshape(SLABS, -1) for each in backs], axis=1).reshape(-1),
        jnp.broadcast_to(overflow.astype(jnp.float32), (SLABS * features // 2,)),
    ]
    short_slabs = jnp.concatenate([each.reshape(SLABS, -1) for each in short], axis=1)
    short_slabs = short_slabs.reshape(SLABS, -1, 4 * size)
    short_slabs = jnp.pad(short_slabs, ((0, 0), (0, 64 - short_slabs.shape[1]), (0, 0)))
    products = attention_products(
        order, normed_one, attended, grad_joined, grad_branch, short_slabs, wait
    )
    if paired:
        products = list(products)
        held = hold_until(
            [products[1], products[3]] + two.go() + input_parts[2:3] + left.send, []
        )
        products[1], products[3] = held[:2]
        input_parts[2] = held[4]
        left.send = held[5:]
        three = Sums((0, 0), *products)
        right = token_sum(*two.land(held[2:4]))
        three.land(arrive([three.go()], right.send, 6)[0])
        left.land(arrive([left.go()], three.send, 12)[0])
        output = place_rows(send, hold_until(parts, left.send))
        three.land(arrive([three.go()], left.send + [output], 10)[0])
        held = arrive([right.go(), input_parts[1:2]], three.send, 2)
        right.land(held[0])
        input_parts[1] = held[1][0]
        top, bottom = three.land(arrive([three.go()], right.send + left.send, 14)[0])
        bottom = jnp.pad(bottom, ((0, top.shape[0] - bottom.shape[0]), (0, 0)))
        last = token_sum(top, bottom, DirectSum)
        held = arrive([right.go(), input_parts[3:]], last.send, 2)
        right.land(held[0])
        input_parts[3] = held[1][0]
        held = arrive([right.go(), left.go()], last.send, 12)
        right.land(held[0])
        first = left.land(held[1])
        last.land(arrive([last.go()], right.send, 12)[0])
        second = right.land(arrive([right.go()], last.send[:1], 8)[0])
        input_grad = place_rows(send, hold_until(input_parts, last.send[:1]))
        grad_fc1 = jnp.concatenate([first[0], second[0]], axis=1).astype(jnp.float32)
        fc2 = [each[1].reshape(SLABS, size, -1) for each in (first, second)]
        fc2 = jnp.stack(fc2, axis=1).transpose(0, 1, 3, 2).reshape(-1, size)
        grad_fc2 = fc2.astype(jnp.float32)
        third = last.land(arrive([last.go()], [input_grad, grad_fc1, grad_fc2], 8)[0])
        halves = [each[: features // 2] for each in third]
        grad_attention = jnp.concatenate(halves, axis=0)
        grad_qkv, grad_out = grad_attention[:, : 3 * size], grad_attention[:, 3 * size :]
        tail = third[0][features // 2 :].reshape(-1).astype(jnp.float32)
        pieces = [tail[i * size : (i + 1) * size] for i in range(8)]
        pieces += [tail[8 * size : 12 * size], tail[12 * size :][:1]]
    else:
        output = place_rows(send, parts)
        input_grad = place_rows(send, input_parts)
        fc1 = jnp.stack([jnp.concatenate(each[:2]) for each in backs], axis=2)
        grad_fc1 = share_columns(fc1.transpose(1, 0, 2, 3).reshape(features, -1))
        fc2 = jnp.stack([jnp.concatenate(each[2:4], axis=1) for each in backs], axis=2)
        fc2 = fc2.transpose(1, 0, 2, 3).reshape(shards, features // shards, -1)
        grad_fc2 = share_slabs(fc2).T
        both = [jnp.concatenate(products[:2])[:, : features // 2], jnp.concatenate(products[2:])]
        both = jnp.concatenate(both, axis=1)
        grad_qkv = share_columns(both[:, :, : 3 * size].transpose(1, 0, 2).reshape(features, -1))
        grad_out = share_columns(both[:, :, 3 * size :].transpose(1, 0, 2).reshape(features, -1))
        widths = [each.shape[0] // shards for each in short]
        packed = jnp.concatenate([each.reshape(shards, -1) for each in short], axis=1)
        packed = share_slabs(packed.astype(LOW)).astype(jnp.float32)
        pieces, at = [], 0
        for width in widths:
            pieces.append(packed[at : at + width])
            at += width
    fast = (
        output.reshape(block_input.shape),
        input_grad.reshape(block_input.shape),
        pieces[0],
        pieces[1],
        grad_qkv.astype(jnp.float32),
        pieces[2],
        pieces[3],
        grad_out.astype(jnp.float32),
        pieces[4],
        pieces[5],
        pieces[6],
        grad_fc1.astype(jnp.float32),
        pieces[8],
        grad_fc2.astype(jnp.float32),
        pieces[7],
    )

    def unfinished(state):
        return state[0] > 0.5

    def redo(state):
        return (
            jnp.float32(0.0),
            in_place(
                block_input,
                crop_ids,
                ln1_gain,
                ln1_bias,
                w_qkv,
                q_bias,
                v_bias,
                w_out,
                out_bias,
                ln2_gain,
                ln2_bias,
                w_fc1,
                fc1_bias,
                w_fc2,
                fc2_bias,
                out_grad,
            ),
        )

    return lax.while_loop(unfinished, redo, (pieces[9][0], fast))[1]


def solution(mesh):
    in_specs = (
        P("batch", "tok", None),
        P("batch", None),
        P(),
        P(),
        P(),
        P(),
        P(),
        P(),
        P(),
        P(),
        P(),
        P(),
        P(),
        P(),
        P(),
        P("batch", "tok", None),
    )
    out_specs = (
        P("batch", "tok", None),
        P("batch", "tok", None),
        P("batch"),
        P("batch"),
        P(None, "batch"),
        P("batch"),
        P("batch"),
        P(None, "batch"),
        P("batch"),
        P("batch"),
        P("batch"),
        P(None, "batch"),
        P("batch"),
        P(None, "batch"),
        P("batch"),
    )
    return jax.shard_map(
        on_device, mesh=mesh, in_specs=in_specs, out_specs=out_specs, check_vma=False
    )
```
